32 devices in a mesh: dp: 2 (over x), row: 4 (over z), col: 4 (over y, core).
Axes of the slice: x: 2, y: 2, z: 4, core: 2. Of those that a mesh axis runs over, the one named last changes fastest.
Arguments:
- tokens: bfloat16 [4, 4096, 1024], P(None, ('dp', 'row', 'col')), may hold values from -6 to 6
- lengths: int32 [2, 4], P('dp'), may hold values from 512 to 2048, as said below
- first_gain: float32 [1024], replicated, may hold values from 0.5 to 1.5
- first_shift: float32 [1024], replicated, may hold values from -1.25 to 1.25
- w_query: bfloat16 [1024, 1024], P(('dp', 'row'), 'col'), may hold values from -0.1875 to 0.1875
- w_key: bfloat16 [1024, 1024], P(('dp', 'row'), 'col'), may hold values from -0.1875 to 0.1875
- w_value: bfloat16 [1024, 1024], P(('dp', 'row'), 'col'), may hold values from -0.1875 to 0.1875
- bias_query: float32 [1024], P('col'), may hold values from -3 to 3
- bias_value: float32 [1024], P('col'), may hold values from -0.3125 to 0.3125
- w_output: bfloat16 [1024, 1024], P('col', ('dp', 'row')), may hold values from -2 to 2
- bias_output: float32 [1024], replicated, may hold values from -1.25 to 1.25
- second_gain: float32 [1024], replicated, may hold values from 0.5 to 1.5
- second_shift: float32 [1024], replicated, may hold values from -1.25 to 1.25
- w_up: bfloat16 [1024, 4096], P(('dp', 'row'), 'col'), may hold values from -0.1875 to 0.1875
- bias_up: float32 [4096], P('col'), may hold values from -1.75 to 1.75
- w_down: bfloat16 [4096, 1024], P('col', ('dp', 'row')), may hold values from -0.09375 to 0.09375
- bias_down: float32 [1024], replicated, may hold values from -1.25 to 1.25
- cotangent: bfloat16 [4, 4096, 1024], P(None, ('dp', 'row', 'col')), may hold values from -6 to 6
Outputs:
- output: bfloat16 [4, 4096, 1024], P(None, ('dp', 'row', 'col'))
- grad_tokens: bfloat16 [4, 4096, 1024], P(None, ('dp', 'row', 'col'))
- grad_first_gain: float32 [1024], replicated
- grad_first_shift: float32 [1024], replicated
- grad_w_query: float32 [1024, 1024], P(('dp', 'row'), 'col')
- grad_w_key: float32 [1024, 1024], P(('dp', 'row'), 'col')
- grad_w_value: float32 [1024, 1024], P(('dp', 'row'), 'col')
- grad_bias_query: float32 [1024], P('col')
- grad_bias_value: float32 [1024], P('col')
- grad_w_output: float32 [1024, 1024], P('col', ('dp', 'row'))
- grad_bias_output: float32 [1024], replicated
- grad_second_gain: float32 [1024], replicated
- grad_second_shift: float32 [1024], replicated
- grad_w_up: float32 [1024, 4096], P(('dp', 'row'), 'col')
- grad_bias_up: float32 [4096], P('col')
- grad_w_down: float32 [4096, 1024], P('col', ('dp', 'row'))
- grad_bias_down: float32 [1024], replicated
The draws below stay inside these ranges and needn't reach their ends.
Inputs may be any that keep to these rules, and one draw needn't show every extreme that they name: `lengths`: in every group one of the 4 sequences, which one drawn from the seed, has exactly 2048 valid tokens.
All inputs are finite; a program needn't handle non-finite values.
Results may differ from the reference program's by a relative error of at most 0.012.
Values may be sent and summed in bfloat16 or wider, within the bound.
A program may use at most 192 MiB of HBM per device.

```python
import jax
import jax.numpy as jnp
from jax import lax

D = 1024
HEADS = 16
HD = 64
FF = 4096
MICRO = 4
LEN = 2048
GROUPS = 2
SLOT_TOK = 4096


def draw_lengths(key, part):
    shortest = LEN // 4
    random_lengths = jax.random.randint(jax.random.fold_in(key, 11), (GROUPS, MICRO), shortest, LEN + 1)
    chosen = jax.random.randint(jax.random.fold_in(key, 12), (GROUPS,), 0, MICRO)
    longest = jnp.arange(MICRO, dtype=jnp.int32)[None, :] == chosen[:, None]
    return jnp.where(longest, LEN, random_lengths).astype(jnp.int32)


def level_of(key, shape, shards, least, largest):
    factor_of = 1.0
    for dim, shards_of in shards:
        draws = jax.random.uniform(jax.random.fold_in(jax.random.fold_in(key, 6), dim), (shards_of,), jnp.float32, least / len(shards), largest / len(shards))
        factor_of = factor_of * jnp.repeat(jnp.exp(draws), shape[dim] // shards_of).reshape((-1,) + (1,) * (len(shape) - 1 - dim))
    return factor_of


def gaussian(key, extent, scale, limit, split=(), kind=jnp.bfloat16):
    array = jax.random.normal(key, extent, jnp.float32) * scale
    if len(split) > 0:
        array = level_of(key, extent, split, -0.22, 0.18) * array
    return jnp.clip(array, min=-limit, max=limit).astype(kind)


def setup_inputs(seed: int = 0) -> dict:
    splits = jax.random.split(jax.random.key(seed), 19)
    tokens = gaussian(splits[0], (MICRO, SLOT_TOK, D), 1.0, 6.0, ((1, 32),))
    lengths = draw_lengths(jax.random.fold_in(splits[18], 71), 0)
    first_gain = jnp.clip(1.0 + 0.1 * jax.random.normal(splits[2], (D,), jnp.float32), 0.5, 1.5)
    first_shift = gaussian(splits[3], (D,), 0.2, 1.25, (), jnp.float32)
    w_query = gaussian(splits[4], (D, D), D ** -0.5, 0.1875, ((0, 8), (1, 4)))
    w_key = gaussian(splits[5], (D, D), D ** -0.5, 0.1875, ((0, 8), (1, 4)))
    w_value = gaussian(splits[6], (D, D), D ** -0.5, 0.1875, ((0, 8), (1, 4)))
    bias_query = gaussian(splits[7], (D,), 0.5, 3.0, ((0, 4),), jnp.float32)
    bias_value = gaussian(splits[8], (D,), 0.05, 0.3125, ((0, 4),), jnp.float32)
    w_output = gaussian(splits[9], (D, D), (max(1, D * 16 // LEN)) ** -0.5, 2.0, ((0, 4), (1, 8)))
    bias_output = gaussian(splits[10], (D,), 0.2, 1.25, (), jnp.float32)
    second_gain = jnp.clip(1.0 + 0.1 * jax.random.normal(splits[11], (D,), jnp.float32), 0.5, 1.5)
    second_shift = gaussian(splits[12], (D,), 0.2, 1.25, (), jnp.float32)
    w_up = gaussian(splits[13], (D, FF), D ** -0.5, 0.1875, ((0, 8), (1, 4)))
    bias_up = gaussian(splits[14], (FF,), 0.3, 1.75, ((0, 4),), jnp.float32)
    w_down = gaussian(splits[15], (FF, D), FF ** -0.5, 0.09375, ((0, 4), (1, 8)))
    bias_down = gaussian(splits[16], (D,), 0.2, 1.25, (), jnp.float32)
    cotangent = gaussian(splits[17], (MICRO, SLOT_TOK, D), 1.0, 6.0, ((1, 32),))
    return {"tokens": tokens, "lengths": lengths, "first_gain": first_gain, "first_shift": first_shift, "w_query": w_query, "w_key": w_key, "w_value": w_value, "bias_query": bias_query, "bias_value": bias_value, "w_output": w_output, "bias_output": bias_output, "second_gain": second_gain, "second_shift": second_shift, "w_up": w_up, "bias_up": bias_up, "w_down": w_down, "bias_down": bias_down, "cotangent": cotangent}


EPSILON = 1e-05
MASKED = -1e+30
HIGHEST = lax.Precision.HIGHEST

@jax.custom_vjp
def low(v):
    return lax.optimization_barrier(v.astype(jnp.bfloat16)).astype(jnp.float32)

@jax.custom_vjp
def low_back(v):
    return v

def low_keep(v):
    return (low(v), None)

def low_pass(kept, grad):
    return (grad,)

def back_keep(v):
    return (v, None)

def back_low(kept, grad):
    return (low(grad),)
low.defvjp(low_keep, low_pass)
low_back.defvjp(back_keep, back_low)

def layer_norm(values, norm_gain, norm_shift):
    centered = values - lax.optimization_barrier(jnp.mean(values, axis=-1, keepdims=True))
    variance = lax.optimization_barrier(jnp.mean(centered * centered, axis=-1, keepdims=True))
    return centered * lax.rsqrt(variance + EPSILON) * norm_gain + norm_shift

def product(former, latter):
    return jnp.dot(former, latter, precision=HIGHEST, preferred_element_type=jnp.float32)

def attend(queries, key_rows, value_rows, length):
    seq_rows = queries.shape[0]
    block_rows = min(512, seq_rows)
    block_count = seq_rows // block_rows
    score_scale = HD ** (-0.5)
    query_blocks = queries.reshape(block_count, block_rows, HEADS, HD)
    key_heads = key_rows.reshape(seq_rows, HEADS, HD)
    value_heads = value_rows.reshape(seq_rows, HEADS, HD)
    positions = jnp.arange(seq_rows, dtype=jnp.int32)

    def one_block(operands):
        query_block, start_row = operands
        rows_here = start_row + jnp.arange(block_rows, dtype=jnp.int32)
        scores = jnp.einsum('qhd,khd->hqk', query_block, key_heads, precision=HIGHEST) * score_scale
        scores = low_back(scores)
        allowed = (positions[None, :] <= rows_here[:, None]) & (positions[None, :] < length)
        scores = jnp.where(allowed[None], scores, MASKED)
        highest = lax.optimization_barrier(jnp.max(scores, axis=-1, keepdims=True))
        exponent = jnp.exp(scores - highest)
        weights = low(exponent / lax.optimization_barrier(jnp.sum(exponent, axis=-1, keepdims=True)))
        return jnp.einsum('hqk,khd->qhd', weights, value_heads, precision=HIGHEST)
    starts = jnp.arange(block_count, dtype=jnp.int32) * block_rows
    attended = lax.map(jax.checkpoint(one_block), (query_blocks, starts))
    return attended.reshape(seq_rows, HEADS * HD)

def forward_sequence(sequence, params, length):
    first_gain, first_shift, w_query, w_key, w_value, bias_query, bias_value, w_output, bias_output, second_gain, second_shift, w_up, bias_up, w_down, bias_down = params
    first_normed = low(layer_norm(sequence, first_gain, first_shift))
    queries = low(low_back(product(first_normed, w_query) + bias_query))
    key_rows = low(low_back(product(first_normed, w_key)))
    value_rows = low(low_back(product(first_normed, w_value) + bias_value))
    attended = low(low_back(attend(queries, key_rows, value_rows, length)))
    branch = low_back(product(attended, w_output) + bias_output)
    middle = sequence + branch
    second_normed = low(layer_norm(middle, second_gain, second_shift))
    pre_activation = low_back(product(second_normed, w_up) + bias_up)
    activated = low(jax.nn.gelu(pre_activation, approximate=True))
    feed = low_back(product(activated, w_down) + bias_down)
    return middle + feed

def reference(tokens, lengths, first_gain, first_shift, w_query, w_key, w_value, bias_query, bias_value, w_output, bias_output, second_gain, second_shift, w_up, bias_up, w_down, bias_down, cotangent):
    micro_count, slot_rows, width = tokens.shape
    group_count = lengths.shape[0]
    seq_rows = slot_rows // group_count
    params = tuple((argument.astype(jnp.float32) for argument in (first_gain, first_shift, w_query, w_key, w_value, bias_query, bias_value, w_output, bias_output, second_gain, second_shift, w_up, bias_up, w_down, bias_down)))

    def regroup(argument):
        shaped = argument.astype(jnp.float32).reshape(micro_count, group_count, seq_rows, width)
        return shaped.transpose(1, 0, 2, 3).reshape(group_count * micro_count, seq_rows, width)
    inputs = regroup(tokens)
    cotangents = regroup(cotangent)
    flat_lengths = lengths.reshape(group_count * micro_count).astype(jnp.int32)

    def one_sequence(totals, operands):
        sequence, grad_rows, length = operands
        validity = (jnp.arange(seq_rows, dtype=jnp.int32) < length).astype(jnp.float32)
        result, backward = jax.vjp(lambda rows_in, weights_in: forward_sequence(rows_in, weights_in, length), sequence, params)
        grad_input, grad_params = backward(grad_rows * validity[:, None])
        totals = jax.tree.map(jnp.add, totals, grad_params)
        return (totals, (result.astype(jnp.bfloat16), grad_input.astype(jnp.bfloat16)))
    initial = tuple((jnp.zeros_like(argument) for argument in params))
    totals, (results, grad_inputs) = lax.scan(one_sequence, initial, (inputs, cotangents, flat_lengths))

    def ungroup(argument):
        shaped = argument.reshape(group_count, micro_count, seq_rows, width)
        return shaped.transpose(1, 0, 2, 3).reshape(micro_count, slot_rows, width)
    grad_first_gain, grad_first_shift, grad_w_query, grad_w_key, grad_w_value, grad_bias_query, grad_bias_value, grad_w_output, grad_bias_output, grad_second_gain, grad_second_shift, grad_w_up, grad_bias_up, grad_w_down, grad_bias_down = totals
    return (ungroup(results), ungroup(grad_inputs), grad_first_gain, grad_first_shift, grad_w_query, grad_w_key, grad_w_value, grad_bias_query, grad_bias_value, grad_w_output, grad_bias_output, grad_second_gain, grad_second_shift, grad_w_up, grad_bias_up, grad_w_down, grad_bias_down)
```

```python
import functools

import jax
import jax.numpy as jnp
from jax import lax
from jax.experimental import pallas as pl
from jax.experimental.pallas import tpu as pltpu
from jax.sharding import PartitionSpec as P

HD = 64


EPSILON = 1e-05
MASKED = -1e30


def layer_norm(values, norm_gain, norm_shift):
    centered = values - jnp.mean(values, axis=-1, keepdims=True)
    variance = jnp.mean(centered * centered, axis=-1, keepdims=True)
    return centered * lax.rsqrt(variance + EPSILON) * norm_gain + norm_shift


def gelu_tanh(values):
    return jax.nn.gelu(values, approximate=True)


def product(former, latter):
    return jnp.dot(former, latter, preferred_element_type=jnp.float32)


def transposed_left(former, latter):
    return lax.dot_general(
        former, latter, (((0,), (0,)), ((), ())), preferred_element_type=jnp.float32
    )


def transposed_right(former, latter):
    return lax.dot_general(
        former, latter, (((1,), (1,)), ((), ())), preferred_element_type=jnp.float32
    )


def spread_rows(rows_block):
    return lax.all_gather(rows_block, "col", axis=0, tiled=True)


def fold_rows(partial_sum):
    return lax.psum_scatter(partial_sum, "col", scatter_dimension=0, tiled=True)


def fetch_weights(w_query, w_key, w_value, w_up, w_output, w_down):
    leading = (
        lax.all_gather(w_query, ("dp", "row"), axis=0, tiled=True),
        lax.all_gather(w_key, ("dp", "row"), axis=0, tiled=True),
        lax.all_gather(w_value, ("dp", "row"), axis=0, tiled=True),
        lax.all_gather(w_up, ("dp", "row"), axis=0, tiled=True),
    )
    trailing = (
        lax.all_gather(w_output, ("dp", "row"), axis=1, tiled=True),
        lax.all_gather(w_down, ("dp", "row"), axis=1, tiled=True),
    )
    return tuple(leading) + tuple(trailing)


def reduce_blocks(gradients):
    leading = (
        lax.psum_scatter(gradients[0], ("dp", "row"), scatter_dimension=0, tiled=True),
        lax.psum_scatter(gradients[1], ("dp", "row"), scatter_dimension=0, tiled=True),
        lax.psum_scatter(gradients[2], ("dp", "row"), scatter_dimension=0, tiled=True),
        lax.psum_scatter(gradients[3], ("dp", "row"), scatter_dimension=0, tiled=True),
    )
    trailing = (
        lax.psum_scatter(gradients[4], ("dp", "row"), scatter_dimension=1, tiled=True),
        lax.psum_scatter(gradients[5], ("dp", "row"), scatter_dimension=1, tiled=True),
    )
    return tuple(leading) + tuple(trailing)


def heads_of(rows_block):
    return rows_block.reshape(rows_block.shape[0], -1, HD)


def block_of(rows_all, start, block_rows):
    return heads_of(lax.dynamic_slice_in_dim(rows_all, start, block_rows, 0))


def block_scores(query_heads, key_heads, query_start, key_start, length):
    block_rows = query_heads.shape[0]
    scores = jnp.einsum(
        "qhd,khd->hqk", query_heads, key_heads, preferred_element_type=jnp.float32
    ) * HD ** (-0.5)
    query_pos = query_start + jnp.arange(block_rows, dtype=jnp.int32)
    key_pos = key_start + jnp.arange(key_heads.shape[0], dtype=jnp.int32)
    allowed = (key_pos[None, :] <= query_pos[:, None]) & (key_pos[None, :] < length)
    return jnp.where(allowed[None], scores, MASKED)


def key_block_count(row_place, length, block_rows):
    return jnp.minimum(row_place + 1, (length + block_rows - 1) // block_rows)


def attention_forward(queries, key_rows, value_rows, row_place, length):
    block_rows = queries.shape[0]
    query_heads = heads_of(queries)
    head_count = query_heads.shape[1]
    query_start = row_place * block_rows
    count = key_block_count(row_place, length, block_rows)

    def stats_step(block_index, carry):
        highest, partition = carry
        start = block_index * block_rows
        scores = block_scores(
            query_heads, block_of(key_rows, start, block_rows), query_start, start, length
        )
        newest = jnp.maximum(highest, jnp.max(scores, axis=-1, keepdims=True))
        partition = partition * jnp.exp(highest - newest) + jnp.sum(
            jnp.exp(scores - newest), axis=-1, keepdims=True
        )
        return (newest, partition)

    start_stats = (
        jnp.full((head_count, block_rows, 1), MASKED, jnp.float32),
        jnp.zeros((head_count, block_rows, 1), jnp.float32),
    )
    highest, partition = lax.fori_loop(0, count, stats_step, start_stats)

    def output_step(block_index, total):
        start = block_index * block_rows
        scores = block_scores(
            query_heads, block_of(key_rows, start, block_rows), query_start, start, length
        )
        weights_low = (jnp.exp(scores - highest) / partition).astype(jnp.bfloat16)
        return total + jnp.einsum(
            "hqk,khd->qhd",
            weights_low,
            block_of(value_rows, start, block_rows),
            preferred_element_type=jnp.float32,
        )

    total = lax.fori_loop(0, count, output_step, jnp.zeros(query_heads.shape, jnp.float32))
    return (total.reshape(block_rows, -1), highest, partition)


def attention_query_side(
    queries, key_rows, value_rows, grad_attended, highest, partition, row_place, length
):
    block_rows = queries.shape[0]
    seq_rows = key_rows.shape[0]
    query_heads = heads_of(queries)
    grad_heads = heads_of(grad_attended)
    head_count = query_heads.shape[1]
    query_start = row_place * block_rows
    count = key_block_count(row_place, length, block_rows)

    def inner_step(block_index, total):
        start = block_index * block_rows
        scores = block_scores(
            query_heads, block_of(key_rows, start, block_rows), query_start, start, length
        )
        weights = jnp.exp(scores - highest) / partition
        grad_weights = jnp.einsum(
            "qhd,khd->hqk",
            grad_heads,
            block_of(value_rows, start, block_rows),
            preferred_element_type=jnp.float32,
        )
        return total + jnp.sum(weights * grad_weights, axis=-1, keepdims=True)

    inner = lax.fori_loop(0, count, inner_step, jnp.zeros((head_count, block_rows, 1), jnp.float32))

    def grad_step(block_index, carry):
        start = block_index * block_rows
        key_heads = block_of(key_rows, start, block_rows)
        scores = block_scores(query_heads, key_heads, query_start, start, length)
        weights = jnp.exp(scores - highest) / partition
        grad_weights = jnp.einsum(
            "qhd,khd->hqk",
            grad_heads,
            block_of(value_rows, start, block_rows),
            preferred_element_type=jnp.float32,
        )
        grad_scores = (weights * (grad_weights - inner)).astype(jnp.bfloat16)
        query_total = carry[0] + jnp.einsum(
            "hqk,khd->qhd", grad_scores, key_heads, preferred_element_type=jnp.float32
        )
        weights_low = weights.astype(jnp.bfloat16)
        key_part = jnp.einsum(
            "hqk,qhd->khd", grad_scores, query_heads, preferred_element_type=jnp.float32
        )
        value_part = jnp.einsum(
            "hqk,qhd->khd", weights_low, grad_heads, preferred_element_type=jnp.float32
        )
        key_total = lax.dynamic_update_slice_in_dim(
            carry[1], lax.dynamic_slice_in_dim(carry[1], start, block_rows, 0) + key_part, start, 0
        )
        value_total = lax.dynamic_update_slice_in_dim(
            carry[2],
            lax.dynamic_slice_in_dim(carry[2], start, block_rows, 0) + value_part,
            start,
            0,
        )
        return (query_total, key_total, value_total)

    start_carry = (jnp.zeros(query_heads.shape, jnp.float32),)
    start_carry = start_carry + (
        jnp.zeros((seq_rows, head_count, HD), jnp.float32),
        jnp.zeros((seq_rows, head_count, HD), jnp.float32),
    )
    totals = lax.fori_loop(0, count, grad_step, start_carry)
    query_terms = totals[0].reshape(block_rows, -1) * HD ** (-0.5)
    return (
        query_terms,
        totals[1].reshape(seq_rows, -1) * HD ** (-0.5),
        totals[2].reshape(seq_rows, -1),
        inner,
    )


def local_general(
    tokens,
    lengths,
    first_gain,
    first_shift,
    w_query,
    w_key,
    w_value,
    bias_query,
    bias_value,
    w_output,
    bias_output,
    second_gain,
    second_shift,
    w_up,
    bias_up,
    w_down,
    bias_down,
    cotangent,
):
    micro_count, own_rows, width = tokens.shape
    col_count = lax.axis_size("col")
    group_rows = own_rows * col_count
    row_place = lax.axis_index("row")
    col_place = lax.axis_index("col")
    head_width = w_query.shape[1]
    hidden_width = w_up.shape[1]
    own_positions = (
        row_place * group_rows + col_place * own_rows + jnp.arange(own_rows, dtype=jnp.int32)
    )
    weight_totals = (
        jnp.zeros((width, head_width), jnp.float32),
        jnp.zeros((width, head_width), jnp.float32),
        jnp.zeros((width, head_width), jnp.float32),
        jnp.zeros((width, hidden_width), jnp.float32),
        jnp.zeros((head_width, width), jnp.float32),
        jnp.zeros((hidden_width, width), jnp.float32),
    )
    vector_totals = (
        jnp.zeros((width,), jnp.float32),
        jnp.zeros((width,), jnp.float32),
        jnp.zeros((head_width,), jnp.float32),
        jnp.zeros((head_width,), jnp.float32),
        jnp.zeros((width,), jnp.float32),
        jnp.zeros((width,), jnp.float32),
        jnp.zeros((width,), jnp.float32),
        jnp.zeros((hidden_width,), jnp.float32),
        jnp.zeros((width,), jnp.float32),
    )
    results = []
    input_grads = []
    for micro_index in range(micro_count):
        gathered = fetch_weights(w_query, w_key, w_value, w_up, w_output, w_down)
        query_full, key_full, value_full, up_full, output_full, down_full = gathered
        length = lengths[0, micro_index]
        inputs = tokens[micro_index].astype(jnp.float32)
        normed = layer_norm(inputs, first_gain, first_shift).astype(jnp.bfloat16)
        normed_all = spread_rows(normed)
        queries = (product(normed_all, query_full) + bias_query).astype(jnp.bfloat16)
        keys_local = product(normed_all, key_full).astype(jnp.bfloat16)
        values_local = (product(normed_all, value_full) + bias_value).astype(jnp.bfloat16)
        keys_all, values_all = (
            lax.all_gather(keys_local, "row", axis=0, tiled=True),
            lax.all_gather(values_local, "row", axis=0, tiled=True),
        )
        attended, maxima, partitions = attention_forward(
            queries, keys_all, values_all, row_place, length
        )
        attended_low = attended.astype(jnp.bfloat16)
        branch = fold_rows(product(attended_low, output_full)) + bias_output
        middle = inputs + branch
        second_normed = layer_norm(middle, second_gain, second_shift).astype(jnp.bfloat16)
        second_all = spread_rows(second_normed)
        pre_activation = product(second_all, up_full) + bias_up
        activated = gelu_tanh(pre_activation).astype(jnp.bfloat16)
        result = middle + (fold_rows(product(activated, down_full)) + bias_down)
        results.append(result.astype(jnp.bfloat16))
        query_full, key_full, value_full, up_full, output_full, down_full = fetch_weights(
            w_query, w_key, w_value, w_up, w_output, w_down
        )
        validity = (own_positions < length).astype(jnp.float32)
        grad_result = cotangent[micro_index].astype(jnp.float32) * validity[:, None]
        grad_result_all = spread_rows(grad_result.astype(jnp.bfloat16))
        grad_down = transposed_left(activated, grad_result_all)
        grad_activated = transposed_right(grad_result_all, down_full)
        gelu_back = jax.vjp(gelu_tanh, pre_activation)[1]
        grad_pre = gelu_back(grad_activated)[0].astype(jnp.bfloat16)
        grad_up = transposed_left(second_all, grad_pre)
        grad_second_normed = fold_rows(transposed_right(grad_pre, up_full))
        second_back = jax.vjp(layer_norm, middle, second_gain, second_shift)[1]
        grad_middle_norm, grad_second_gain, grad_second_shift = second_back(grad_second_normed)
        grad_middle = grad_result + grad_middle_norm
        grad_branch = grad_middle.astype(jnp.bfloat16)
        grad_branch_all = spread_rows(grad_branch)
        grad_output = transposed_left(attended_low, grad_branch_all)
        grad_attended = transposed_right(grad_branch_all, output_full).astype(jnp.bfloat16)
        query_terms, key_terms, value_terms, inner = attention_query_side(
            queries, keys_all, values_all, grad_attended, maxima, partitions, row_place, length
        )
        key_sums, value_sums = (
            lax.psum_scatter(key_terms, "row", scatter_dimension=0, tiled=True),
            lax.psum_scatter(value_terms, "row", scatter_dimension=0, tiled=True),
        )
        grad_queries = query_terms.astype(jnp.bfloat16)
        grad_keys = key_sums.astype(jnp.bfloat16)
        grad_values = value_sums.astype(jnp.bfloat16)
        grad_query = transposed_left(normed_all, grad_queries)
        grad_key = transposed_left(normed_all, grad_keys)
        grad_value = transposed_left(normed_all, grad_values)
        grad_normed = fold_rows(
            transposed_right(grad_queries, query_full)
            + transposed_right(grad_keys, key_full)
            + transposed_right(grad_values, value_full)
        )
        first_back = jax.vjp(layer_norm, inputs, first_gain, first_shift)[1]
        grad_inputs_norm, grad_first_gain, grad_first_shift = first_back(grad_normed)
        input_grads.append((grad_middle + grad_inputs_norm).astype(jnp.bfloat16))
        local_grads = (grad_query, grad_key, grad_value, grad_up, grad_output, grad_down)
        weight_totals = tuple(
            (former + latter for former, latter in zip(weight_totals, local_grads))
        )
        local_vectors = (
            grad_first_gain,
            grad_first_shift,
            jnp.sum(grad_queries.astype(jnp.float32), axis=0),
            jnp.sum(grad_values.astype(jnp.float32), axis=0),
            jnp.sum(grad_branch.astype(jnp.float32), axis=0),
            grad_second_gain,
            grad_second_shift,
            jnp.sum(grad_pre.astype(jnp.float32), axis=0),
            jnp.sum(grad_result, axis=0),
        )
        vector_totals = tuple(
            (former + latter for former, latter in zip(vector_totals, local_vectors))
        )
    weight_totals = reduce_blocks(weight_totals)

    def widen(vector_part):
        blank = jnp.zeros((vector_part.shape[0] * col_count,), jnp.float32)
        return lax.dynamic_update_slice(blank, vector_part, (col_place * vector_part.shape[0],))

    def narrow(whole_vector, piece_width):
        return lax.dynamic_slice_in_dim(whole_vector, col_place * piece_width, piece_width)

    (
        sum_first_gain,
        sum_first_shift,
        sum_bias_query,
        sum_bias_value,
        sum_bias_output,
        sum_second_gain,
        sum_second_shift,
        sum_bias_up,
        sum_bias_down,
    ) = lax.psum(
        (
            vector_totals[0],
            vector_totals[1],
            widen(vector_totals[2]),
            widen(vector_totals[3]),
            vector_totals[4],
            vector_totals[5],
            vector_totals[6],
            widen(vector_totals[7]),
            vector_totals[8],
        ),
        ("dp", "row", "col"),
    )
    grad_w_query, grad_w_key, grad_w_value, grad_w_up, grad_w_output, grad_w_down = weight_totals
    return (
        jnp.stack(results, axis=0),
        jnp.stack(input_grads, axis=0),
        sum_first_gain,
        sum_first_shift,
        grad_w_query,
        grad_w_key,
        grad_w_value,
        narrow(sum_bias_query, head_width),
        narrow(sum_bias_value, head_width),
        grad_w_output,
        sum_bias_output,
        sum_second_gain,
        sum_second_shift,
        grad_w_up,
        narrow(sum_bias_up, hidden_width),
        grad_w_down,
        sum_bias_down,
    )


F32 = jnp.float32
LOW = jnp.bfloat16
VMEM_LIMIT = 56 * 1024 * 1024


def fits(mesh):
    return mesh.shape["row"] == 4 and mesh.shape["col"] == 4 and mesh.shape["dp"] == 2


def contract(former, latter, former_dim, latter_dim):
    return lax.dot_general(
        former,
        latter,
        (((former_dim,), (latter_dim,)), ((), ())),
        preferred_element_type=jnp.float32,
    )


def attention_out_kernel(q_ref, k_ref, v_ref, key_bias_ref, causal_ref, o_ref, lse_ref):
    block = q_ref.shape[0]
    chunks = k_ref.shape[0] // block
    place = pl.program_id(1)
    lane = lax.broadcasted_iota(jnp.int32, q_ref.shape, 1)
    queries = q_ref[...]
    for index in range(chunks):

        @pl.when(place == index)
        def _():
            wide = (index + 1) * block
            parts = []
            for head in range(2):
                mine = (lane // HD) == head
                masked = jnp.where(mine, queries, 0) * jnp.asarray(HD**-0.5, LOW)
                scores = contract(masked, k_ref[:wide], 1, 1) + key_bias_ref[:, :wide]
                last = scores[:, wide - block :] + causal_ref[...]
                scores = last if index == 0 else jnp.concatenate([scores[:, : wide - block], last], axis=1)
                highest = jnp.max(scores, axis=1, keepdims=True)
                weights = jnp.exp(scores - highest)
                total = jnp.sum(weights, axis=1, keepdims=True)
                parts.append(contract(weights.astype(LOW), v_ref[:wide], 1, 0) / total)
                spread = jnp.broadcast_to(highest + jnp.log(total), (block, 128))
                lse_ref[0, 0, head : head + 1, :] = spread.T[:1]
            o_ref[...] = jnp.where(lane < HD, parts[0], parts[1]).astype(LOW)


def attention_out(queries, keys, values, key_bias, causal):
    rows, width = queries.shape
    block = causal.shape[0]
    pairs, chunks = width // 128, rows // block
    row_spec = pl.BlockSpec((block, 128), lambda p, r: (r, p))
    full_spec = pl.BlockSpec((rows, 128), lambda p, r: (0, p))
    return pl.pallas_call(
        attention_out_kernel,
        grid=(pairs, chunks),
        in_specs=[
            row_spec,
            full_spec,
            full_spec,
            pl.BlockSpec((1, rows), lambda p, r: (0, 0)),
            pl.BlockSpec((block, block), lambda p, r: (0, 0)),
        ],
        out_specs=[row_spec, pl.BlockSpec((1, 1, 2, block), lambda p, r: (p, r, 0, 0))],
        out_shape=[
            jax.ShapeDtypeStruct((rows, width), LOW),
            jax.ShapeDtypeStruct((pairs, chunks, 2, block), F32),
        ],
        compiler_params=pltpu.CompilerParams(vmem_limit_bytes=VMEM_LIMIT),
        cost_estimate=pl.CostEstimate(flops=40_000_000_000, bytes_accessed=4_000_000, transcendentals=0),
        name="attention_out",
    )(queries, keys, values, key_bias.reshape(1, rows), causal)


def attention_back_kernel(
    q_ref, k_ref, v_ref, do_ref, o_ref, lse_ref, key_bias_ref, causal_ref, dq_ref, dk_ref, dv_ref, dk_sum, dv_sum
):
    block = q_ref.shape[0]
    chunks = k_ref.shape[0] // block
    place = pl.program_id(1)
    lane = lax.broadcasted_iota(jnp.int32, q_ref.shape, 1)
    queries = q_ref[...]
    grads = do_ref[...]
    inner = (grads.astype(F32) * o_ref[...].astype(F32)).T

    @pl.when(place == 0)
    def _():
        dk_sum[...] = jnp.zeros_like(dk_sum)
        dv_sum[...] = jnp.zeros_like(dv_sum)

    for index in range(chunks):

        @pl.when(place == index)
        def _():
            wide = (index + 1) * block
            parts = []
            for head in range(2):
                mine = (lane // HD) == head
                masked = jnp.where(mine, queries, 0) * jnp.asarray(HD**-0.5, LOW)
                masked_grads = jnp.where(mine, grads, 0)
                inner_row = jnp.sum(inner[head * HD : (head + 1) * HD], axis=0, keepdims=True)
                scores = contract(k_ref[:wide], masked, 1, 1) + key_bias_ref[:wide]
                last = scores[wide - block :] + causal_ref[...]
                scores = last if index == 0 else jnp.concatenate([scores[: wide - block], last], axis=0)
                weights = jnp.exp(scores - lse_ref[0, 0, head : head + 1, :])
                grad_weights = contract(v_ref[:wide], masked_grads, 1, 1)
                grad_scores = (weights * (grad_weights - inner_row)).astype(LOW)
                dv_sum[:wide] += contract(weights.astype(LOW), masked_grads, 1, 0)
                dk_sum[:wide] += contract(grad_scores, masked, 1, 0)
                parts.append(contract(grad_scores, k_ref[:wide], 0, 0))
            dq_ref[...] = (jnp.where(lane < HD, parts[0], parts[1]) * HD**-0.5).astype(LOW)

    @pl.when(place == chunks - 1)
    def _():
        dk_ref[...] = dk_sum[...].astype(LOW)
        dv_ref[...] = dv_sum[...].astype(LOW)


def attention_back(queries, keys, values, grads, attended, lse, key_bias, causal):
    rows, width = queries.shape
    block = causal.shape[0]
    pairs, chunks = width // 128, rows // block
    row_spec = pl.BlockSpec((block, 128), lambda p, r: (r, p))
    full_spec = pl.BlockSpec((rows, 128), lambda p, r: (0, p))
    return pl.pallas_call(
        attention_back_kernel,
        grid=(pairs, chunks),
        in_specs=[
            row_spec,
            full_spec,
            full_spec,
            row_spec,
            row_spec,
            pl.BlockSpec((1, 1, 2, block), lambda p, r: (p, r, 0, 0)),
            pl.BlockSpec((rows, 1), lambda p, r: (0, 0)),
            pl.BlockSpec((block, block), lambda p, r: (0, 0)),
        ],
        out_specs=[row_spec, full_spec, full_spec],
        out_shape=[jax.ShapeDtypeStruct((rows, width), LOW)] * 3,
        scratch_shapes=[pltpu.VMEM((rows, 128), F32)] * 2,
        compiler_params=pltpu.CompilerParams(vmem_limit_bytes=VMEM_LIMIT),
        cost_estimate=pl.CostEstimate(flops=80_000_000_000, bytes_accessed=6_000_000, transcendentals=0),
        name="attention_back",
    )(queries, keys, values, grads, attended, lse, key_bias.reshape(rows, 1), causal.T)


def swap(array, axis, flip):
    size = lax.axis_size(axis)
    return lax.ppermute(array, axis, [(place, place ^ flip) for place in range(size)])


def gather_rows(own):
    core = swap(own, "col", 1)
    far = swap(own, "col", 2)
    return jnp.stack([own, core, far, swap(far, "col", 1)], axis=1)


def scatter_rows(partial_sum):
    arrived = swap(partial_sum[:, 1::2], "col", 1)
    kept = partial_sum[:, 0::2] + arrived
    return kept[:, 0] + swap(kept[:, 1].astype(LOW), "col", 2).astype(F32)


def trade_rows(array):
    return lax.all_to_all(array, "row", split_axis=0, concat_axis=0)


def scatter_blocks(gradient, dim):
    dp_place = lax.axis_index("dp")
    row_place = lax.axis_index("row")
    total = gradient
    for axis, flip, place in (("dp", 1, dp_place), ("row", 2, row_place // 2), ("row", 1, row_place % 2)):
        half = total.shape[dim] // 2
        mine = lax.dynamic_slice_in_dim(total, place * half, half, dim)
        other = lax.dynamic_slice_in_dim(total, (1 - place) * half, half, dim)
        total = mine + swap(other.astype(LOW), axis, flip).astype(F32)
    return total


def norm_parts(values):
    centered = values - jnp.mean(values, axis=-1, keepdims=True)
    scale = lax.rsqrt(jnp.mean(centered * centered, axis=-1, keepdims=True) + EPSILON)
    return centered * scale, scale


def norm_back(grads, gain, unit, scale):
    inner = grads * gain
    mean_inner = jnp.mean(inner, axis=-1, keepdims=True)
    mean_unit = jnp.mean(inner * unit, axis=-1, keepdims=True)
    return scale * (inner - mean_inner - unit * mean_unit)


def local_sequence(
    tokens,
    lengths,
    first_gain,
    first_shift,
    w_query,
    w_key,
    w_value,
    bias_query,
    bias_value,
    w_output,
    bias_output,
    second_gain,
    second_shift,
    w_up,
    bias_up,
    w_down,
    bias_down,
    cotangent,
):
    micro_count, own_rows, width = tokens.shape
    col_count = lax.axis_size("col")
    row_place = lax.axis_index("row")
    col_place = lax.axis_index("col")
    chunk = own_rows * col_count
    seq_rows = chunk * micro_count
    head_width = w_query.shape[1]
    hidden_width = w_up.shape[1]
    length = lax.dynamic_slice_in_dim(lengths[0], row_place, 1)[0]

    inside = (col_place ^ jnp.arange(col_count, dtype=jnp.int32))[:, None] * own_rows + jnp.arange(
        own_rows, dtype=jnp.int32
    )
    inside = inside.reshape(-1)
    positions = (jnp.arange(micro_count, dtype=jnp.int32)[:, None] * chunk + inside).reshape(-1)
    key_bias = jnp.where(positions < length, 0.0, MASKED).astype(F32)
    causal = jnp.where(inside[None, :] <= inside[:, None], 0.0, MASKED).astype(F32)
    own_positions = positions.reshape(micro_count, col_count, own_rows)[:, 0]
    validity = (own_positions < length).astype(F32)[:, :, None]

    query_key_value = lax.all_gather(
        jnp.concatenate([w_query, w_key, w_value], axis=1), ("dp", "row"), axis=0, tiled=True
    )
    trailing = lax.all_gather(jnp.concatenate([w_output, w_down], axis=0), ("dp", "row"), axis=1, tiled=True)
    output_full, down_full = trailing[:head_width], trailing[head_width:]
    up_full = lax.all_gather(w_up, ("dp", "row"), axis=0, tiled=True)

    inputs_low = trade_rows(tokens)
    inputs = inputs_low.astype(F32)
    grad_result = trade_rows(cotangent).astype(F32) * validity
    tokens_all = gather_rows(inputs_low).reshape(seq_rows, width).astype(F32)
    grad_result_all = gather_rows(grad_result.astype(LOW)).reshape(seq_rows, width)

    normed_all = (norm_parts(tokens_all)[0] * first_gain + first_shift).astype(LOW)
    projected = product(normed_all, query_key_value)
    queries = (projected[:, :head_width] + bias_query).astype(LOW)
    keys = projected[:, head_width : 2 * head_width].astype(LOW)
    values = (projected[:, 2 * head_width :] + bias_value).astype(LOW)
    attended, lse = attention_out(queries, keys, values, key_bias, causal)

    def split_rows(array):
        return array.reshape(micro_count, col_count, own_rows, -1)

    branch = scatter_rows(split_rows(product(attended, output_full))) + bias_output
    middle = inputs + branch
    unit, scale = norm_parts(middle)
    second_normed = (unit * second_gain + second_shift).astype(LOW)
    second_all = gather_rows(second_normed).reshape(seq_rows, width)
    pre_activation = product(second_all, up_full) + bias_up
    activated = gelu_tanh(pre_activation).astype(LOW)
    result = middle + scatter_rows(split_rows(product(activated, down_full))) + bias_down
    result = trade_rows(result.astype(LOW))

    grad_down = transposed_left(activated, grad_result_all)
    grad_activated = transposed_right(grad_result_all, down_full)
    gelu_back = jax.vjp(gelu_tanh, pre_activation)[1]
    grad_pre = gelu_back(grad_activated)[0].astype(LOW)
    grad_up = transposed_left(second_all, grad_pre)
    grad_second = scatter_rows(split_rows(transposed_right(grad_pre, up_full)))
    grad_middle = grad_result + norm_back(grad_second, second_gain, unit, scale)
    grad_branch = grad_middle.astype(LOW)
    grad_branch_all = gather_rows(grad_branch).reshape(seq_rows, width)
    grad_output = transposed_left(attended, grad_branch_all)
    grad_attended = transposed_right(grad_branch_all, output_full).astype(LOW)
    grad_queries, grad_keys, grad_values = attention_back(
        queries, keys, values, grad_attended, attended, lse, key_bias, causal
    )
    grad_projected = jnp.concatenate([grad_queries, grad_keys, grad_values], axis=1)
    grad_w = transposed_left(normed_all, grad_projected)
    grad_first = scatter_rows(split_rows(transposed_right(grad_projected, query_key_value)))
    first_unit, first_scale = norm_parts(inputs)
    grad_tokens = grad_middle + norm_back(grad_first, first_gain, first_unit, first_scale)
    grad_tokens = trade_rows(grad_tokens.astype(LOW))

    grad_w = scatter_blocks(grad_w, 0)
    grad_trailing = scatter_blocks(jnp.concatenate([grad_output, grad_down], axis=0), 1)
    grad_up = scatter_blocks(grad_up, 0)

    def over_rows(array):
        return jnp.sum(array.astype(F32).reshape(-1, array.shape[-1]), axis=0)

    shared = lax.psum(
        jnp.stack(
            [
                over_rows(grad_first * first_unit),
                over_rows(grad_first),
                over_rows(grad_branch),
                over_rows(grad_second * unit),
                over_rows(grad_second),
                over_rows(grad_result),
            ]
        ),
        ("dp", "row", "col"),
    )
    by_col = lax.psum(
        jnp.concatenate([over_rows(grad_queries), over_rows(grad_values), over_rows(grad_pre)]), ("dp", "row")
    )
    return (
        result,
        grad_tokens,
        shared[0],
        shared[1],
        grad_w[:, :head_width],
        grad_w[:, head_width : 2 * head_width],
        grad_w[:, 2 * head_width :],
        by_col[:head_width],
        by_col[head_width : 2 * head_width],
        grad_trailing[:head_width],
        shared[2],
        shared[3],
        shared[4],
        grad_up,
        by_col[2 * head_width :],
        grad_trailing[head_width:],
        shared[5],
    )


def solution(mesh):
    return jax.shard_map(
        local_sequence if fits(mesh) else local_general,
        mesh=mesh,
        in_specs=(
            P(None, ("dp", "row", "col"), None),
            P("dp", None),
            P(),
            P(),
            P(("dp", "row"), "col"),
            P(("dp", "row"), "col"),
            P(("dp", "row"), "col"),
            P("col"),
            P("col"),
            P("col", ("dp", "row")),
            P(),
            P(),
            P(),
            P(("dp", "row"), "col"),
            P("col"),
            P("col", ("dp", "row")),
            P(),
            P(None, ("dp", "row", "col"), None),
        ),
        out_specs=(
            P(None, ("dp", "row", "col"), None),
            P(None, ("dp", "row", "col"), None),
            P(),
            P(),
            P(("dp", "row"), "col"),
            P(("dp", "row"), "col"),
            P(("dp", "row"), "col"),
            P("col"),
            P("col"),
            P("col", ("dp", "row")),
            P(),
            P(),
            P(),
            P(("dp", "row"), "col"),
            P("col"),
            P("col", ("dp", "row")),
            P(),
        ),
        check_vma=False,
    )
```

```python
import functools

import jax
import jax.numpy as jnp
from jax import lax
from jax.experimental import pallas as pl
from jax.experimental.pallas import tpu as pltpu
from jax.sharding import PartitionSpec as P

HD = 64


EPSILON = 1e-05
MASKED = -1e30


def layer_norm(values, norm_gain, norm_shift):
    centered = values - jnp.mean(values, axis=-1, keepdims=True)
    variance = jnp.mean(centered * centered, axis=-1, keepdims=True)
    return centered * lax.rsqrt(variance + EPSILON) * norm_gain + norm_shift


def gelu_tanh(values):
    return jax.nn.gelu(values, approximate=True)


def product(former, latter):
    return jnp.dot(former, latter, preferred_element_type=jnp.float32)


def transposed_left(former, latter):
    return lax.dot_general(
        former, latter, (((0,), (0,)), ((), ())), preferred_element_type=jnp.float32
    )


def transposed_right(former, latter):
    return lax.dot_general(
        former, latter, (((1,), (1,)), ((), ())), preferred_element_type=jnp.float32
    )


def spread_rows(rows_block):
    return lax.all_gather(rows_block, "col", axis=0, tiled=True)


def fold_rows(partial_sum):
    return lax.psum_scatter(partial_sum, "col", scatter_dimension=0, tiled=True)


def fetch_weights(w_query, w_key, w_value, w_up, w_output, w_down):
    leading = (
        lax.all_gather(w_query, ("dp", "row"), axis=0, tiled=True),
        lax.all_gather(w_key, ("dp", "row"), axis=0, tiled=True),
        lax.all_gather(w_value, ("dp", "row"), axis=0, tiled=True),
        lax.all_gather(w_up, ("dp", "row"), axis=0, tiled=True),
    )
    trailing = (
        lax.all_gather(w_output, ("dp", "row"), axis=1, tiled=True),
        lax.all_gather(w_down, ("dp", "row"), axis=1, tiled=True),
    )
    return tuple(leading) + tuple(trailing)


def reduce_blocks(gradients):
    leading = (
        lax.psum_scatter(gradients[0], ("dp", "row"), scatter_dimension=0, tiled=True),
        lax.psum_scatter(gradients[1], ("dp", "row"), scatter_dimension=0, tiled=True),
        lax.psum_scatter(gradients[2], ("dp", "row"), scatter_dimension=0, tiled=True),
        lax.psum_scatter(gradients[3], ("dp", "row"), scatter_dimension=0, tiled=True),
    )
    trailing = (
        lax.psum_scatter(gradients[4], ("dp", "row"), scatter_dimension=1, tiled=True),
        lax.psum_scatter(gradients[5], ("dp", "row"), scatter_dimension=1, tiled=True),
    )
    return tuple(leading) + tuple(trailing)


def heads_of(rows_block):
    return rows_block.reshape(rows_block.shape[0], -1, HD)


def block_of(rows_all, start, block_rows):
    return heads_of(lax.dynamic_slice_in_dim(rows_all, start, block_rows, 0))


def block_scores(query_heads, key_heads, query_start, key_start, length):
    block_rows = query_heads.shape[0]
    scores = jnp.einsum(
        "qhd,khd->hqk", query_heads, key_heads, preferred_element_type=jnp.float32
    ) * HD ** (-0.5)
    query_pos = query_start + jnp.arange(block_rows, dtype=jnp.int32)
    key_pos = key_start + jnp.arange(key_heads.shape[0], dtype=jnp.int32)
    allowed = (key_pos[None, :] <= query_pos[:, None]) & (key_pos[None, :] < length)
    return jnp.where(allowed[None], scores, MASKED)


def key_block_count(row_place, length, block_rows):
    return jnp.minimum(row_place + 1, (length + block_rows - 1) // block_rows)


def attention_forward(queries, key_rows, value_rows, row_place, length):
    block_rows = queries.shape[0]
    query_heads = heads_of(queries)
    head_count = query_heads.shape[1]
    query_start = row_place * block_rows
    count = key_block_count(row_place, length, block_rows)

    def stats_step(block_index, carry):
        highest, partition = carry
        start = block_index * block_rows
        scores = block_scores(
            query_heads, block_of(key_rows, start, block_rows), query_start, start, length
        )
        newest = jnp.maximum(highest, jnp.max(scores, axis=-1, keepdims=True))
        partition = partition * jnp.exp(highest - newest) + jnp.sum(
            jnp.exp(scores - newest), axis=-1, keepdims=True
        )
        return (newest, partition)

    start_stats = (
        jnp.full((head_count, block_rows, 1), MASKED, jnp.float32),
        jnp.zeros((head_count, block_rows, 1), jnp.float32),
    )
    highest, partition = lax.fori_loop(0, count, stats_step, start_stats)

    def output_step(block_index, total):
        start = block_index * block_rows
        scores = block_scores(
            query_heads, block_of(key_rows, start, block_rows), query_start, start, length
        )
        weights_low = (jnp.exp(scores - highest) / partition).astype(jnp.bfloat16)
        return total + jnp.einsum(
            "hqk,khd->qhd",
            weights_low,
            block_of(value_rows, start, block_rows),
            preferred_element_type=jnp.float32,
        )

    total = lax.fori_loop(0, count, output_step, jnp.zeros(query_heads.shape, jnp.float32))
    return (total.reshape(block_rows, -1), highest, partition)


def attention_query_side(
    queries, key_rows, value_rows, grad_attended, highest, partition, row_place, length
):
    block_rows = queries.shape[0]
    seq_rows = key_rows.shape[0]
    query_heads = heads_of(queries)
    grad_heads = heads_of(grad_attended)
    head_count = query_heads.shape[1]
    query_start = row_place * block_rows
    count = key_block_count(row_place, length, block_rows)

    def inner_step(block_index, total):
        start = block_index * block_rows
        scores = block_scores(
            query_heads, block_of(key_rows, start, block_rows), query_start, start, length
        )
        weights = jnp.exp(scores - highest) / partition
        grad_weights = jnp.einsum(
            "qhd,khd->hqk",
            grad_heads,
            block_of(value_rows, start, block_rows),
            preferred_element_type=jnp.float32,
        )
        return total + jnp.sum(weights * grad_weights, axis=-1, keepdims=True)

    inner = lax.fori_loop(0, count, inner_step, jnp.zeros((head_count, block_rows, 1), jnp.float32))

    def grad_step(block_index, carry):
        start = block_index * block_rows
        key_heads = block_of(key_rows, start, block_rows)
        scores = block_scores(query_heads, key_heads, query_start, start, length)
        weights = jnp.exp(scores - highest) / partition
        grad_weights = jnp.einsum(
            "qhd,khd->hqk",
            grad_heads,
            block_of(value_rows, start, block_rows),
            preferred_element_type=jnp.float32,
        )
        grad_scores = (weights * (grad_weights - inner)).astype(jnp.bfloat16)
        query_total = carry[0] + jnp.einsum(
            "hqk,khd->qhd", grad_scores, key_heads, preferred_element_type=jnp.float32
        )
        weights_low = weights.astype(jnp.bfloat16)
        key_part = jnp.einsum(
            "hqk,qhd->khd", grad_scores, query_heads, preferred_element_type=jnp.float32
        )
        value_part = jnp.einsum(
            "hqk,qhd->khd", weights_low, grad_heads, preferred_element_type=jnp.float32
        )
        key_total = lax.dynamic_update_slice_in_dim(
            carry[1], lax.dynamic_slice_in_dim(carry[1], start, block_rows, 0) + key_part, start, 0
        )
        value_total = lax.dynamic_update_slice_in_dim(
            carry[2],
            lax.dynamic_slice_in_dim(carry[2], start, block_rows, 0) + value_part,
            start,
            0,
        )
        return (query_total, key_total, value_total)

    start_carry = (jnp.zeros(query_heads.shape, jnp.float32),)
    start_carry = start_carry + (
        jnp.zeros((seq_rows, head_count, HD), jnp.float32),
        jnp.zeros((seq_rows, head_count, HD), jnp.float32),
    )
    totals = lax.fori_loop(0, count, grad_step, start_carry)
    query_terms = totals[0].reshape(block_rows, -1) * HD ** (-0.5)
    return (
        query_terms,
        totals[1].reshape(seq_rows, -1) * HD ** (-0.5),
        totals[2].reshape(seq_rows, -1),
        inner,
    )


def local_general(
    tokens,
    lengths,
    first_gain,
    first_shift,
    w_query,
    w_key,
    w_value,
    bias_query,
    bias_value,
    w_output,
    bias_output,
    second_gain,
    second_shift,
    w_up,
    bias_up,
    w_down,
    bias_down,
    cotangent,
):
    micro_count, own_rows, width = tokens.shape
    col_count = lax.axis_size("col")
    group_rows = own_rows * col_count
    row_place = lax.axis_index("row")
    col_place = lax.axis_index("col")
    head_width = w_query.shape[1]
    hidden_width = w_up.shape[1]
    own_positions = (
        row_place * group_rows + col_place * own_rows + jnp.arange(own_rows, dtype=jnp.int32)
    )
    weight_totals = (
        jnp.zeros((width, head_width), jnp.float32),
        jnp.zeros((width, head_width), jnp.float32),
        jnp.zeros((width, head_width), jnp.float32),
        jnp.zeros((width, hidden_width), jnp.float32),
        jnp.zeros((head_width, width), jnp.float32),
        jnp.zeros((hidden_width, width), jnp.float32),
    )
    vector_totals = (
        jnp.zeros((width,), jnp.float32),
        jnp.zeros((width,), jnp.float32),
        jnp.zeros((head_width,), jnp.float32),
        jnp.zeros((head_width,), jnp.float32),
        jnp.zeros((width,), jnp.float32),
        jnp.zeros((width,), jnp.float32),
        jnp.zeros((width,), jnp.float32),
        jnp.zeros((hidden_width,), jnp.float32),
        jnp.zeros((width,), jnp.float32),
    )
    results = []
    input_grads = []
    for micro_index in range(micro_count):
        gathered = fetch_weights(w_query, w_key, w_value, w_up, w_output, w_down)
        query_full, key_full, value_full, up_full, output_full, down_full = gathered
        length = lengths[0, micro_index]
        inputs = tokens[micro_index].astype(jnp.float32)
        normed = layer_norm(inputs, first_gain, first_shift).astype(jnp.bfloat16)
        normed_all = spread_rows(normed)
        queries = (product(normed_all, query_full) + bias_query).astype(jnp.bfloat16)
        keys_local = product(normed_all, key_full).astype(jnp.bfloat16)
        values_local = (product(normed_all, value_full) + bias_value).astype(jnp.bfloat16)
        keys_all, values_all = (
            lax.all_gather(keys_local, "row", axis=0, tiled=True),
            lax.all_gather(values_local, "row", axis=0, tiled=True),
        )
        attended, maxima, partitions = attention_forward(
            queries, keys_all, values_all, row_place, length
        )
        attended_low = attended.astype(jnp.bfloat16)
        branch = fold_rows(product(attended_low, output_full)) + bias_output
        middle = inputs + branch
        second_normed = layer_norm(middle, second_gain, second_shift).astype(jnp.bfloat16)
        second_all = spread_rows(second_normed)
        pre_activation = product(second_all, up_full) + bias_up
        activated = gelu_tanh(pre_activation).astype(jnp.bfloat16)
        result = middle + (fold_rows(product(activated, down_full)) + bias_down)
        results.append(result.astype(jnp.bfloat16))
        query_full, key_full, value_full, up_full, output_full, down_full = fetch_weights(
            w_query, w_key, w_value, w_up, w_output, w_down
        )
        validity = (own_positions < length).astype(jnp.float32)
        grad_result = cotangent[micro_index].astype(jnp.float32) * validity[:, None]
        grad_result_all = spread_rows(grad_result.astype(jnp.bfloat16))
        grad_down = transposed_left(activated, grad_result_all)
        grad_activated = transposed_right(grad_result_all, down_full)
        gelu_back = jax.vjp(gelu_tanh, pre_activation)[1]
        grad_pre = gelu_back(grad_activated)[0].astype(jnp.bfloat16)
        grad_up = transposed_left(second_all, grad_pre)
        grad_second_normed = fold_rows(transposed_right(grad_pre, up_full))
        second_back = jax.vjp(layer_norm, middle, second_gain, second_shift)[1]
        grad_middle_norm, grad_second_gain, grad_second_shift = second_back(grad_second_normed)
        grad_middle = grad_result + grad_middle_norm
        grad_branch = grad_middle.astype(jnp.bfloat16)
        grad_branch_all = spread_rows(grad_branch)
        grad_output = transposed_left(attended_low, grad_branch_all)
        grad_attended = transposed_right(grad_branch_all, output_full).astype(jnp.bfloat16)
        query_terms, key_terms, value_terms, inner = attention_query_side(
            queries, keys_all, values_all, grad_attended, maxima, partitions, row_place, length
        )
        key_sums, value_sums = (
            lax.psum_scatter(key_terms, "row", scatter_dimension=0, tiled=True),
            lax.psum_scatter(value_terms, "row", scatter_dimension=0, tiled=True),
        )
        grad_queries = query_terms.astype(jnp.bfloat16)
        grad_keys = key_sums.astype(jnp.bfloat16)
        grad_values = value_sums.astype(jnp.bfloat16)
        grad_query = transposed_left(normed_all, grad_queries)
        grad_key = transposed_left(normed_all, grad_keys)
        grad_value = transposed_left(normed_all, grad_values)
        grad_normed = fold_rows(
            transposed_right(grad_queries, query_full)
            + transposed_right(grad_keys, key_full)
            + transposed_right(grad_values, value_full)
        )
        first_back = jax.vjp(layer_norm, inputs, first_gain, first_shift)[1]
        grad_inputs_norm, grad_first_gain, grad_first_shift = first_back(grad_normed)
        input_grads.append((grad_middle + grad_inputs_norm).astype(jnp.bfloat16))
        local_grads = (grad_query, grad_key, grad_value, grad_up, grad_output, grad_down)
        weight_totals = tuple(
            (former + latter for former, latter in zip(weight_totals, local_grads))
        )
        local_vectors = (
            grad_first_gain,
            grad_first_shift,
            jnp.sum(grad_queries.astype(jnp.float32), axis=0),
            jnp.sum(grad_values.astype(jnp.float32), axis=0),
            jnp.sum(grad_branch.astype(jnp.float32), axis=0),
            grad_second_gain,
            grad_second_shift,
            jnp.sum(grad_pre.astype(jnp.float32), axis=0),
            jnp.sum(grad_result, axis=0),
        )
        vector_totals = tuple(
            (former + latter for former, latter in zip(vector_totals, local_vectors))
        )
    weight_totals = reduce_blocks(weight_totals)

    def widen(vector_part):
        blank = jnp.zeros((vector_part.shape[0] * col_count,), jnp.float32)
        return lax.dynamic_update_slice(blank, vector_part, (col_place * vector_part.shape[0],))

    def narrow(whole_vector, piece_width):
        return lax.dynamic_slice_in_dim(whole_vector, col_place * piece_width, piece_width)

    (
        sum_first_gain,
        sum_first_shift,
        sum_bias_query,
        sum_bias_value,
        sum_bias_output,
        sum_second_gain,
        sum_second_shift,
        sum_bias_up,
        sum_bias_down,
    ) = lax.psum(
        (
            vector_totals[0],
            vector_totals[1],
            widen(vector_totals[2]),
            widen(vector_totals[3]),
            vector_totals[4],
            vector_totals[5],
            vector_totals[6],
            widen(vector_totals[7]),
            vector_totals[8],
        ),
        ("dp", "row", "col"),
    )
    grad_w_query, grad_w_key, grad_w_value, grad_w_up, grad_w_output, grad_w_down = weight_totals
    return (
        jnp.stack(results, axis=0),
        jnp.stack(input_grads, axis=0),
        sum_first_gain,
        sum_first_shift,
        grad_w_query,
        grad_w_key,
        grad_w_value,
        narrow(sum_bias_query, head_width),
        narrow(sum_bias_value, head_width),
        grad_w_output,
        sum_bias_output,
        sum_second_gain,
        sum_second_shift,
        grad_w_up,
        narrow(sum_bias_up, hidden_width),
        grad_w_down,
        sum_bias_down,
    )


F32 = jnp.float32
LOW = jnp.bfloat16
VMEM_LIMIT = 56 * 1024 * 1024


def fits(mesh):
    return mesh.shape["row"] == 4 and mesh.shape["col"] == 4 and mesh.shape["dp"] == 2


def contract(former, latter, former_dim, latter_dim):
    return lax.dot_general(
        former,
        latter,
        (((former_dim,), (latter_dim,)), ((), ())),
        preferred_element_type=jnp.float32,
    )


def attention_out_kernel(q_ref, k_ref, v_ref, key_bias_ref, causal_ref, o_ref, lse_ref):
    block = q_ref.shape[0]
    chunks = k_ref.shape[0] // block
    place = pl.program_id(1)
    lane = lax.broadcasted_iota(jnp.int32, q_ref.shape, 1)
    queries = q_ref[...]
    for index in range(chunks):

        @pl.when(place == index)
        def _():
            wide = (index + 1) * block
            parts = []
            for head in range(2):
                mine = (lane // HD) == head
                masked = jnp.where(mine, queries, 0) * jnp.asarray(HD**-0.5, LOW)
                scores = contract(masked, k_ref[:wide], 1, 1) + key_bias_ref[:, :wide]
                last = scores[:, wide - block :] + causal_ref[...]
                scores = last if index == 0 else jnp.concatenate([scores[:, : wide - block], last], axis=1)
                highest = jnp.max(scores, axis=1, keepdims=True)
                weights = jnp.exp(scores - highest)
                total = jnp.sum(weights, axis=1, keepdims=True)
                parts.append(contract(weights.astype(LOW), v_ref[:wide], 1, 0) / total)
                spread = jnp.broadcast_to(highest + jnp.log(total), (block, 128))
                lse_ref[0, 0, head : head + 1, :] = spread.T[:1]
            o_ref[...] = jnp.where(lane < HD, parts[0], parts[1]).astype(LOW)


def attention_out(queries, keys, values, key_bias, causal):
    rows, width = queries.shape
    block = causal.shape[0]
    pairs, chunks = width // 128, rows // block
    row_spec = pl.BlockSpec((block, 128), lambda p, r: (r, p))
    full_spec = pl.BlockSpec((rows, 128), lambda p, r: (0, p))
    return pl.pallas_call(
        attention_out_kernel,
        grid=(pairs, chunks),
        in_specs=[
            row_spec,
            full_spec,
            full_spec,
            pl.BlockSpec((1, rows), lambda p, r: (0, 0)),
            pl.BlockSpec((block, block), lambda p, r: (0, 0)),
        ],
        out_specs=[row_spec, pl.BlockSpec((1, 1, 2, block), lambda p, r: (p, r, 0, 0))],
        out_shape=[
            jax.ShapeDtypeStruct((rows, width), LOW),
            jax.ShapeDtypeStruct((pairs, chunks, 2, block), F32),
        ],
        compiler_params=pltpu.CompilerParams(vmem_limit_bytes=VMEM_LIMIT),
        cost_estimate=pl.CostEstimate(flops=40_000_000_000, bytes_accessed=4_000_000, transcendentals=0),
        name="attention_out",
    )(queries, keys, values, key_bias.reshape(1, rows), causal)


def attention_back_kernel(
    q_ref, k_ref, v_ref, do_ref, o_ref, lse_ref, key_bias_ref, causal_ref, dq_ref, dk_ref, dv_ref, dk_sum, dv_sum
):
    block = q_ref.shape[0]
    chunks = k_ref.shape[0] // block
    place = pl.program_id(1)
    lane = lax.broadcasted_iota(jnp.int32, q_ref.shape, 1)
    queries = q_ref[...]
    grads = do_ref[...]
    inner = (grads.astype(F32) * o_ref[...].astype(F32)).T

    @pl.when(place == 0)
    def _():
        dk_sum[...] = jnp.zeros_like(dk_sum)
        dv_sum[...] = jnp.zeros_like(dv_sum)

    for index in range(chunks):

        @pl.when(place == index)
        def _():
            wide = (index + 1) * block
            parts = []
            for head in range(2):
                mine = (lane // HD) == head
                masked = jnp.where(mine, queries, 0) * jnp.asarray(HD**-0.5, LOW)
                masked_grads = jnp.where(mine, grads, 0)
                inner_row = jnp.sum(inner[head * HD : (head + 1) * HD], axis=0, keepdims=True)
                scores = contract(k_ref[:wide], masked, 1, 1) + key_bias_ref[:wide]
                last = scores[wide - block :] + causal_ref[...]
                scores = last if index == 0 else jnp.concatenate([scores[: wide - block], last], axis=0)
                weights = jnp.exp(scores - lse_ref[0, 0, head : head + 1, :])
                grad_weights = contract(v_ref[:wide], masked_grads, 1, 1)
                grad_scores = (weights * (grad_weights - inner_row)).astype(LOW)
                dv_sum[:wide] += contract(weights.astype(LOW), masked_grads, 1, 0)
                dk_sum[:wide] += contract(grad_scores, masked, 1, 0)
                parts.append(contract(grad_scores, k_ref[:wide], 0, 0))
            dq_ref[...] = (jnp.where(lane < HD, parts[0], parts[1]) * HD**-0.5).astype(LOW)

    @pl.when(place == chunks - 1)
    def _():
        dk_ref[...] = dk_sum[...].astype(LOW)
        dv_ref[...] = dv_sum[...].astype(LOW)


def attention_back(queries, keys, values, grads, attended, lse, key_bias, causal):
    rows, width = queries.shape
    block = causal.shape[0]
    pairs, chunks = width // 128, rows // block
    row_spec = pl.BlockSpec((block, 128), lambda p, r: (r, p))
    full_spec = pl.BlockSpec((rows, 128), lambda p, r: (0, p))
    return pl.pallas_call(
        attention_back_kernel,
        grid=(pairs, chunks),
        in_specs=[
            row_spec,
            full_spec,
            full_spec,
            row_spec,
            row_spec,
            pl.BlockSpec((1, 1, 2, block), lambda p, r: (p, r, 0, 0)),
            pl.BlockSpec((rows, 1), lambda p, r: (0, 0)),
            pl.BlockSpec((block, block), lambda p, r: (0, 0)),
        ],
        out_specs=[row_spec, full_spec, full_spec],
        out_shape=[jax.ShapeDtypeStruct((rows, width), LOW)] * 3,
        scratch_shapes=[pltpu.VMEM((rows, 128), F32)] * 2,
        compiler_params=pltpu.CompilerParams(vmem_limit_bytes=VMEM_LIMIT),
        cost_estimate=pl.CostEstimate(flops=80_000_000_000, bytes_accessed=6_000_000, transcendentals=0),
        name="attention_back",
    )(queries, keys, values, grads, attended, lse, key_bias.reshape(rows, 1), causal.T)


def swap(array, axis, flip):
    size = lax.axis_size(axis)
    return lax.ppermute(array, axis, [(place, place ^ flip) for place in range(size)])


def gather_parts(own):
    core = swap(own, "col", 1)
    far = swap(own, "col", 2)
    return own, core, far, swap(far, "col", 1)


def gather_rows(own):
    return jnp.stack(gather_parts(own), axis=1)


def scatter_rows(partial_sum):
    arrived = swap(partial_sum[:, 1::2], "col", 1)
    kept = partial_sum[:, 0::2] + arrived
    return kept[:, 0] + swap(kept[:, 1].astype(LOW), "col", 2).astype(F32)


def trade_rows(array):
    return lax.all_to_all(array, "row", split_axis=0, concat_axis=0)


def scatter_blocks(gradient, dim):
    dp_place = lax.axis_index("dp")
    row_place = lax.axis_index("row")
    total = gradient.astype(F32)
    for axis, flip, place in (("dp", 1, dp_place), ("row", 2, row_place // 2), ("row", 1, row_place % 2)):
        half = total.shape[dim] // 2
        mine = lax.dynamic_slice_in_dim(total, place * half, half, dim)
        other = lax.dynamic_slice_in_dim(total, (1 - place) * half, half, dim)
        total = mine + swap(other.astype(LOW), axis, flip).astype(F32)
    return total


def norm_parts(values):
    centered = values - jnp.mean(values, axis=-1, keepdims=True)
    scale = lax.rsqrt(jnp.mean(centered * centered, axis=-1, keepdims=True) + EPSILON)
    return centered * scale, scale


def norm_back(grads, gain, unit, scale):
    inner = grads * gain
    mean_inner = jnp.mean(inner, axis=-1, keepdims=True)
    mean_unit = jnp.mean(inner * unit, axis=-1, keepdims=True)
    return scale * (inner - mean_inner - unit * mean_unit)


GELU_SCALE = 0.7978845608028654
GELU_CUBE = 0.044715


def gelu_parts(values):
    square = values * values
    curve = jnp.tanh(GELU_SCALE * values * (1.0 + GELU_CUBE * square))
    half = 0.5 + 0.5 * curve
    slope = half + 0.5 * values * (1.0 - curve * curve) * (GELU_SCALE * (1.0 + 3.0 * GELU_CUBE * square))
    return values * half, slope


def peers():
    place = lax.axis_index("col")
    return {"col": place + 1 - 2 * (place % 2)}, {"col": (place + 2) % 4}


def greet(devices):
    barrier = pltpu.get_barrier_semaphore()
    for device in devices:
        pl.semaphore_signal(barrier, inc=1, device_id=device, device_id_type=pl.DeviceIdType.MESH)
    pl.semaphore_wait(barrier, len(devices))


def remote(source, target, send_sem, recv_sem, device):
    return pltpu.make_async_remote_copy(
        src_ref=source,
        dst_ref=target,
        send_sem=send_sem,
        recv_sem=recv_sem,
        device_id=device,
        device_id_type=pl.DeviceIdType.MESH,
    )


def feed_kernel(
    att_ref,
    wo_ref,
    wu_ref,
    wd_ref,
    tok_ref,
    g0_ref,
    g1_ref,
    g2_ref,
    g3_ref,
    vec_ref,
    bias_up_ref,
    result_ref,
    gatt_ref,
    gmid_ref,
    gout_ref,
    gup_ref,
    gdown_ref,
    sums_ref,
    sum_up_ref,
    g_all,
    kept,
    kept_q,
    core_out,
    core_in,
    core_in_q,
    far_out,
    far_in,
    far_out_q,
    far_in_q,
    middle,
    second,
    act,
    gpre,
    branch,
    stage,
    local_sems,
    stage_sems,
    send_sems,
    recv_sems,
):
    chunks, blocks, own, width = second.shape
    rows = blocks * own
    hidden = wu_ref.shape[1]
    core, far = peers()

    for j, source in enumerate((g0_ref, g1_ref, g2_ref, g3_ref)):
        pltpu.make_async_copy(source, g_all.at[:, j], local_sems.at[j]).start()

    def core_copy(step, r, source, target):
        return remote(source.at[r], target.at[r], send_sems.at[step, r], recv_sems.at[step, r], core)

    def far_copy(step, r, source, target):
        return remote(source.at[r], target.at[r], send_sems.at[step, r], recv_sems.at[step, r], far)

    def spread_core(step, r, rows_ref):
        return remote(rows_ref.at[r, 0], rows_ref.at[r, 1], send_sems.at[step, r], recv_sems.at[step, r], core)

    def spread_far(step, r, rows_ref):
        return remote(rows_ref.at[r, 0], rows_ref.at[r, 2], send_sems.at[step, r], recv_sems.at[step, r], far)

    def spread_relay(step, r, rows_ref):
        return remote(rows_ref.at[r, 2], rows_ref.at[r, 3], send_sems.at[step, r], recv_sems.at[step, r], core)

    def split(r, total, kept_ref, out_ref):
        kept_ref[r, 0] = total[:own].astype(kept_ref.dtype)
        out_ref[r, 0] = total[own : 2 * own].astype(LOW)
        kept_ref[r, 1] = total[2 * own : 3 * own].astype(kept_ref.dtype)
        out_ref[r, 1] = total[3 * own :].astype(LOW)

    def fold(r, kept_ref, in_ref, out_ref):
        out_ref[r] = (kept_ref[r, 1].astype(F32) + in_ref[r, 1].astype(F32)).astype(LOW)
        kept_ref[r, 0] = (kept_ref[r, 0].astype(F32) + in_ref[r, 0].astype(F32)).astype(kept_ref.dtype)

    def each(body):
        lax.fori_loop(0, chunks, lambda r, carry: (body(r), carry)[1], 0)

    greet((core, far))

    def out_projection(r):
        rows_here = pl.ds(pl.multiple_of(r * rows, rows), rows)
        split(r, contract(att_ref[rows_here], wo_ref[...], 1, 0), kept, core_out)
        core_copy(0, r, core_out, core_in).start()

    each(out_projection)

    def out_fold(r):
        core_copy(0, r, core_out, core_in).wait()
        fold(r, kept, core_in, far_out)
        far_copy(1, r, far_out, far_in).start()

    each(out_fold)

    def norm(r):
        far_copy(1, r, far_out, far_in).wait()
        values = tok_ref[r].astype(F32) + (kept[r, 0] + far_in[r].astype(F32) + vec_ref[0:1])
        middle[r] = values
        second[r, 0] = (norm_parts(values)[0] * vec_ref[1:2] + vec_ref[2:3]).astype(LOW)
        spread_core(2, r, second).start()
        spread_far(3, r, second).start()

    each(norm)
    for j, source in enumerate((g0_ref, g1_ref, g2_ref, g3_ref)):
        pltpu.make_async_copy(source, g_all.at[:, j], local_sems.at[j]).wait()

    sum_up_ref[...] = jnp.zeros_like(sum_up_ref)

    def feed(r):
        spread_far(3, r, second).wait()
        spread_relay(4, r, second).start()
        spread_core(2, r, second).wait()
        spread_relay(4, r, second).wait()
        pre = contract(second[r].reshape(rows, width), wu_ref[...], 1, 0) + bias_up_ref[...]
        activated, slope = gelu_parts(pre)
        act[r] = activated.astype(LOW).reshape(blocks, own, hidden)
        grads = contract(g_all[r].reshape(rows, width), wd_ref[...], 1, 1) * slope
        grads_low = grads.astype(LOW)
        gpre[r] = grads_low.reshape(blocks, own, hidden)
        sum_up_ref[...] += jnp.sum(grads_low.astype(F32), axis=0, keepdims=True)
        split(r, contract(grads_low, wu_ref[...], 1, 1), kept, core_out)
        core_copy(5, r, core_out, core_in).start()
        core_copy(5, r, core_out, core_in).wait()
        fold(r, kept, core_in, far_out)
        far_copy(6, r, far_out, far_in).start()
        split(r, contract(act[r].reshape(rows, hidden), wd_ref[...], 1, 0), kept_q, core_out)
        core_copy(7, r, core_out, core_in_q).start()

    each(feed)
    sums_ref[...] = jnp.zeros_like(sums_ref)

    def norm_grad(r):
        far_copy(6, r, far_out, far_in).wait()
        grads = kept[r, 0] + far_in[r].astype(F32)
        unit, scale = norm_parts(middle[r])
        place = g_all[r, 0].astype(F32)
        total = place + norm_back(grads, vec_ref[1:2], unit, scale)
        gmid_ref[r] = total
        low = total.astype(LOW)
        branch[r, 0] = low
        spread_core(9, r, branch).start()
        spread_far(10, r, branch).start()
        sums_ref[0:1] += jnp.sum(low.astype(F32), axis=0, keepdims=True)
        sums_ref[1:2] += jnp.sum(grads * unit, axis=0, keepdims=True)
        sums_ref[2:3] += jnp.sum(grads, axis=0, keepdims=True)
        sums_ref[3:4] += jnp.sum(place, axis=0, keepdims=True)

    each(norm_grad)

    def result_fold(r):
        core_copy(7, r, core_out, core_in_q).wait()
        fold(r, kept_q, core_in_q, far_out_q)
        far_copy(8, r, far_out_q, far_in_q).start()

    each(result_fold)

    wide = 256
    flat_second = second.reshape(chunks * rows, width)
    flat_act = act.reshape(chunks * rows, hidden)
    flat_gpre = gpre.reshape(chunks * rows, hidden)
    flat_g = g_all.reshape(chunks * rows, width)
    flat_branch = branch.reshape(chunks * rows, width)

    def down_grad(t):
        part = pl.ds(pl.multiple_of(t * wide, wide), wide)
        total = contract(flat_act[:, part], flat_g[...], 0, 0).astype(LOW)
        for b in range(8):
            stage[b] = total[:, b * own : (b + 1) * own]
        copy = pltpu.make_async_copy(stage, gdown_ref.at[:, part], stage_sems.at[0])
        copy.start()
        copy.wait()

    lax.fori_loop(0, hidden // wide, lambda t, c: (down_grad(t), c)[1], 0)

    def attended_grad(r):
        spread_far(10, r, branch).wait()
        spread_relay(11, r, branch).start()
        spread_core(9, r, branch).wait()
        spread_relay(11, r, branch).wait()
        rows_here = pl.ds(pl.multiple_of(r * rows, rows), rows)
        gatt_ref[rows_here] = contract(branch[r].reshape(rows, width), wo_ref[...], 1, 1).astype(LOW)

    each(attended_grad)

    def up_grad(t):
        part = pl.ds(pl.multiple_of(t * wide, wide), wide)
        total = contract(flat_second[:, part], flat_gpre[...], 0, 0).astype(LOW)
        for b in range(2):
            gup_ref[2 * t + b] = total[b * own : (b + 1) * own]

    lax.fori_loop(0, width // wide, lambda t, c: (up_grad(t), c)[1], 0)
    total_out = contract(att_ref[...], flat_branch[...], 0, 0).astype(LOW)
    for b in range(8):
        gout_ref[b] = total_out[:, b * own : (b + 1) * own]

    def finish(r):
        far_copy(8, r, far_out_q, far_in_q).wait()
        total = kept_q[r, 0].astype(F32) + far_in_q[r].astype(F32)
        result_ref[r] = (middle[r] + (total + vec_ref[3:4])).astype(LOW)

    each(finish)


def feed_block(attended, w_output, w_up, w_down, own_tokens, grads, vectors, bias_up):
    chunks, own, width = own_tokens.shape
    rows = chunks * 4 * own
    head_width = w_output.shape[0]
    hidden = w_up.shape[1]
    half = (chunks, 2, own, width)
    one = (chunks, own, width)
    all_rows = (chunks, 4, own, width)
    vmem = pl.BlockSpec(memory_space=pltpu.VMEM)
    hbm = pl.BlockSpec(memory_space=pl.ANY)
    return pl.pallas_call(
        feed_kernel,
        in_specs=[vmem] * 5 + [hbm] * 4 + [vmem] * 2,
        out_specs=[vmem] * 5 + [hbm] + [vmem] * 2,
        out_shape=[
            jax.ShapeDtypeStruct(one, LOW),
            jax.ShapeDtypeStruct((rows, head_width), LOW),
            jax.ShapeDtypeStruct(one, F32),
            jax.ShapeDtypeStruct((8, head_width, width // 8), LOW),
            jax.ShapeDtypeStruct((8, width // 8, hidden), LOW),
            jax.ShapeDtypeStruct((8, hidden, width // 8), LOW),
            jax.ShapeDtypeStruct((8, width), F32),
            jax.ShapeDtypeStruct((1, hidden), F32),
        ],
        scratch_shapes=[
            pltpu.VMEM(all_rows, LOW),
            pltpu.VMEM(half, F32),
            pltpu.VMEM(half, LOW),
            pltpu.VMEM(half, LOW),
            pltpu.VMEM(half, LOW),
            pltpu.VMEM(half, LOW),
            pltpu.VMEM(one, LOW),
            pltpu.VMEM(one, LOW),
            pltpu.VMEM(one, LOW),
            pltpu.VMEM(one, LOW),
            pltpu.VMEM(one, F32),
            pltpu.VMEM(all_rows, LOW),
            pltpu.VMEM((chunks, 4, own, hidden), LOW),
            pltpu.VMEM((chunks, 4, own, hidden), LOW),
            pltpu.VMEM(all_rows, LOW),
            pltpu.VMEM((8, 256, width // 8), LOW),
            pltpu.SemaphoreType.DMA((4,)),
            pltpu.SemaphoreType.DMA((2,)),
            pltpu.SemaphoreType.DMA((12, chunks)),
            pltpu.SemaphoreType.DMA((12, chunks)),
        ],
        compiler_params=pltpu.CompilerParams(
            collective_id=1, has_side_effects=True, vmem_limit_bytes=61 * 1024 * 1024
        ),
        cost_estimate=pl.CostEstimate(flops=100_000_000_000, bytes_accessed=30_000_000, transcendentals=0),
        name="feed_block",
    )(attended, w_output, w_up, w_down, own_tokens, *grads, vectors, bias_up)


def local_sequence(
    tokens,
    lengths,
    first_gain,
    first_shift,
    w_query,
    w_key,
    w_value,
    bias_query,
    bias_value,
    w_output,
    bias_output,
    second_gain,
    second_shift,
    w_up,
    bias_up,
    w_down,
    bias_down,
    cotangent,
):
    micro_count, own_rows, width = tokens.shape
    col_count = lax.axis_size("col")
    row_place = lax.axis_index("row")
    col_place = lax.axis_index("col")
    chunk = own_rows * col_count
    seq_rows = chunk * micro_count
    head_width = w_query.shape[1]
    hidden_width = w_up.shape[1]
    length = lax.dynamic_slice_in_dim(lengths[0], row_place, 1)[0]

    inside = (col_place ^ jnp.arange(col_count, dtype=jnp.int32))[:, None] * own_rows + jnp.arange(
        own_rows, dtype=jnp.int32
    )
    inside = inside.reshape(-1)
    positions = (jnp.arange(micro_count, dtype=jnp.int32)[:, None] * chunk + inside).reshape(-1)
    key_bias = jnp.where(positions < length, 0.0, MASKED).astype(F32)
    causal = jnp.where(inside[None, :] <= inside[:, None], 0.0, MASKED).astype(F32)
    own_positions = positions.reshape(micro_count, col_count, own_rows)[:, 0]
    validity = (own_positions < length).astype(F32)[:, :, None]

    query_key_value = lax.all_gather(
        jnp.concatenate([w_query, w_key, w_value], axis=1), ("dp", "row"), axis=0, tiled=True
    )
    trailing = lax.all_gather(jnp.concatenate([w_output, w_down], axis=0), ("dp", "row"), axis=1, tiled=True)
    output_full, down_full = trailing[:head_width], trailing[head_width:]
    up_full = lax.all_gather(w_up, ("dp", "row"), axis=0, tiled=True)

    inputs_low = trade_rows(tokens)
    inputs = inputs_low.astype(F32)
    grad_result = trade_rows(cotangent).astype(F32) * validity
    tokens_all = gather_rows(inputs_low).reshape(seq_rows, width).astype(F32)
    grad_all = gather_parts(grad_result.astype(LOW))

    normed_all = (norm_parts(tokens_all)[0] * first_gain + first_shift).astype(LOW)
    projected = product(normed_all, query_key_value)
    queries = (projected[:, :head_width] + bias_query).astype(LOW)
    keys = projected[:, head_width : 2 * head_width].astype(LOW)
    values = (projected[:, 2 * head_width :] + bias_value).astype(LOW)
    attended, lse = attention_out(queries, keys, values, key_bias, causal)

    def split_rows(array):
        return array.reshape(micro_count, col_count, own_rows, -1)

    vectors = jnp.concatenate(
        [jnp.stack([bias_output, second_gain, second_shift, bias_down]), jnp.zeros((4, width), F32)]
    )
    result, grad_attended, grad_middle, grad_output, grad_up, grad_down, sums, sum_up = feed_block(
        attended, output_full, up_full, down_full, inputs_low, grad_all, vectors, bias_up.reshape(1, -1)
    )
    result = trade_rows(result)
    grad_queries, grad_keys, grad_values = attention_back(
        queries, keys, values, grad_attended, attended, lse, key_bias, causal
    )
    grad_projected = jnp.concatenate([grad_queries, grad_keys, grad_values], axis=1)
    grad_w = transposed_left(normed_all, grad_projected)
    grad_first = scatter_rows(split_rows(transposed_right(grad_projected, query_key_value)))
    first_unit, first_scale = norm_parts(inputs)
    grad_tokens = grad_middle + norm_back(grad_first, first_gain, first_unit, first_scale)
    grad_tokens = trade_rows(grad_tokens.astype(LOW))

    grad_w = scatter_blocks(grad_w, 0)
    grad_output = scatter_blocks(grad_output, 0)[0]
    grad_down = scatter_blocks(grad_down, 0)[0]
    grad_up = scatter_blocks(grad_up, 0)[0]

    def over_rows(array):
        return jnp.sum(array.astype(F32).reshape(-1, array.shape[-1]), axis=0)

    shared = lax.psum(
        jnp.stack(
            [
                over_rows(grad_first * first_unit),
                over_rows(grad_first),
                sums[0],
                sums[1],
                sums[2],
                sums[3],
            ]
        ),
        ("dp", "row", "col"),
    )
    by_col = lax.psum(
        jnp.concatenate([over_rows(grad_queries), over_rows(grad_values), sum_up[0]]), ("dp", "row")
    )
    return (
        result,
        grad_tokens,
        shared[0],
        shared[1],
        grad_w[:, :head_width],
        grad_w[:, head_width : 2 * head_width],
        grad_w[:, 2 * head_width :],
        by_col[:head_width],
        by_col[head_width : 2 * head_width],
        grad_output,
        shared[2],
        shared[3],
        shared[4],
        grad_up,
        by_col[2 * head_width :],
        grad_down,
        shared[5],
    )


def solution(mesh):
    return jax.shard_map(
        local_sequence if fits(mesh) else local_general,
        mesh=mesh,
        in_specs=(
            P(None, ("dp", "row", "col"), None),
            P("dp", None),
            P(),
            P(),
            P(("dp", "row"), "col"),
            P(("dp", "row"), "col"),
            P(("dp", "row"), "col"),
            P("col"),
            P("col"),
            P("col", ("dp", "row")),
            P(),
            P(),
            P(),
            P(("dp", "row"), "col"),
            P("col"),
            P("col", ("dp", "row")),
            P(),
            P(None, ("dp", "row", "col"), None),
        ),
        out_specs=(
            P(None, ("dp", "row", "col"), None),
            P(None, ("dp", "row", "col"), None),
            P(),
            P(),
            P(("dp", "row"), "col"),
            P(("dp", "row"), "col"),
            P(("dp", "row"), "col"),
            P("col"),
            P("col"),
            P("col", ("dp", "row")),
            P(),
            P(),
            P(),
            P(("dp", "row"), "col"),
            P("col"),
            P("col", ("dp", "row")),
            P(),
        ),
        check_vma=False,
    )
```

```python
import functools

import jax
import jax.numpy as jnp
from jax import lax
from jax.experimental import pallas as pl
from jax.experimental.pallas import tpu as pltpu
from jax.sharding import PartitionSpec as P

HD = 64


EPSILON = 1e-05
MASKED = -1e30


def layer_norm(values, norm_gain, norm_shift):
    centered = values - jnp.mean(values, axis=-1, keepdims=True)
    variance = jnp.mean(centered * centered, axis=-1, keepdims=True)
    return centered * lax.rsqrt(variance + EPSILON) * norm_gain + norm_shift


def gelu_tanh(values):
    return jax.nn.gelu(values, approximate=True)


def product(former, latter):
    return jnp.dot(former, latter, preferred_element_type=jnp.float32)


def transposed_left(former, latter):
    return lax.dot_general(
        former, latter, (((0,), (0,)), ((), ())), preferred_element_type=jnp.float32
    )


def transposed_right(former, latter):
    return lax.dot_general(
        former, latter, (((1,), (1,)), ((), ())), preferred_element_type=jnp.float32
    )


def spread_rows(rows_block):
    return lax.all_gather(rows_block, "col", axis=0, tiled=True)


def fold_rows(partial_sum):
    return lax.psum_scatter(partial_sum, "col", scatter_dimension=0, tiled=True)


def fetch_weights(w_query, w_key, w_value, w_up, w_output, w_down):
    leading = (
        lax.all_gather(w_query, ("dp", "row"), axis=0, tiled=True),
        lax.all_gather(w_key, ("dp", "row"), axis=0, tiled=True),
        lax.all_gather(w_value, ("dp", "row"), axis=0, tiled=True),
        lax.all_gather(w_up, ("dp", "row"), axis=0, tiled=True),
    )
    trailing = (
        lax.all_gather(w_output, ("dp", "row"), axis=1, tiled=True),
        lax.all_gather(w_down, ("dp", "row"), axis=1, tiled=True),
    )
    return tuple(leading) + tuple(trailing)


def reduce_blocks(gradients):
    leading = (
        lax.psum_scatter(gradients[0], ("dp", "row"), scatter_dimension=0, tiled=True),
        lax.psum_scatter(gradients[1], ("dp", "row"), scatter_dimension=0, tiled=True),
        lax.psum_scatter(gradients[2], ("dp", "row"), scatter_dimension=0, tiled=True),
        lax.psum_scatter(gradients[3], ("dp", "row"), scatter_dimension=0, tiled=True),
    )
    trailing = (
        lax.psum_scatter(gradients[4], ("dp", "row"), scatter_dimension=1, tiled=True),
        lax.psum_scatter(gradients[5], ("dp", "row"), scatter_dimension=1, tiled=True),
    )
    return tuple(leading) + tuple(trailing)


def heads_of(rows_block):
    return rows_block.reshape(rows_block.shape[0], -1, HD)


def block_of(rows_all, start, block_rows):
    return heads_of(lax.dynamic_slice_in_dim(rows_all, start, block_rows, 0))


def block_scores(query_heads, key_heads, query_start, key_start, length):
    block_rows = query_heads.shape[0]
    scores = jnp.einsum(
        "qhd,khd->hqk", query_heads, key_heads, preferred_element_type=jnp.float32
    ) * HD ** (-0.5)
    query_pos = query_start + jnp.arange(block_rows, dtype=jnp.int32)
    key_pos = key_start + jnp.arange(key_heads.shape[0], dtype=jnp.int32)
    allowed = (key_pos[None, :] <= query_pos[:, None]) & (key_pos[None, :] < length)
    return jnp.where(allowed[None], scores, MASKED)


def key_block_count(row_place, length, block_rows):
    return jnp.minimum(row_place + 1, (length + block_rows - 1) // block_rows)


def attention_forward(queries, key_rows, value_rows, row_place, length):
    block_rows = queries.shape[0]
    query_heads = heads_of(queries)
    head_count = query_heads.shape[1]
    query_start = row_place * block_rows
    count = key_block_count(row_place, length, block_rows)

    def stats_step(block_index, carry):
        highest, partition = carry
        start = block_index * block_rows
        scores = block_scores(
            query_heads, block_of(key_rows, start, block_rows), query_start, start, length
        )
        newest = jnp.maximum(highest, jnp.max(scores, axis=-1, keepdims=True))
        partition = partition * jnp.exp(highest - newest) + jnp.sum(
            jnp.exp(scores - newest), axis=-1, keepdims=True
        )
        return (newest, partition)

    start_stats = (
        jnp.full((head_count, block_rows, 1), MASKED, jnp.float32),
        jnp.zeros((head_count, block_rows, 1), jnp.float32),
    )
    highest, partition = lax.fori_loop(0, count, stats_step, start_stats)

    def output_step(block_index, total):
        start = block_index * block_rows
        scores = block_scores(
            query_heads, block_of(key_rows, start, block_rows), query_start, start, length
        )
        weights_low = (jnp.exp(scores - highest) / partition).astype(jnp.bfloat16)
        return total + jnp.einsum(
            "hqk,khd->qhd",
            weights_low,
            block_of(value_rows, start, block_rows),
            preferred_element_type=jnp.float32,
        )

    total = lax.fori_loop(0, count, output_step, jnp.zeros(query_heads.shape, jnp.float32))
    return (total.reshape(block_rows, -1), highest, partition)


def attention_query_side(
    queries, key_rows, value_rows, grad_attended, highest, partition, row_place, length
):
    block_rows = queries.shape[0]
    seq_rows = key_rows.shape[0]
    query_heads = heads_of(queries)
    grad_heads = heads_of(grad_attended)
    head_count = query_heads.shape[1]
    query_start = row_place * block_rows
    count = key_block_count(row_place, length, block_rows)

    def inner_step(block_index, total):
        start = block_index * block_rows
        scores = block_scores(
            query_heads, block_of(key_rows, start, block_rows), query_start, start, length
        )
        weights = jnp.exp(scores - highest) / partition
        grad_weights = jnp.einsum(
            "qhd,khd->hqk",
            grad_heads,
            block_of(value_rows, start, block_rows),
            preferred_element_type=jnp.float32,
        )
        return total + jnp.sum(weights * grad_weights, axis=-1, keepdims=True)

    inner = lax.fori_loop(0, count, inner_step, jnp.zeros((head_count, block_rows, 1), jnp.float32))

    def grad_step(block_index, carry):
        start = block_index * block_rows
        key_heads = block_of(key_rows, start, block_rows)
        scores = block_scores(query_heads, key_heads, query_start, start, length)
        weights = jnp.exp(scores - highest) / partition
        grad_weights = jnp.einsum(
            "qhd,khd->hqk",
            grad_heads,
            block_of(value_rows, start, block_rows),
            preferred_element_type=jnp.float32,
        )
        grad_scores = (weights * (grad_weights - inner)).astype(jnp.bfloat16)
        query_total = carry[0] + jnp.einsum(
            "hqk,khd->qhd", grad_scores, key_heads, preferred_element_type=jnp.float32
        )
        weights_low = weights.astype(jnp.bfloat16)
        key_part = jnp.einsum(
            "hqk,qhd->khd", grad_scores, query_heads, preferred_element_type=jnp.float32
        )
        value_part = jnp.einsum(
            "hqk,qhd->khd", weights_low, grad_heads, preferred_element_type=jnp.float32
        )
        key_total = lax.dynamic_update_slice_in_dim(
            carry[1], lax.dynamic_slice_in_dim(carry[1], start, block_rows, 0) + key_part, start, 0
        )
        value_total = lax.dynamic_update_slice_in_dim(
            carry[2],
            lax.dynamic_slice_in_dim(carry[2], start, block_rows, 0) + value_part,
            start,
            0,
        )
        return (query_total, key_total, value_total)

    start_carry = (jnp.zeros(query_heads.shape, jnp.float32),)
    start_carry = start_carry + (
        jnp.zeros((seq_rows, head_count, HD), jnp.float32),
        jnp.zeros((seq_rows, head_count, HD), jnp.float32),
    )
    totals = lax.fori_loop(0, count, grad_step, start_carry)
    query_terms = totals[0].reshape(block_rows, -1) * HD ** (-0.5)
    return (
        query_terms,
        totals[1].reshape(seq_rows, -1) * HD ** (-0.5),
        totals[2].reshape(seq_rows, -1),
        inner,
    )


def local_general(
    tokens,
    lengths,
    first_gain,
    first_shift,
    w_query,
    w_key,
    w_value,
    bias_query,
    bias_value,
    w_output,
    bias_output,
    second_gain,
    second_shift,
    w_up,
    bias_up,
    w_down,
    bias_down,
    cotangent,
):
    micro_count, own_rows, width = tokens.shape
    col_count = lax.axis_size("col")
    group_rows = own_rows * col_count
    row_place = lax.axis_index("row")
    col_place = lax.axis_index("col")
    head_width = w_query.shape[1]
    hidden_width = w_up.shape[1]
    own_positions = (
        row_place * group_rows + col_place * own_rows + jnp.arange(own_rows, dtype=jnp.int32)
    )
    weight_totals = (
        jnp.zeros((width, head_width), jnp.float32),
        jnp.zeros((width, head_width), jnp.float32),
        jnp.zeros((width, head_width), jnp.float32),
        jnp.zeros((width, hidden_width), jnp.float32),
        jnp.zeros((head_width, width), jnp.float32),
        jnp.zeros((hidden_width, width), jnp.float32),
    )
    vector_totals = (
        jnp.zeros((width,), jnp.float32),
        jnp.zeros((width,), jnp.float32),
        jnp.zeros((head_width,), jnp.float32),
        jnp.zeros((head_width,), jnp.float32),
        jnp.zeros((width,), jnp.float32),
        jnp.zeros((width,), jnp.float32),
        jnp.zeros((width,), jnp.float32),
        jnp.zeros((hidden_width,), jnp.float32),
        jnp.zeros((width,), jnp.float32),
    )
    results = []
    input_grads = []
    for micro_index in range(micro_count):
        gathered = fetch_weights(w_query, w_key, w_value, w_up, w_output, w_down)
        query_full, key_full, value_full, up_full, output_full, down_full = gathered
        length = lengths[0, micro_index]
        inputs = tokens[micro_index].astype(jnp.float32)
        normed = layer_norm(inputs, first_gain, first_shift).astype(jnp.bfloat16)
        normed_all = spread_rows(normed)
        queries = (product(normed_all, query_full) + bias_query).astype(jnp.bfloat16)
        keys_local = product(normed_all, key_full).astype(jnp.bfloat16)
        values_local = (product(normed_all, value_full) + bias_value).astype(jnp.bfloat16)
        keys_all, values_all = (
            lax.all_gather(keys_local, "row", axis=0, tiled=True),
            lax.all_gather(values_local, "row", axis=0, tiled=True),
        )
        attended, maxima, partitions = attention_forward(
            queries, keys_all, values_all, row_place, length
        )
        attended_low = attended.astype(jnp.bfloat16)
        branch = fold_rows(product(attended_low, output_full)) + bias_output
        middle = inputs + branch
        second_normed = layer_norm(middle, second_gain, second_shift).astype(jnp.bfloat16)
        second_all = spread_rows(second_normed)
        pre_activation = product(second_all, up_full) + bias_up
        activated = gelu_tanh(pre_activation).astype(jnp.bfloat16)
        result = middle + (fold_rows(product(activated, down_full)) + bias_down)
        results.append(result.astype(jnp.bfloat16))
        query_full, key_full, value_full, up_full, output_full, down_full = fetch_weights(
            w_query, w_key, w_value, w_up, w_output, w_down
        )
        validity = (own_positions < length).astype(jnp.float32)
        grad_result = cotangent[micro_index].astype(jnp.float32) * validity[:, None]
        grad_result_all = spread_rows(grad_result.astype(jnp.bfloat16))
        grad_down = transposed_left(activated, grad_result_all)
        grad_activated = transposed_right(grad_result_all, down_full)
        gelu_back = jax.vjp(gelu_tanh, pre_activation)[1]
        grad_pre = gelu_back(grad_activated)[0].astype(jnp.bfloat16)
        grad_up = transposed_left(second_all, grad_pre)
        grad_second_normed = fold_rows(transposed_right(grad_pre, up_full))
        second_back = jax.vjp(layer_norm, middle, second_gain, second_shift)[1]
        grad_middle_norm, grad_second_gain, grad_second_shift = second_back(grad_second_normed)
        grad_middle = grad_result + grad_middle_norm
        grad_branch = grad_middle.astype(jnp.bfloat16)
        grad_branch_all = spread_rows(grad_branch)
        grad_output = transposed_left(attended_low, grad_branch_all)
        grad_attended = transposed_right(grad_branch_all, output_full).astype(jnp.bfloat16)
        query_terms, key_terms, value_terms, inner = attention_query_side(
            queries, keys_all, values_all, grad_attended, maxima, partitions, row_place, length
        )
        key_sums, value_sums = (
            lax.psum_scatter(key_terms, "row", scatter_dimension=0, tiled=True),
            lax.psum_scatter(value_terms, "row", scatter_dimension=0, tiled=True),
        )
        grad_queries = query_terms.astype(jnp.bfloat16)
        grad_keys = key_sums.astype(jnp.bfloat16)
        grad_values = value_sums.astype(jnp.bfloat16)
        grad_query = transposed_left(normed_all, grad_queries)
        grad_key = transposed_left(normed_all, grad_keys)
        grad_value = transposed_left(normed_all, grad_values)
        grad_normed = fold_rows(
            transposed_right(grad_queries, query_full)
            + transposed_right(grad_keys, key_full)
            + transposed_right(grad_values, value_full)
        )
        first_back = jax.vjp(layer_norm, inputs, first_gain, first_shift)[1]
        grad_inputs_norm, grad_first_gain, grad_first_shift = first_back(grad_normed)
        input_grads.append((grad_middle + grad_inputs_norm).astype(jnp.bfloat16))
        local_grads = (grad_query, grad_key, grad_value, grad_up, grad_output, grad_down)
        weight_totals = tuple(
            (former + latter for former, latter in zip(weight_totals, local_grads))
        )
        local_vectors = (
            grad_first_gain,
            grad_first_shift,
            jnp.sum(grad_queries.astype(jnp.float32), axis=0),
            jnp.sum(grad_values.astype(jnp.float32), axis=0),
            jnp.sum(grad_branch.astype(jnp.float32), axis=0),
            grad_second_gain,
            grad_second_shift,
            jnp.sum(grad_pre.astype(jnp.float32), axis=0),
            jnp.sum(grad_result, axis=0),
        )
        vector_totals = tuple(
            (former + latter for former, latter in zip(vector_totals, local_vectors))
        )
    weight_totals = reduce_blocks(weight_totals)

    def widen(vector_part):
        blank = jnp.zeros((vector_part.shape[0] * col_count,), jnp.float32)
        return lax.dynamic_update_slice(blank, vector_part, (col_place * vector_part.shape[0],))

    def narrow(whole_vector, piece_width):
        return lax.dynamic_slice_in_dim(whole_vector, col_place * piece_width, piece_width)

    (
        sum_first_gain,
        sum_first_shift,
        sum_bias_query,
        sum_bias_value,
        sum_bias_output,
        sum_second_gain,
        sum_second_shift,
        sum_bias_up,
        sum_bias_down,
    ) = lax.psum(
        (
            vector_totals[0],
            vector_totals[1],
            widen(vector_totals[2]),
            widen(vector_totals[3]),
            vector_totals[4],
            vector_totals[5],
            vector_totals[6],
            widen(vector_totals[7]),
            vector_totals[8],
        ),
        ("dp", "row", "col"),
    )
    grad_w_query, grad_w_key, grad_w_value, grad_w_up, grad_w_output, grad_w_down = weight_totals
    return (
        jnp.stack(results, axis=0),
        jnp.stack(input_grads, axis=0),
        sum_first_gain,
        sum_first_shift,
        grad_w_query,
        grad_w_key,
        grad_w_value,
        narrow(sum_bias_query, head_width),
        narrow(sum_bias_value, head_width),
        grad_w_output,
        sum_bias_output,
        sum_second_gain,
        sum_second_shift,
        grad_w_up,
        narrow(sum_bias_up, hidden_width),
        grad_w_down,
        sum_bias_down,
    )


F32 = jnp.float32
LOW = jnp.bfloat16
VMEM_LIMIT = 56 * 1024 * 1024


def fits(mesh):
    return mesh.shape["row"] == 4 and mesh.shape["col"] == 4 and mesh.shape["dp"] == 2


def contract(former, latter, former_dim, latter_dim):
    return lax.dot_general(
        former,
        latter,
        (((former_dim,), (latter_dim,)), ((), ())),
        preferred_element_type=jnp.float32,
    )


def attention_out_kernel(q_ref, k_ref, v_ref, key_bias_ref, causal_ref, o_ref, lse_ref):
    block = q_ref.shape[0]
    chunks = k_ref.shape[0] // block
    place = pl.program_id(1)
    lane = lax.broadcasted_iota(jnp.int32, q_ref.shape, 1)
    queries = q_ref[...]
    for index in range(chunks):

        @pl.when(place == index)
        def _():
            wide = (index + 1) * block
            parts = []
            for head in range(2):
                mine = (lane // HD) == head
                masked = jnp.where(mine, queries, 0) * jnp.asarray(HD**-0.5, LOW)
                scores = contract(masked, k_ref[:wide], 1, 1) + key_bias_ref[:, :wide]
                last = scores[:, wide - block :] + causal_ref[...]
                scores = last if index == 0 else jnp.concatenate([scores[:, : wide - block], last], axis=1)
                highest = jnp.max(scores, axis=1, keepdims=True)
                weights = jnp.exp(scores - highest)
                total = jnp.sum(weights, axis=1, keepdims=True)
                parts.append(contract(weights.astype(LOW), v_ref[:wide], 1, 0) / total)
                spread = jnp.broadcast_to(highest + jnp.log(total), (block, 128))
                lse_ref[0, 0, head : head + 1, :] = spread.T[:1]
            o_ref[...] = jnp.where(lane < HD, parts[0], parts[1]).astype(LOW)


def attention_out(queries, keys, values, key_bias, causal):
    rows, width = queries.shape
    block = causal.shape[0]
    pairs, chunks = width // 128, rows // block
    row_spec = pl.BlockSpec((block, 128), lambda p, r: (r, p))
    full_spec = pl.BlockSpec((rows, 128), lambda p, r: (0, p))
    return pl.pallas_call(
        attention_out_kernel,
        grid=(pairs, chunks),
        in_specs=[
            row_spec,
            full_spec,
            full_spec,
            pl.BlockSpec((1, rows), lambda p, r: (0, 0)),
            pl.BlockSpec((block, block), lambda p, r: (0, 0)),
        ],
        out_specs=[row_spec, pl.BlockSpec((1, 1, 2, block), lambda p, r: (p, r, 0, 0))],
        out_shape=[
            jax.ShapeDtypeStruct((rows, width), LOW),
            jax.ShapeDtypeStruct((pairs, chunks, 2, block), F32),
        ],
        compiler_params=pltpu.CompilerParams(vmem_limit_bytes=VMEM_LIMIT),
        cost_estimate=pl.CostEstimate(flops=40_000_000_000, bytes_accessed=4_000_000, transcendentals=0),
        name="attention_out",
    )(queries, keys, values, key_bias.reshape(1, rows), causal)


def attention_back_kernel(
    q_ref, k_ref, v_ref, do_ref, o_ref, lse_ref, key_bias_ref, causal_ref, dq_ref, dk_ref, dv_ref, dk_sum, dv_sum
):
    block = q_ref.shape[0]
    chunks = k_ref.shape[0] // block
    place = pl.program_id(1)
    lane = lax.broadcasted_iota(jnp.int32, q_ref.shape, 1)
    queries = q_ref[...]
    grads = do_ref[...]
    inner = (grads.astype(F32) * o_ref[...].astype(F32)).T

    @pl.when(place == 0)
    def _():
        dk_sum[...] = jnp.zeros_like(dk_sum)
        dv_sum[...] = jnp.zeros_like(dv_sum)

    for index in range(chunks):

        @pl.when(place == index)
        def _():
            wide = (index + 1) * block
            parts = []
            for head in range(2):
                mine = (lane // HD) == head
                masked = jnp.where(mine, queries, 0) * jnp.asarray(HD**-0.5, LOW)
                masked_grads = jnp.where(mine, grads, 0)
                inner_row = jnp.sum(inner[head * HD : (head + 1) * HD], axis=0, keepdims=True)
                scores = contract(k_ref[:wide], masked, 1, 1) + key_bias_ref[:wide]
                last = scores[wide - block :] + causal_ref[...]
                scores = last if index == 0 else jnp.concatenate([scores[: wide - block], last], axis=0)
                weights = jnp.exp(scores - lse_ref[0, 0, head : head + 1, :])
                grad_weights = contract(v_ref[:wide], masked_grads, 1, 1)
                grad_scores = (weights * (grad_weights - inner_row)).astype(LOW)
                dv_sum[:wide] += contract(weights.astype(LOW), masked_grads, 1, 0)
                dk_sum[:wide] += contract(grad_scores, masked, 1, 0)
                parts.append(contract(grad_scores, k_ref[:wide], 0, 0))
            dq_ref[...] = (jnp.where(lane < HD, parts[0], parts[1]) * HD**-0.5).astype(LOW)

    @pl.when(place == chunks - 1)
    def _():
        dk_ref[...] = dk_sum[...].astype(LOW)
        dv_ref[...] = dv_sum[...].astype(LOW)


def attention_back(queries, keys, values, grads, attended, lse, key_bias, causal):
    rows, width = queries.shape
    block = causal.shape[0]
    pairs, chunks = width // 128, rows // block
    row_spec = pl.BlockSpec((block, 128), lambda p, r: (r, p))
    full_spec = pl.BlockSpec((rows, 128), lambda p, r: (0, p))
    return pl.pallas_call(
        attention_back_kernel,
        grid=(pairs, chunks),
        in_specs=[
            row_spec,
            full_spec,
            full_spec,
            row_spec,
            row_spec,
            pl.BlockSpec((1, 1, 2, block), lambda p, r: (p, r, 0, 0)),
            pl.BlockSpec((rows, 1), lambda p, r: (0, 0)),
            pl.BlockSpec((block, block), lambda p, r: (0, 0)),
        ],
        out_specs=[row_spec, full_spec, full_spec],
        out_shape=[jax.ShapeDtypeStruct((rows, width), LOW)] * 3,
        scratch_shapes=[pltpu.VMEM((rows, 128), F32)] * 2,
        compiler_params=pltpu.CompilerParams(vmem_limit_bytes=VMEM_LIMIT),
        cost_estimate=pl.CostEstimate(flops=80_000_000_000, bytes_accessed=6_000_000, transcendentals=0),
        name="attention_back",
    )(queries, keys, values, grads, attended, lse, key_bias.reshape(rows, 1), causal.T)


def swap(array, axis, flip):
    size = lax.axis_size(axis)
    return lax.ppermute(array, axis, [(place, place ^ flip) for place in range(size)])


def gather_parts(own):
    core = swap(own, "col", 1)
    far = swap(own, "col", 2)
    return own, core, far, swap(far, "col", 1)


def gather_rows(own):
    return jnp.stack(gather_parts(own), axis=1)


def scatter_rows(partial_sum):
    arrived = swap(partial_sum[:, 1::2], "col", 1)
    kept = partial_sum[:, 0::2] + arrived
    return kept[:, 0] + swap(kept[:, 1].astype(LOW), "col", 2).astype(F32)


def trade_rows(array):
    return lax.all_to_all(array, "row", split_axis=0, concat_axis=0)


def scatter_blocks(gradient, dim):
    dp_place = lax.axis_index("dp")
    row_place = lax.axis_index("row")
    total = gradient.astype(F32)
    for axis, flip, place in (("dp", 1, dp_place), ("row", 2, row_place // 2), ("row", 1, row_place % 2)):
        half = total.shape[dim] // 2
        mine = lax.dynamic_slice_in_dim(total, place * half, half, dim)
        other = lax.dynamic_slice_in_dim(total, (1 - place) * half, half, dim)
        total = mine + swap(other.astype(LOW), axis, flip).astype(F32)
    return total


def norm_parts(values):
    centered = values - jnp.mean(values, axis=-1, keepdims=True)
    scale = lax.rsqrt(jnp.mean(centered * centered, axis=-1, keepdims=True) + EPSILON)
    return centered * scale, scale


def norm_back(grads, gain, unit, scale):
    inner = grads * gain
    mean_inner = jnp.mean(inner, axis=-1, keepdims=True)
    mean_unit = jnp.mean(inner * unit, axis=-1, keepdims=True)
    return scale * (inner - mean_inner - unit * mean_unit)


GELU_SCALE = 0.7978845608028654
GELU_CUBE = 0.044715


def gelu_parts(values):
    square = values * values
    curve = jnp.tanh(GELU_SCALE * values * (1.0 + GELU_CUBE * square))
    half = 0.5 + 0.5 * curve
    slope = half + 0.5 * values * (1.0 - curve * curve) * (GELU_SCALE * (1.0 + 3.0 * GELU_CUBE * square))
    return values * half, slope


def peers():
    place = lax.axis_index("col")
    return {"col": place + 1 - 2 * (place % 2)}, {"col": (place + 2) % 4}


def greet(devices):
    barrier = pltpu.get_barrier_semaphore()
    for device in devices:
        pl.semaphore_signal(barrier, inc=1, device_id=device, device_id_type=pl.DeviceIdType.MESH)
    pl.semaphore_wait(barrier, len(devices))


def remote(source, target, send_sem, recv_sem, device):
    return pltpu.make_async_remote_copy(
        src_ref=source,
        dst_ref=target,
        send_sem=send_sem,
        recv_sem=recv_sem,
        device_id=device,
        device_id_type=pl.DeviceIdType.MESH,
    )


def feed_kernel(
    att_ref,
    wo_ref,
    wu_ref,
    wd_ref,
    tok_ref,
    g0_ref,
    g1_ref,
    g2_ref,
    g3_ref,
    vec_ref,
    bias_up_ref,
    result_ref,
    gatt_ref,
    gmid_ref,
    gout_ref,
    gup_ref,
    gdown_ref,
    sums_ref,
    sum_up_ref,
    g_all,
    kept,
    kept_q,
    core_out,
    core_in,
    core_in_q,
    far_out,
    far_in,
    far_out_q,
    far_in_q,
    middle,
    second,
    act,
    gpre,
    branch,
    stage,
    local_sems,
    stage_sems,
    send_sems,
    recv_sems,
):
    chunks, blocks, own, width = second.shape
    rows = blocks * own
    hidden = wu_ref.shape[1]
    core, far = peers()

    for j, source in enumerate((g0_ref, g1_ref, g2_ref, g3_ref)):
        pltpu.make_async_copy(source, g_all.at[:, j], local_sems.at[j]).start()

    def core_copy(step, r, source, target):
        return remote(source.at[r], target.at[r], send_sems.at[step, r], recv_sems.at[step, r], core)

    def far_copy(step, r, source, target):
        return remote(source.at[r], target.at[r], send_sems.at[step, r], recv_sems.at[step, r], far)

    def spread_core(step, r, rows_ref):
        return remote(rows_ref.at[r, 0], rows_ref.at[r, 1], send_sems.at[step, r], recv_sems.at[step, r], core)

    def spread_far(step, r, rows_ref):
        return remote(rows_ref.at[r, 0], rows_ref.at[r, 2], send_sems.at[step, r], recv_sems.at[step, r], far)

    def spread_relay(step, r, rows_ref):
        return remote(rows_ref.at[r, 2], rows_ref.at[r, 3], send_sems.at[step, r], recv_sems.at[step, r], core)

    def split(r, total, kept_ref, out_ref):
        kept_ref[r, 0] = total[:own].astype(kept_ref.dtype)
        out_ref[r, 0] = total[own : 2 * own].astype(LOW)
        kept_ref[r, 1] = total[2 * own : 3 * own].astype(kept_ref.dtype)
        out_ref[r, 1] = total[3 * own :].astype(LOW)

    def fold(r, kept_ref, in_ref, out_ref):
        out_ref[r] = (kept_ref[r, 1].astype(F32) + in_ref[r, 1].astype(F32)).astype(LOW)
        kept_ref[r, 0] = (kept_ref[r, 0].astype(F32) + in_ref[r, 0].astype(F32)).astype(kept_ref.dtype)

    def each(body):
        lax.fori_loop(0, chunks, lambda r, carry: (body(r), carry)[1], 0)

    greet((core, far))

    def out_projection(r):
        rows_here = pl.ds(pl.multiple_of(r * rows, rows), rows)
        split(r, contract(att_ref[rows_here], wo_ref[...], 1, 0), kept, core_out)
        core_copy(0, r, core_out, core_in).start()

    each(out_projection)

    def out_fold(r):
        core_copy(0, r, core_out, core_in).wait()
        fold(r, kept, core_in, far_out)
        far_copy(1, r, far_out, far_in).start()

    each(out_fold)

    def norm(r):
        far_copy(1, r, far_out, far_in).wait()
        values = tok_ref[r].astype(F32) + (kept[r, 0] + far_in[r].astype(F32) + vec_ref[0:1])
        middle[r] = values
        second[r, 0] = (norm_parts(values)[0] * vec_ref[1:2] + vec_ref[2:3]).astype(LOW)
        spread_core(2, r, second).start()
        spread_far(3, r, second).start()

    each(norm)
    for j, source in enumerate((g0_ref, g1_ref, g2_ref, g3_ref)):
        pltpu.make_async_copy(source, g_all.at[:, j], local_sems.at[j]).wait()

    sum_up_ref[...] = jnp.zeros_like(sum_up_ref)

    def feed(r):
        spread_far(3, r, second).wait()
        spread_relay(4, r, second).start()
        spread_core(2, r, second).wait()
        spread_relay(4, r, second).wait()
        pre = contract(second[r].reshape(rows, width), wu_ref[...], 1, 0) + bias_up_ref[...]
        activated, slope = gelu_parts(pre)
        act[r] = activated.astype(LOW).reshape(blocks, own, hidden)
        grads = contract(g_all[r].reshape(rows, width), wd_ref[...], 1, 1) * slope
        grads_low = grads.astype(LOW)
        gpre[r] = grads_low.reshape(blocks, own, hidden)
        sum_up_ref[...] += jnp.sum(grads_low.astype(F32), axis=0, keepdims=True)
        split(r, contract(grads_low, wu_ref[...], 1, 1), kept, core_out)
        core_copy(5, r, core_out, core_in).start()
        core_copy(5, r, core_out, core_in).wait()
        fold(r, kept, core_in, far_out)
        far_copy(6, r, far_out, far_in).start()
        split(r, contract(act[r].reshape(rows, hidden), wd_ref[...], 1, 0), kept_q, core_out)
        core_copy(7, r, core_out, core_in_q).start()

    each(feed)
    sums_ref[...] = jnp.zeros_like(sums_ref)

    def norm_grad(r):
        far_copy(6, r, far_out, far_in).wait()
        grads = kept[r, 0] + far_in[r].astype(F32)
        unit, scale = norm_parts(middle[r])
        place = g_all[r, 0].astype(F32)
        total = place + norm_back(grads, vec_ref[1:2], unit, scale)
        gmid_ref[r] = total
        low = total.astype(LOW)
        branch[r, 0] = low
        spread_core(9, r, branch).start()
        spread_far(10, r, branch).start()
        sums_ref[0:1] += jnp.sum(low.astype(F32), axis=0, keepdims=True)
        sums_ref[1:2] += jnp.sum(grads * unit, axis=0, keepdims=True)
        sums_ref[2:3] += jnp.sum(grads, axis=0, keepdims=True)
        sums_ref[3:4] += jnp.sum(place, axis=0, keepdims=True)

    each(norm_grad)

    def result_fold(r):
        core_copy(7, r, core_out, core_in_q).wait()
        fold(r, kept_q, core_in_q, far_out_q)
        far_copy(8, r, far_out_q, far_in_q).start()

    each(result_fold)

    wide = 256
    flat_second = second.reshape(chunks * rows, width)
    flat_act = act.reshape(chunks * rows, hidden)
    flat_gpre = gpre.reshape(chunks * rows, hidden)
    flat_g = g_all.reshape(chunks * rows, width)
    flat_branch = branch.reshape(chunks * rows, width)

    def down_grad(t):
        part = pl.ds(pl.multiple_of(t * wide, wide), wide)
        total = contract(flat_act[:, part], flat_g[...], 0, 0).astype(LOW)
        for b in range(8):
            stage[b] = total[:, b * own : (b + 1) * own]
        copy = pltpu.make_async_copy(stage, gdown_ref.at[:, part], stage_sems.at[0])
        copy.start()
        copy.wait()

    lax.fori_loop(0, hidden // wide, lambda t, c: (down_grad(t), c)[1], 0)

    def attended_grad(r):
        spread_far(10, r, branch).wait()
        spread_relay(11, r, branch).start()
        spread_core(9, r, branch).wait()
        spread_relay(11, r, branch).wait()
        rows_here = pl.ds(pl.multiple_of(r * rows, rows), rows)
        gatt_ref[rows_here] = contract(branch[r].reshape(rows, width), wo_ref[...], 1, 1).astype(LOW)

    each(attended_grad)

    def up_grad(t):
        part = pl.ds(pl.multiple_of(t * wide, wide), wide)
        total = contract(flat_second[:, part], flat_gpre[...], 0, 0).astype(LOW)
        for b in range(2):
            gup_ref[2 * t + b] = total[b * own : (b + 1) * own]

    lax.fori_loop(0, width // wide, lambda t, c: (up_grad(t), c)[1], 0)
    total_out = contract(att_ref[...], flat_branch[...], 0, 0).astype(LOW)
    for b in range(8):
        gout_ref[b] = total_out[:, b * own : (b + 1) * own]

    def finish(r):
        far_copy(8, r, far_out_q, far_in_q).wait()
        total = kept_q[r, 0].astype(F32) + far_in_q[r].astype(F32)
        result_ref[r] = (middle[r] + (total + vec_ref[3:4])).astype(LOW)

    each(finish)


def feed_block(attended, w_output, w_up, w_down, own_tokens, grads, vectors, bias_up):
    chunks, own, width = own_tokens.shape
    rows = chunks * 4 * own
    head_width = w_output.shape[0]
    hidden = w_up.shape[1]
    half = (chunks, 2, own, width)
    one = (chunks, own, width)
    all_rows = (chunks, 4, own, width)
    vmem = pl.BlockSpec(memory_space=pltpu.VMEM)
    hbm = pl.BlockSpec(memory_space=pl.ANY)
    return pl.pallas_call(
        feed_kernel,
        in_specs=[vmem] * 5 + [hbm] * 4 + [vmem] * 2,
        out_specs=[vmem] * 5 + [hbm] + [vmem] * 2,
        out_shape=[
            jax.ShapeDtypeStruct(one, LOW),
            jax.ShapeDtypeStruct((rows, head_width), LOW),
            jax.ShapeDtypeStruct(one, F32),
            jax.ShapeDtypeStruct((8, head_width, width // 8), LOW),
            jax.ShapeDtypeStruct((8, width // 8, hidden), LOW),
            jax.ShapeDtypeStruct((8, hidden, width // 8), LOW),
            jax.ShapeDtypeStruct((8, width), F32),
            jax.ShapeDtypeStruct((1, hidden), F32),
        ],
        scratch_shapes=[
            pltpu.VMEM(all_rows, LOW),
            pltpu.VMEM(half, F32),
            pltpu.VMEM(half, LOW),
            pltpu.VMEM(half, LOW),
            pltpu.VMEM(half, LOW),
            pltpu.VMEM(half, LOW),
            pltpu.VMEM(one, LOW),
            pltpu.VMEM(one, LOW),
            pltpu.VMEM(one, LOW),
            pltpu.VMEM(one, LOW),
            pltpu.VMEM(one, F32),
            pltpu.VMEM(all_rows, LOW),
            pltpu.VMEM((chunks, 4, own, hidden), LOW),
            pltpu.VMEM((chunks, 4, own, hidden), LOW),
            pltpu.VMEM(all_rows, LOW),
            pltpu.VMEM((8, 256, width // 8), LOW),
            pltpu.SemaphoreType.DMA((4,)),
            pltpu.SemaphoreType.DMA((2,)),
            pltpu.SemaphoreType.DMA((12, chunks)),
            pltpu.SemaphoreType.DMA((12, chunks)),
        ],
        compiler_params=pltpu.CompilerParams(
            collective_id=1, has_side_effects=True, vmem_limit_bytes=61 * 1024 * 1024
        ),
        cost_estimate=pl.CostEstimate(flops=100_000_000_000, bytes_accessed=30_000_000, transcendentals=0),
        name="feed_block",
    )(attended, w_output, w_up, w_down, own_tokens, *grads, vectors, bias_up)


def back_kernel(
    q_ref,
    k_ref,
    v_ref,
    do_ref,
    o_ref,
    lse_ref,
    key_bias_ref,
    causal_ref,
    w_ref,
    tok_ref,
    gmid_ref,
    res_ref,
    gdown_ref,
    gup_ref,
    gout_ref,
    gain_ref,
    sums_ref,
    sum_up_ref,
    normed_ref,
    res_out,
    gtok_out,
    down_out,
    up_out,
    out_out,
    proj_out,
    shared_out,
    by_col_out,
    dk_sum,
    dv_sum,
    dproj,
    gproj,
    kept,
    core_out,
    core_in,
    far_out,
    far_in,
    gtok,
    norm_tile,
    x_down,
    x_up,
    x_out,
    x_proj,
    z_down,
    z_up,
    z_out,
    z_proj,
    vec,
    vec_in,
    res_send,
    res_recv,
    tok_send,
    tok_recv,
    fold_send,
    fold_recv,
    x_send,
    x_recv,
    z_send,
    z_recv,
    vec_send,
    vec_recv,
    tile_sem,
):
    chunks, own, width = tok_ref.shape
    rows = 4 * own
    head_width = q_ref.shape[1]
    core, far = peers()
    row = lax.axis_index("row")
    dp = lax.axis_index("dp")
    cross = {"dp": 1 - dp}
    other = lambda r: {"row": r}
    sets = (
        (gdown_ref, x_down, z_down, down_out),
        (gup_ref, x_up, z_up, up_out),
        (gout_ref, x_out, z_out, out_out),
        (gproj, x_proj, z_proj, proj_out),
    )

    barrier = pltpu.get_barrier_semaphore()
    for device in (core, far, cross, other((row + 1) % 4), other((row + 2) % 4), other((row + 3) % 4)):
        pl.semaphore_signal(barrier, inc=1, device_id=device, device_id_type=pl.DeviceIdType.MESH)
    pl.semaphore_wait(barrier, 6)

    def trade(r, source, target, send, recv):
        return remote(source.at[r], target.at[row], send.at[r], recv.at[row], other(r))

    def trade_start(r, source, target, send, recv):
        @pl.when(row != r)
        def _():
            trade(r, source, target, send, recv).start()

        @pl.when(row == r)
        def _():
            target[r] = source[r]

    def trade_wait(source, target, send, recv):
        for r in range(4):

            @pl.when(row != r)
            def _():
                trade(r, source, target, send, recv).wait_send()
                remote(source.at[r], target.at[r], send.at[r], recv.at[r], other(r)).wait_recv()

    def x_copy(i):
        grads, arrived, _, _ = sets[i]
        return remote(grads.at[pl.ds((1 - dp) * 4, 4)], arrived, x_send.at[i], x_recv.at[i], cross)

    def x_add(i):
        grads, arrived, _, _ = sets[i]
        x_copy(i).wait()
        for b in range(4):
            arrived[b] = (arrived[b].astype(F32) + grads[dp * 4 + b].astype(F32)).astype(LOW)

    def lanes(d):
        place = row if d == 0 else 3 - row
        following = {"row": jnp.minimum(row + 1, 3)} if d == 0 else {"row": jnp.maximum(row - 1, 0)}
        return place, following

    def z_first(i, d, k):
        _, sums, moving, _ = sets[i]
        place, following = lanes(d)
        block = 3 - k if d == 0 else k
        return remote(sums.at[block], moving.at[d, k], z_send.at[i, d, k], z_recv.at[i, d, k], following)

    def z_next(i, d, k):
        _, sums, moving, _ = sets[i]
        place, following = lanes(d)
        return remote(moving.at[d, k - 1], moving.at[d, k], z_send.at[i, d, k], z_recv.at[i, d, k], following)

    def z_pump(i, k):
        _, sums, moving, _ = sets[i]
        for d in range(2):
            place, following = lanes(d)

            @pl.when(place == 0)
            def _():
                z_first(i, d, k).start()

            if k >= 1:

                @pl.when((place >= 1) & (place <= k))
                def _():
                    block = 3 - k + place if d == 0 else k - place
                    z_first(i, d, k - 1).wait_recv()
                    moving[d, k - 1] = (moving[d, k - 1].astype(F32) + sums[block].astype(F32)).astype(LOW)
                    z_next(i, d, k).start()

    def z_finish(i):
        _, sums, moving, out = sets[i]
        out[...] = sums[row].astype(F32)
        for d in range(2):
            place, following = lanes(d)

            @pl.when(place >= 1)
            def _():
                z_first(i, d, 2).wait_recv()
                out[...] += moving[d, 2].astype(F32)

        for d in range(2):
            place, following = lanes(d)
            for k in range(3):

                @pl.when(place <= k)
                def _():
                    z_first(i, d, k).wait_send()

    for i in range(3):
        x_copy(i).start()
    for r in range(4):
        trade_start(r, res_ref, res_out, res_send, res_recv)

    block = 256
    lane = lax.broadcasted_iota(jnp.int32, (block, 128), 1)

    def attention(r):
        wide = (r + 1) * rows

        def part(step, carry):
            here = pl.ds(pl.multiple_of(r * rows + (step % 2) * block, block), block)
            pair = pl.ds(pl.multiple_of((step // 2) * 128, 128), 128)
            inside = pl.ds(pl.multiple_of((step % 2) * block, block), block)
            queries = q_ref[here, pair]
            grads = do_ref[here, pair]
            inner = (grads.astype(F32) * o_ref[here, pair].astype(F32)).T
            parts = []
            for head in range(2):
                mine = (lane // HD) == head
                masked = jnp.where(mine, queries, 0) * jnp.asarray(HD**-0.5, LOW)
                masked_grads = jnp.where(mine, grads, 0)
                inner_row = jnp.sum(inner[head * HD : (head + 1) * HD], axis=0, keepdims=True)
                scores = contract(k_ref[:wide, pair], masked, 1, 1) + key_bias_ref[:wide]
                last = scores[wide - rows :] + causal_ref[:, inside]
                scores = last if r == 0 else jnp.concatenate([scores[: wide - rows], last], axis=0)
                weights = jnp.exp(scores - lse_ref[step // 2, r, head : head + 1, inside])
                grad_weights = contract(v_ref[:wide, pair], masked_grads, 1, 1)
                grad_scores = (weights * (grad_weights - inner_row)).astype(LOW)
                dv_sum[:wide, pair] += contract(weights.astype(LOW), masked_grads, 1, 0)
                dk_sum[:wide, pair] += contract(grad_scores, masked, 1, 0)
                parts.append(contract(grad_scores, k_ref[:wide, pair], 0, 0))
            dproj[here, pair] = (jnp.where(lane < HD, parts[0], parts[1]) * HD**-0.5).astype(LOW)
            return carry

        lax.fori_loop(0, 4, part, 0)
        end = slice(wide - rows, wide)
        dproj[end, head_width : 2 * head_width] = dk_sum[end].astype(LOW)
        dproj[end, 2 * head_width :] = dv_sum[end].astype(LOW)

    def core_copy(r):
        return remote(core_out.at[r], core_in.at[r], fold_send.at[0, r], fold_recv.at[0, r], core)

    def far_copy(r):
        return remote(far_out.at[r], far_in.at[r], fold_send.at[1, r], fold_recv.at[1, r], far)

    def project(r):
        total = contract(dproj[r * rows : (r + 1) * rows], w_ref[...], 1, 1)
        kept[r, 0] = total[:own]
        core_out[r, 0] = total[own : 2 * own].astype(LOW)
        kept[r, 1] = total[2 * own : 3 * own]
        core_out[r, 1] = total[3 * own :].astype(LOW)
        core_copy(r).start()

    def fold(r):
        core_copy(r).wait()
        far_out[r] = (kept[r, 1] + core_in[r, 1].astype(F32)).astype(LOW)
        kept[r, 0] = kept[r, 0] + core_in[r, 0].astype(F32)
        far_copy(r).start()

    vec[...] = jnp.zeros_like(vec)

    def norm_grad(r):
        far_copy(r).wait()
        grads = kept[r, 0] + far_in[r].astype(F32)
        unit, scale = norm_parts(tok_ref[r].astype(F32))
        gtok[r] = (gmid_ref[r] + norm_back(grads, gain_ref[...], unit, scale)).astype(LOW)
        trade_start(r, gtok, gtok_out, tok_send, tok_recv)
        vec[0:1] += jnp.sum(grads * unit, axis=0, keepdims=True)
        vec[1:2] += jnp.sum(grads, axis=0, keepdims=True)

    def tile_copy(t):
        part = slice(t * 256, (t + 1) * 256)
        return pltpu.make_async_copy(normed_ref.at[:, part], norm_tile.at[t % 2], tile_sem.at[t % 2])

    dk_sum[...] = jnp.zeros_like(dk_sum)
    dv_sum[...] = jnp.zeros_like(dv_sum)
    tile_copy(0).start()
    tile_copy(1).start()
    attention(3)
    project(3)
    fold(3)
    attention(2)
    project(2)
    fold(2)
    x_add(0)
    z_pump(0, 0)
    attention(1)
    project(1)
    fold(1)
    norm_grad(3)
    z_pump(0, 1)
    attention(0)
    project(0)
    fold(0)
    for t in range(width // 256):
        tile_copy(t).wait()
        total = contract(norm_tile[t % 2], dproj[...], 0, 0).astype(LOW)
        gproj[2 * t] = total[:own]
        gproj[2 * t + 1] = total[own:]
        if t + 2 < width // 256:
            tile_copy(t + 2).start()
    x_copy(3).start()
    norm_grad(2)
    z_pump(0, 2)
    x_add(1)
    z_pump(1, 0)
    norm_grad(1)
    z_pump(1, 1)
    norm_grad(0)
    x_add(2)
    z_pump(2, 0)
    z_pump(1, 2)
    x_add(3)
    z_pump(3, 0)
    z_pump(2, 1)
    z_pump(3, 1)
    z_pump(2, 2)
    z_pump(3, 2)

    vec[2:6] = sums_ref[0:4]
    vec[8:9] = sum_up_ref[...]
    low_sum = jnp.sum(dproj[:, :head_width].astype(F32), axis=0, keepdims=True)
    value_sum = jnp.sum(dproj[:, 2 * head_width :].astype(F32), axis=0, keepdims=True)
    vec[9:10, :head_width] = low_sum
    vec[9:10, head_width : 2 * head_width] = value_sum
    steps = (cross, other(row + 1 - 2 * (row % 2)), other((row + 2) % 4), core, far)
    for step, device in enumerate(steps):
        size = 16 if step < 3 else 8
        copy = remote(vec.at[:size], vec_in.at[step, :size], vec_send.at[step], vec_recv.at[step], device)
        copy.start()
        copy.wait()
        vec[:size] = vec[:size] + vec_in[step, :size]
    shared_out[...] = vec[:8]
    by_col_out[...] = vec[8:]

    for i in range(4):
        z_finish(i)
    trade_wait(res_ref, res_out, res_send, res_recv)
    trade_wait(gtok, gtok_out, tok_send, tok_recv)


def back_block(
    queries, keys, values, grads, attended, lse, key_bias, causal, w_proj, tokens, gmid, result, gdown, gup, gout, gain, sums, sum_up, normed
):
    chunks, own, width = tokens.shape
    rows, head_width = queries.shape
    half = (chunks, 2, own, width)
    one = (chunks, own, width)
    blocks = ((gdown.shape[1], gdown.shape[2]), (gup.shape[1], gup.shape[2]), (gout.shape[1], gout.shape[2]), (own, 3 * head_width))
    vmem = pl.BlockSpec(memory_space=pltpu.VMEM)
    hbm = pl.BlockSpec(memory_space=pl.ANY)
    dma = pltpu.SemaphoreType.DMA
    return pl.pallas_call(
        back_kernel,
        in_specs=[vmem] * 18 + [hbm],
        out_specs=[vmem] * 8,
        out_shape=[jax.ShapeDtypeStruct(one, LOW), jax.ShapeDtypeStruct(one, LOW)]
        + [jax.ShapeDtypeStruct(shape, F32) for shape in blocks]
        + [jax.ShapeDtypeStruct((8, width), F32)] * 2,
        scratch_shapes=[
            pltpu.VMEM((rows, head_width), F32),
            pltpu.VMEM((rows, head_width), F32),
            pltpu.VMEM((rows, 3 * head_width), LOW),
            pltpu.VMEM((8, own, 3 * head_width), LOW),
            pltpu.VMEM(half, F32),
            pltpu.VMEM(half, LOW),
            pltpu.VMEM(half, LOW),
            pltpu.VMEM(one, LOW),
            pltpu.VMEM(one, LOW),
            pltpu.VMEM(one, LOW),
            pltpu.VMEM((2, rows, 256), LOW),
        ]
        + [pltpu.VMEM((4,) + shape, LOW) for shape in blocks]
        + [pltpu.VMEM((2, 3) + shape, LOW) for shape in blocks]
        + [
            pltpu.VMEM((16, width), F32),
            pltpu.VMEM((5, 16, width), F32),
            dma((4,)),
            dma((4,)),
            dma((4,)),
            dma((4,)),
            dma((2, 4)),
            dma((2, 4)),
            dma((4,)),
            dma((4,)),
            dma((4, 2, 3)),
            dma((4, 2, 3)),
            dma((5,)),
            dma((5,)),
            dma((2,)),
        ],
        compiler_params=pltpu.CompilerParams(
            collective_id=2, has_side_effects=True, vmem_limit_bytes=61 * 1024 * 1024
        ),
        cost_estimate=pl.CostEstimate(flops=100_000_000_000, bytes_accessed=30_000_000, transcendentals=0),
        name="back_block",
    )(
        queries, keys, values, grads, attended, lse, key_bias, causal, w_proj, tokens, gmid, result, gdown, gup, gout, gain, sums, sum_up, normed
    )


def local_sequence(
    tokens,
    lengths,
    first_gain,
    first_shift,
    w_query,
    w_key,
    w_value,
    bias_query,
    bias_value,
    w_output,
    bias_output,
    second_gain,
    second_shift,
    w_up,
    bias_up,
    w_down,
    bias_down,
    cotangent,
):
    micro_count, own_rows, width = tokens.shape
    col_count = lax.axis_size("col")
    row_place = lax.axis_index("row")
    col_place = lax.axis_index("col")
    chunk = own_rows * col_count
    seq_rows = chunk * micro_count
    head_width = w_query.shape[1]
    hidden_width = w_up.shape[1]
    length = lax.dynamic_slice_in_dim(lengths[0], row_place, 1)[0]

    inside = (col_place ^ jnp.arange(col_count, dtype=jnp.int32))[:, None] * own_rows + jnp.arange(
        own_rows, dtype=jnp.int32
    )
    inside = inside.reshape(-1)
    positions = (jnp.arange(micro_count, dtype=jnp.int32)[:, None] * chunk + inside).reshape(-1)
    key_bias = jnp.where(positions < length, 0.0, MASKED).astype(F32)
    causal = jnp.where(inside[None, :] <= inside[:, None], 0.0, MASKED).astype(F32)
    own_positions = positions.reshape(micro_count, col_count, own_rows)[:, 0]
    validity = (own_positions < length).astype(F32)[:, :, None]

    query_key_value = lax.all_gather(
        jnp.concatenate([w_query, w_key, w_value], axis=1), ("dp", "row"), axis=0, tiled=True
    )
    trailing = lax.all_gather(jnp.concatenate([w_output, w_down], axis=0), ("dp", "row"), axis=1, tiled=True)
    output_full, down_full = trailing[:head_width], trailing[head_width:]
    up_full = lax.all_gather(w_up, ("dp", "row"), axis=0, tiled=True)

    inputs_low = trade_rows(tokens)
    inputs = inputs_low.astype(F32)
    grad_result = trade_rows(cotangent).astype(F32) * validity
    tokens_all = gather_rows(inputs_low).reshape(seq_rows, width).astype(F32)
    grad_all = gather_parts(grad_result.astype(LOW))

    normed_all = (norm_parts(tokens_all)[0] * first_gain + first_shift).astype(LOW)
    projected = product(normed_all, query_key_value)
    queries = (projected[:, :head_width] + bias_query).astype(LOW)
    keys = projected[:, head_width : 2 * head_width].astype(LOW)
    values = (projected[:, 2 * head_width :] + bias_value).astype(LOW)
    attended, lse = attention_out(queries, keys, values, key_bias, causal)

    def split_rows(array):
        return array.reshape(micro_count, col_count, own_rows, -1)

    vectors = jnp.concatenate(
        [jnp.stack([bias_output, second_gain, second_shift, bias_down]), jnp.zeros((4, width), F32)]
    )
    result, grad_attended, grad_middle, grad_output, grad_up, grad_down, sums, sum_up = feed_block(
        attended, output_full, up_full, down_full, inputs_low, grad_all, vectors, bias_up.reshape(1, -1)
    )
    result, grad_tokens, grad_down, grad_up, grad_output, grad_w, shared, by_col = back_block(
        queries,
        keys,
        values,
        grad_attended,
        attended,
        lse,
        key_bias.reshape(seq_rows, 1),
        causal.T,
        query_key_value,
        inputs_low,
        grad_middle,
        result,
        grad_down,
        grad_up,
        grad_output,
        first_gain.reshape(1, width),
        sums,
        sum_up,
        normed_all,
    )
    return (
        result,
        grad_tokens,
        shared[0],
        shared[1],
        grad_w[:, :head_width],
        grad_w[:, head_width : 2 * head_width],
        grad_w[:, 2 * head_width :],
        by_col[1, :head_width],
        by_col[1, head_width : 2 * head_width],
        grad_output,
        shared[2],
        shared[3],
        shared[4],
        grad_up,
        by_col[0],
        grad_down,
        shared[5],
    )


def solution(mesh):
    return jax.shard_map(
        local_sequence if fits(mesh) else local_general,
        mesh=mesh,
        in_specs=(
            P(None, ("dp", "row", "col"), None),
            P("dp", None),
            P(),
            P(),
            P(("dp", "row"), "col"),
            P(("dp", "row"), "col"),
            P(("dp", "row"), "col"),
            P("col"),
            P("col"),
            P("col", ("dp", "row")),
            P(),
            P(),
            P(),
            P(("dp", "row"), "col"),
            P("col"),
            P("col", ("dp", "row")),
            P(),
            P(None, ("dp", "row", "col"), None),
        ),
        out_specs=(
            P(None, ("dp", "row", "col"), None),
            P(None, ("dp", "row", "col"), None),
            P(),
            P(),
            P(("dp", "row"), "col"),
            P(("dp", "row"), "col"),
            P(("dp", "row"), "col"),
            P("col"),
            P("col"),
            P("col", ("dp", "row")),
            P(),
            P(),
            P(),
            P(("dp", "row"), "col"),
            P("col"),
            P("col", ("dp", "row")),
            P(),
        ),
        check_vma=False,
    )
```

```python
import functools

import jax
import jax.numpy as jnp
from jax import lax
from jax.experimental import pallas as pl
from jax.experimental.pallas import tpu as pltpu
from jax.sharding import PartitionSpec as P

HD = 64


EPSILON = 1e-05
MASKED = -1e30


def layer_norm(values, norm_gain, norm_shift):
    centered = values - jnp.mean(values, axis=-1, keepdims=True)
    variance = jnp.mean(centered * centered, axis=-1, keepdims=True)
    return centered * lax.rsqrt(variance + EPSILON) * norm_gain + norm_shift


def gelu_tanh(values):
    return jax.nn.gelu(values, approximate=True)


def product(former, latter):
    return jnp.dot(former, latter, preferred_element_type=jnp.float32)


def transposed_left(former, latter):
    return lax.dot_general(
        former, latter, (((0,), (0,)), ((), ())), preferred_element_type=jnp.float32
    )


def transposed_right(former, latter):
    return lax.dot_general(
        former, latter, (((1,), (1,)), ((), ())), preferred_element_type=jnp.float32
    )


def spread_rows(rows_block):
    return lax.all_gather(rows_block, "col", axis=0, tiled=True)


def fold_rows(partial_sum):
    return lax.psum_scatter(partial_sum, "col", scatter_dimension=0, tiled=True)


def fetch_weights(w_query, w_key, w_value, w_up, w_output, w_down):
    leading = (
        lax.all_gather(w_query, ("dp", "row"), axis=0, tiled=True),
        lax.all_gather(w_key, ("dp", "row"), axis=0, tiled=True),
        lax.all_gather(w_value, ("dp", "row"), axis=0, tiled=True),
        lax.all_gather(w_up, ("dp", "row"), axis=0, tiled=True),
    )
    trailing = (
        lax.all_gather(w_output, ("dp", "row"), axis=1, tiled=True),
        lax.all_gather(w_down, ("dp", "row"), axis=1, tiled=True),
    )
    return tuple(leading) + tuple(trailing)


def reduce_blocks(gradients):
    leading = (
        lax.psum_scatter(gradients[0], ("dp", "row"), scatter_dimension=0, tiled=True),
        lax.psum_scatter(gradients[1], ("dp", "row"), scatter_dimension=0, tiled=True),
        lax.psum_scatter(gradients[2], ("dp", "row"), scatter_dimension=0, tiled=True),
        lax.psum_scatter(gradients[3], ("dp", "row"), scatter_dimension=0, tiled=True),
    )
    trailing = (
        lax.psum_scatter(gradients[4], ("dp", "row"), scatter_dimension=1, tiled=True),
        lax.psum_scatter(gradients[5], ("dp", "row"), scatter_dimension=1, tiled=True),
    )
    return tuple(leading) + tuple(trailing)


def heads_of(rows_block):
    return rows_block.reshape(rows_block.shape[0], -1, HD)


def block_of(rows_all, start, block_rows):
    return heads_of(lax.dynamic_slice_in_dim(rows_all, start, block_rows, 0))


def block_scores(query_heads, key_heads, query_start, key_start, length):
    block_rows = query_heads.shape[0]
    scores = jnp.einsum(
        "qhd,khd->hqk", query_heads, key_heads, preferred_element_type=jnp.float32
    ) * HD ** (-0.5)
    query_pos = query_start + jnp.arange(block_rows, dtype=jnp.int32)
    key_pos = key_start + jnp.arange(key_heads.shape[0], dtype=jnp.int32)
    allowed = (key_pos[None, :] <= query_pos[:, None]) & (key_pos[None, :] < length)
    return jnp.where(allowed[None], scores, MASKED)


def key_block_count(row_place, length, block_rows):
    return jnp.minimum(row_place + 1, (length + block_rows - 1) // block_rows)


def attention_forward(queries, key_rows, value_rows, row_place, length):
    block_rows = queries.shape[0]
    query_heads = heads_of(queries)
    head_count = query_heads.shape[1]
    query_start = row_place * block_rows
    count = key_block_count(row_place, length, block_rows)

    def stats_step(block_index, carry):
        highest, partition = carry
        start = block_index * block_rows
        scores = block_scores(
            query_heads, block_of(key_rows, start, block_rows), query_start, start, length
        )
        newest = jnp.maximum(highest, jnp.max(scores, axis=-1, keepdims=True))
        partition = partition * jnp.exp(highest - newest) + jnp.sum(
            jnp.exp(scores - newest), axis=-1, keepdims=True
        )
        return (newest, partition)

    start_stats = (
        jnp.full((head_count, block_rows, 1), MASKED, jnp.float32),
        jnp.zeros((head_count, block_rows, 1), jnp.float32),
    )
    highest, partition = lax.fori_loop(0, count, stats_step, start_stats)

    def output_step(block_index, total):
        start = block_index * block_rows
        scores = block_scores(
            query_heads, block_of(key_rows, start, block_rows), query_start, start, length
        )
        weights_low = (jnp.exp(scores - highest) / partition).astype(jnp.bfloat16)
        return total + jnp.einsum(
            "hqk,khd->qhd",
            weights_low,
            block_of(value_rows, start, block_rows),
            preferred_element_type=jnp.float32,
        )

    total = lax.fori_loop(0, count, output_step, jnp.zeros(query_heads.shape, jnp.float32))
    return (total.reshape(block_rows, -1), highest, partition)


def attention_query_side(
    queries, key_rows, value_rows, grad_attended, highest, partition, row_place, length
):
    block_rows = queries.shape[0]
    seq_rows = key_rows.shape[0]
    query_heads = heads_of(queries)
    grad_heads = heads_of(grad_attended)
    head_count = query_heads.shape[1]
    query_start = row_place * block_rows
    count = key_block_count(row_place, length, block_rows)

    def inner_step(block_index, total):
        start = block_index * block_rows
        scores = block_scores(
            query_heads, block_of(key_rows, start, block_rows), query_start, start, length
        )
        weights = jnp.exp(scores - highest) / partition
        grad_weights = jnp.einsum(
            "qhd,khd->hqk",
            grad_heads,
            block_of(value_rows, start, block_rows),
            preferred_element_type=jnp.float32,
        )
        return total + jnp.sum(weights * grad_weights, axis=-1, keepdims=True)

    inner = lax.fori_loop(0, count, inner_step, jnp.zeros((head_count, block_rows, 1), jnp.float32))

    def grad_step(block_index, carry):
        start = block_index * block_rows
        key_heads = block_of(key_rows, start, block_rows)
        scores = block_scores(query_heads, key_heads, query_start, start, length)
        weights = jnp.exp(scores - highest) / partition
        grad_weights = jnp.einsum(
            "qhd,khd->hqk",
            grad_heads,
            block_of(value_rows, start, block_rows),
            preferred_element_type=jnp.float32,
        )
        grad_scores = (weights * (grad_weights - inner)).astype(jnp.bfloat16)
        query_total = carry[0] + jnp.einsum(
            "hqk,khd->qhd", grad_scores, key_heads, preferred_element_type=jnp.float32
        )
        weights_low = weights.astype(jnp.bfloat16)
        key_part = jnp.einsum(
            "hqk,qhd->khd", grad_scores, query_heads, preferred_element_type=jnp.float32
        )
        value_part = jnp.einsum(
            "hqk,qhd->khd", weights_low, grad_heads, preferred_element_type=jnp.float32
        )
        key_total = lax.dynamic_update_slice_in_dim(
            carry[1], lax.dynamic_slice_in_dim(carry[1], start, block_rows, 0) + key_part, start, 0
        )
        value_total = lax.dynamic_update_slice_in_dim(
            carry[2],
            lax.dynamic_slice_in_dim(carry[2], start, block_rows, 0) + value_part,
            start,
            0,
        )
        return (query_total, key_total, value_total)

    start_carry = (jnp.zeros(query_heads.shape, jnp.float32),)
    start_carry = start_carry + (
        jnp.zeros((seq_rows, head_count, HD), jnp.float32),
        jnp.zeros((seq_rows, head_count, HD), jnp.float32),
    )
    totals = lax.fori_loop(0, count, grad_step, start_carry)
    query_terms = totals[0].reshape(block_rows, -1) * HD ** (-0.5)
    return (
        query_terms,
        totals[1].reshape(seq_rows, -1) * HD ** (-0.5),
        totals[2].reshape(seq_rows, -1),
        inner,
    )


def local_general(
    tokens,
    lengths,
    first_gain,
    first_shift,
    w_query,
    w_key,
    w_value,
    bias_query,
    bias_value,
    w_output,
    bias_output,
    second_gain,
    second_shift,
    w_up,
    bias_up,
    w_down,
    bias_down,
    cotangent,
):
    micro_count, own_rows, width = tokens.shape
    col_count = lax.axis_size("col")
    group_rows = own_rows * col_count
    row_place = lax.axis_index("row")
    col_place = lax.axis_index("col")
    head_width = w_query.shape[1]
    hidden_width = w_up.shape[1]
    own_positions = (
        row_place * group_rows + col_place * own_rows + jnp.arange(own_rows, dtype=jnp.int32)
    )
    weight_totals = (
        jnp.zeros((width, head_width), jnp.float32),
        jnp.zeros((width, head_width), jnp.float32),
        jnp.zeros((width, head_width), jnp.float32),
        jnp.zeros((width, hidden_width), jnp.float32),
        jnp.zeros((head_width, width), jnp.float32),
        jnp.zeros((hidden_width, width), jnp.float32),
    )
    vector_totals = (
        jnp.zeros((width,), jnp.float32),
        jnp.zeros((width,), jnp.float32),
        jnp.zeros((head_width,), jnp.float32),
        jnp.zeros((head_width,), jnp.float32),
        jnp.zeros((width,), jnp.float32),
        jnp.zeros((width,), jnp.float32),
        jnp.zeros((width,), jnp.float32),
        jnp.zeros((hidden_width,), jnp.float32),
        jnp.zeros((width,), jnp.float32),
    )
    results = []
    input_grads = []
    for micro_index in range(micro_count):
        gathered = fetch_weights(w_query, w_key, w_value, w_up, w_output, w_down)
        query_full, key_full, value_full, up_full, output_full, down_full = gathered
        length = lengths[0, micro_index]
        inputs = tokens[micro_index].astype(jnp.float32)
        normed = layer_norm(inputs, first_gain, first_shift).astype(jnp.bfloat16)
        normed_all = spread_rows(normed)
        queries = (product(normed_all, query_full) + bias_query).astype(jnp.bfloat16)
        keys_local = product(normed_all, key_full).astype(jnp.bfloat16)
        values_local = (product(normed_all, value_full) + bias_value).astype(jnp.bfloat16)
        keys_all, values_all = (
            lax.all_gather(keys_local, "row", axis=0, tiled=True),
            lax.all_gather(values_local, "row", axis=0, tiled=True),
        )
        attended, maxima, partitions = attention_forward(
            queries, keys_all, values_all, row_place, length
        )
        attended_low = attended.astype(jnp.bfloat16)
        branch = fold_rows(product(attended_low, output_full)) + bias_output
        middle = inputs + branch
        second_normed = layer_norm(middle, second_gain, second_shift).astype(jnp.bfloat16)
        second_all = spread_rows(second_normed)
        pre_activation = product(second_all, up_full) + bias_up
        activated = gelu_tanh(pre_activation).astype(jnp.bfloat16)
        result = middle + (fold_rows(product(activated, down_full)) + bias_down)
        results.append(result.astype(jnp.bfloat16))
        query_full, key_full, value_full, up_full, output_full, down_full = fetch_weights(
            w_query, w_key, w_value, w_up, w_output, w_down
        )
        validity = (own_positions < length).astype(jnp.float32)
        grad_result = cotangent[micro_index].astype(jnp.float32) * validity[:, None]
        grad_result_all = spread_rows(grad_result.astype(jnp.bfloat16))
        grad_down = transposed_left(activated, grad_result_all)
        grad_activated = transposed_right(grad_result_all, down_full)
        gelu_back = jax.vjp(gelu_tanh, pre_activation)[1]
        grad_pre = gelu_back(grad_activated)[0].astype(jnp.bfloat16)
        grad_up = transposed_left(second_all, grad_pre)
        grad_second_normed = fold_rows(transposed_right(grad_pre, up_full))
        second_back = jax.vjp(layer_norm, middle, second_gain, second_shift)[1]
        grad_middle_norm, grad_second_gain, grad_second_shift = second_back(grad_second_normed)
        grad_middle = grad_result + grad_middle_norm
        grad_branch = grad_middle.astype(jnp.bfloat16)
        grad_branch_all = spread_rows(grad_branch)
        grad_output = transposed_left(attended_low, grad_branch_all)
        grad_attended = transposed_right(grad_branch_all, output_full).astype(jnp.bfloat16)
        query_terms, key_terms, value_terms, inner = attention_query_side(
            queries, keys_all, values_all, grad_attended, maxima, partitions, row_place, length
        )
        key_sums, value_sums = (
            lax.psum_scatter(key_terms, "row", scatter_dimension=0, tiled=True),
            lax.psum_scatter(value_terms, "row", scatter_dimension=0, tiled=True),
        )
        grad_queries = query_terms.astype(jnp.bfloat16)
        grad_keys = key_sums.astype(jnp.bfloat16)
        grad_values = value_sums.astype(jnp.bfloat16)
        grad_query = transposed_left(normed_all, grad_queries)
        grad_key = transposed_left(normed_all, grad_keys)
        grad_value = transposed_left(normed_all, grad_values)
        grad_normed = fold_rows(
            transposed_right(grad_queries, query_full)
            + transposed_right(grad_keys, key_full)
            + transposed_right(grad_values, value_full)
        )
        first_back = jax.vjp(layer_norm, inputs, first_gain, first_shift)[1]
        grad_inputs_norm, grad_first_gain, grad_first_shift = first_back(grad_normed)
        input_grads.append((grad_middle + grad_inputs_norm).astype(jnp.bfloat16))
        local_grads = (grad_query, grad_key, grad_value, grad_up, grad_output, grad_down)
        weight_totals = tuple(
            (former + latter for former, latter in zip(weight_totals, local_grads))
        )
        local_vectors = (
            grad_first_gain,
            grad_first_shift,
            jnp.sum(grad_queries.astype(jnp.float32), axis=0),
            jnp.sum(grad_values.astype(jnp.float32), axis=0),
            jnp.sum(grad_branch.astype(jnp.float32), axis=0),
            grad_second_gain,
            grad_second_shift,
            jnp.sum(grad_pre.astype(jnp.float32), axis=0),
            jnp.sum(grad_result, axis=0),
        )
        vector_totals = tuple(
            (former + latter for former, latter in zip(vector_totals, local_vectors))
        )
    weight_totals = reduce_blocks(weight_totals)

    def widen(vector_part):
        blank = jnp.zeros((vector_part.shape[0] * col_count,), jnp.float32)
        return lax.dynamic_update_slice(blank, vector_part, (col_place * vector_part.shape[0],))

    def narrow(whole_vector, piece_width):
        return lax.dynamic_slice_in_dim(whole_vector, col_place * piece_width, piece_width)

    (
        sum_first_gain,
        sum_first_shift,
        sum_bias_query,
        sum_bias_value,
        sum_bias_output,
        sum_second_gain,
        sum_second_shift,
        sum_bias_up,
        sum_bias_down,
    ) = lax.psum(
        (
            vector_totals[0],
            vector_totals[1],
            widen(vector_totals[2]),
            widen(vector_totals[3]),
            vector_totals[4],
            vector_totals[5],
            vector_totals[6],
            widen(vector_totals[7]),
            vector_totals[8],
        ),
        ("dp", "row", "col"),
    )
    grad_w_query, grad_w_key, grad_w_value, grad_w_up, grad_w_output, grad_w_down = weight_totals
    return (
        jnp.stack(results, axis=0),
        jnp.stack(input_grads, axis=0),
        sum_first_gain,
        sum_first_shift,
        grad_w_query,
        grad_w_key,
        grad_w_value,
        narrow(sum_bias_query, head_width),
        narrow(sum_bias_value, head_width),
        grad_w_output,
        sum_bias_output,
        sum_second_gain,
        sum_second_shift,
        grad_w_up,
        narrow(sum_bias_up, hidden_width),
        grad_w_down,
        sum_bias_down,
    )


F32 = jnp.float32
LOW = jnp.bfloat16
VMEM_LIMIT = 56 * 1024 * 1024


def fits(mesh):
    return mesh.shape["row"] == 4 and mesh.shape["col"] == 4 and mesh.shape["dp"] == 2


def contract(former, latter, former_dim, latter_dim):
    return lax.dot_general(
        former,
        latter,
        (((former_dim,), (latter_dim,)), ((), ())),
        preferred_element_type=jnp.float32,
    )


def norm_parts(values):
    centered = values - jnp.mean(values, axis=-1, keepdims=True)
    scale = lax.rsqrt(jnp.mean(centered * centered, axis=-1, keepdims=True) + EPSILON)
    return centered * scale, scale


def norm_back(grads, gain, unit, scale):
    inner = grads * gain
    mean_inner = jnp.mean(inner, axis=-1, keepdims=True)
    mean_unit = jnp.mean(inner * unit, axis=-1, keepdims=True)
    return scale * (inner - mean_inner - unit * mean_unit)


GELU_SCALE = 0.7978845608028654
GELU_CUBE = 0.044715


def gelu_parts(values):
    square = values * values
    curve = jnp.tanh(GELU_SCALE * values * (1.0 + GELU_CUBE * square))
    half = 0.5 + 0.5 * curve
    slope = half + 0.5 * values * (1.0 - curve * curve) * (GELU_SCALE * (1.0 + 3.0 * GELU_CUBE * square))
    return values * half, slope


def peers():
    place = lax.axis_index("col")
    return {"col": place + 1 - 2 * (place % 2)}, {"col": (place + 2) % 4}


def remote(source, target, send_sem, recv_sem, device):
    return pltpu.make_async_remote_copy(
        src_ref=source,
        dst_ref=target,
        send_sem=send_sem,
        recv_sem=recv_sem,
        device_id=device,
        device_id_type=pl.DeviceIdType.MESH,
    )


def row_peers():
    row = lax.axis_index("row")
    return row + 1 - 2 * (row % 2), (row + 2) % 4, 3 - row


def greet_all(core, far):
    row = lax.axis_index("row")
    cross = {"dp": 1 - lax.axis_index("dp")}
    barrier = pltpu.get_barrier_semaphore()
    rows = [{"row": (row + step) % 4} for step in (1, 2, 3)]
    for device in [core, far, cross] + rows:
        pl.semaphore_signal(barrier, inc=1, device_id=device, device_id_type=pl.DeviceIdType.MESH)
    pl.semaphore_wait(barrier, 6)


class Gather:
    def __init__(self, slot, z_send, z_recv, x_send, x_recv):
        self.slot, self.z_send, self.z_recv, self.x_send, self.x_recv = slot, z_send, z_recv, x_send, x_recv
        self.row, self.dp = lax.axis_index("row"), lax.axis_index("dp")

    def lane(self, d):
        if d == 0:
            return self.row, {"row": jnp.minimum(self.row + 1, 3)}
        return 3 - self.row, {"row": jnp.maximum(self.row - 1, 0)}

    def z_copy(self, d, k, block):
        view = self.slot(self.dp * 4 + block)
        return remote(view, view, self.z_send.at[d, k], self.z_recv.at[d, k], self.lane(d)[1])

    def x_copy(self, block):
        view = self.slot(self.dp * 4 + block)
        return remote(view, view, self.x_send.at[block], self.x_recv.at[block], {"dp": 1 - self.dp})

    def pump(self, k):
        for d in range(2):
            place, _ = self.lane(d)
            block = self.row - k if d == 0 else self.row + k
            if k == 0:
                if d == 0:
                    self.x_copy(block).start()

                @pl.when(place <= 2)
                def _():
                    self.z_copy(d, 0, block).start()
            else:

                @pl.when(place >= k)
                def _():
                    self.z_copy(d, k - 1, block).wait_recv()
                    if k < 3:

                        @pl.when(place <= 2)
                        def _():
                            self.z_copy(d, k, block).start()

                    self.x_copy(block).start()

    def arrive(self):
        for block in range(4):
            view = self.slot((1 - self.dp) * 4 + block)
            remote(view, view, self.x_send.at[block], self.x_recv.at[block], {"dp": 1 - self.dp}).wait_recv()

    def sent(self):
        for block in range(4):
            self.x_copy(block).wait_send()
        for d in range(2):
            place, _ = self.lane(d)
            for k in range(3):

                @pl.when((place >= k) & (place <= 2))
                def _():
                    self.z_copy(d, k, self.row - k if d == 0 else self.row + k).wait_send()


class Spread:
    def __init__(self, source, target, trade_send, trade_recv, send, recv):
        self.source, self.target = source, target
        self.trade_send, self.trade_recv, self.send, self.recv = trade_send, trade_recv, send, recv
        self.core, self.far = peers()
        self.row = lax.axis_index("row")

    def trade_copy(self, place):
        return remote(
            self.source.at[place],
            self.target.at[self.row, 0],
            self.trade_send.at[place],
            self.trade_recv.at[self.row],
            {"row": place},
        )

    def trade(self):
        for place in row_peers():
            self.trade_copy(place).start()

    def traded(self):
        for place in row_peers():
            self.trade_copy(place).wait_send()

    def hop(self, step, r):
        source, target, device = ((0, 1, self.core), (0, 2, self.far), (2, 3, self.core))[step]
        return remote(
            self.target.at[r, source], self.target.at[r, target], self.send.at[step, r], self.recv.at[step, r], device
        )

    def first(self, r, own):
        if not own:
            remote(
                self.source.at[r],
                self.target.at[r, 0],
                self.trade_send.at[r],
                self.trade_recv.at[r],
                {"row": r},
            ).wait_recv()
        self.hop(1, r).start()
        self.hop(0, r).start()

    def relay(self, r):
        self.hop(1, r).wait()
        self.hop(2, r).start()

    def done(self, r):
        self.hop(0, r).wait()
        self.hop(2, r).wait()


def front_kernel(
    tokens_ref,
    wq_ref,
    wk_ref,
    wv_ref,
    wo_ref,
    gain_ref,
    shift_ref,
    bias_q_ref,
    bias_v_ref,
    q_out,
    k_out,
    v_out,
    tok_out,
    proj_out,
    wo_out,
    normed_out,
    rows_all,
    normed,
    trade_send,
    trade_recv,
    send,
    recv,
    za_send,
    za_recv,
    xa_send,
    xa_recv,
    zb_send,
    zb_recv,
    xb_send,
    xb_recv,
    out_sems,
):
    chunks, own, width = tokens_ref.shape
    rows = 4 * own
    head_width = wq_ref.shape[1]
    row = lax.axis_index("row")
    mine = lax.axis_index("dp") * 4 + row
    core, far = peers()

    def wo_slot(block):
        return wo_out.at[:, pl.ds(pl.multiple_of(block * own, own), own)]

    rows_all[row, 0] = tokens_ref[row]
    proj_out[mine, :, :head_width] = wq_ref[...]
    proj_out[mine, :, head_width : 2 * head_width] = wk_ref[...]
    proj_out[mine, :, 2 * head_width :] = wv_ref[...]
    wo_out[:, pl.ds(pl.multiple_of(mine * own, own), own)] = wo_ref[...]
    greet_all(core, far)
    spread = Spread(tokens_ref, rows_all, trade_send, trade_recv, send, recv)
    proj = Gather(lambda block: proj_out.at[block], za_send, za_recv, xa_send, xa_recv)
    output = Gather(wo_slot, zb_send, zb_recv, xb_send, xb_recv)
    near, middle, distant = row_peers()
    spread.trade()
    proj.pump(0)
    spread.first(row, True)
    proj.pump(1)
    spread.first(near, False)
    spread.relay(row)
    proj.pump(2)
    output.pump(0)
    spread.first(middle, False)
    proj.pump(3)
    spread.relay(near)
    spread.first(distant, False)
    output.pump(1)
    proj.arrive()

    def project(r):
        spread.done(r)
        here = pl.ds(pl.multiple_of(r * rows, rows), rows)
        values = rows_all[r].reshape(rows, width).astype(F32)
        low = (norm_parts(values)[0] * gain_ref[...] + shift_ref[...]).astype(LOW)
        normed[here] = low
        pltpu.make_async_copy(normed.at[here], normed_out.at[here], out_sems.at[r]).start()
        total = contract(low, proj_out.reshape(8 * own, 3 * head_width)[...], 1, 0)
        q_out[here] = (total[:, :head_width] + bias_q_ref[...]).astype(LOW)
        k_out[here] = total[:, head_width : 2 * head_width].astype(LOW)
        v_out[here] = (total[:, 2 * head_width :] + bias_v_ref[...]).astype(LOW)
        tok_out[r] = rows_all[r, 0]

    project(row)
    output.pump(2)
    spread.relay(middle)
    project(near)
    output.pump(3)
    spread.relay(distant)
    project(middle)
    project(distant)
    output.arrive()
    spread.traded()
    proj.sent()
    output.sent()
    for r in range(4):
        here = slice(r * rows, (r + 1) * rows)
        pltpu.make_async_copy(normed.at[here], normed_out.at[here], out_sems.at[r]).wait()


def front_block(tokens, w_query, w_key, w_value, w_output, gain, shift, bias_query, bias_value):
    chunks, own, width = tokens.shape
    rows = chunks * 4 * own
    head_width = w_query.shape[1]
    vmem = pl.BlockSpec(memory_space=pltpu.VMEM)
    dma = pltpu.SemaphoreType.DMA
    gather_sems = [dma((2, 3)), dma((2, 3)), dma((4,)), dma((4,))]
    return pl.pallas_call(
        front_kernel,
        in_specs=[vmem] * 9,
        out_specs=[vmem] * 6 + [pl.BlockSpec(memory_space=pl.ANY)],
        out_shape=[
            jax.ShapeDtypeStruct((rows, head_width), LOW),
            jax.ShapeDtypeStruct((rows, head_width), LOW),
            jax.ShapeDtypeStruct((rows, head_width), LOW),
            jax.ShapeDtypeStruct((chunks, own, width), LOW),
            jax.ShapeDtypeStruct((8, own, 3 * head_width), LOW),
            jax.ShapeDtypeStruct((head_width, width), LOW),
            jax.ShapeDtypeStruct((rows, width), LOW),
        ],
        scratch_shapes=[
            pltpu.VMEM((chunks, 4, own, width), LOW),
            pltpu.VMEM((rows, width), LOW),
            dma((4,)),
            dma((4,)),
            dma((3, 4)),
            dma((3, 4)),
        ]
        + gather_sems
        + gather_sems
        + [dma((4,))],
        compiler_params=pltpu.CompilerParams(
            collective_id=3, has_side_effects=True, vmem_limit_bytes=56 * 1024 * 1024
        ),
        cost_estimate=pl.CostEstimate(flops=20_000_000_000, bytes_accessed=20_000_000, transcendentals=0),
        name="front_block",
    )(tokens, w_query, w_key, w_value, w_output, gain, shift, bias_query, bias_value)


def feed_kernel(
    q_ref,
    k_ref,
    v_ref,
    key_bias_ref,
    causal_ref,
    wo_ref,
    wu_shard,
    wd_shard,
    tok_ref,
    cot_ref,
    vec_ref,
    bias_up_ref,
    att_ref,
    lse_ref,
    result_ref,
    gatt_ref,
    gmid_ref,
    gout_ref,
    gup_ref,
    gdown_ref,
    sums_ref,
    sum_up_ref,
    wu_all,
    wd_ref,
    g_all,
    kept,
    kept_q,
    core_out,
    core_in,
    core_in_q,
    far_out,
    far_in,
    far_out_q,
    far_in_q,
    middle,
    second,
    act,
    gpre,
    branch,
    stage,
    stage_up,
    stage_sems,
    send_sems,
    recv_sems,
    trade_send,
    trade_recv,
    g_send,
    g_recv,
    zu_send,
    zu_recv,
    xu_send,
    xu_recv,
    zd_send,
    zd_recv,
    xd_send,
    xd_recv,
):
    chunks, blocks, own, width = second.shape
    rows = blocks * own
    hidden = wu_all.shape[2]
    core, far = peers()
    row = lax.axis_index("row")
    mine = lax.axis_index("dp") * 4 + row
    wu_ref = wu_all.reshape(width, hidden)

    def wd_slot(block):
        return wd_ref.at[:, pl.ds(pl.multiple_of(block * own, own), own)]

    g_all[row, 0] = cot_ref[row]
    wu_all[mine] = wu_shard[...]
    wd_ref[:, pl.ds(pl.multiple_of(mine * own, own), own)] = wd_shard[...]
    spread = Spread(cot_ref, g_all, trade_send, trade_recv, g_send, g_recv)
    up = Gather(lambda block: wu_all.at[block], zu_send, zu_recv, xu_send, xu_recv)
    down = Gather(wd_slot, zd_send, zd_recv, xd_send, xd_recv)
    near, halfway, distant = row_peers()

    def core_copy(step, r, source, target):
        return remote(source.at[r], target.at[r], send_sems.at[step, r], recv_sems.at[step, r], core)

    def far_copy(step, r, source, target):
        return remote(source.at[r], target.at[r], send_sems.at[step, r], recv_sems.at[step, r], far)

    def spread_core(step, r, rows_ref):
        return remote(rows_ref.at[r, 0], rows_ref.at[r, 1], send_sems.at[step, r], recv_sems.at[step, r], core)

    def spread_far(step, r, rows_ref):
        return remote(rows_ref.at[r, 0], rows_ref.at[r, 2], send_sems.at[step, r], recv_sems.at[step, r], far)

    def spread_relay(step, r, rows_ref):
        return remote(rows_ref.at[r, 2], rows_ref.at[r, 3], send_sems.at[step, r], recv_sems.at[step, r], core)

    def split(r, total, kept_ref, out_ref):
        kept_ref[r, 0] = total[:own].astype(kept_ref.dtype)
        out_ref[r, 0] = total[own : 2 * own].astype(LOW)
        kept_ref[r, 1] = total[2 * own : 3 * own].astype(kept_ref.dtype)
        out_ref[r, 1] = total[3 * own :].astype(LOW)

    def fold(r, kept_ref, in_ref, out_ref):
        out_ref[r] = (kept_ref[r, 1].astype(F32) + in_ref[r, 1].astype(F32)).astype(LOW)
        kept_ref[r, 0] = (kept_ref[r, 0].astype(F32) + in_ref[r, 0].astype(F32)).astype(kept_ref.dtype)

    def each(body):
        lax.fori_loop(0, chunks, lambda r, carry: (body(r), carry)[1], 0)

    def out_projection(r):
        split(r, contract(att_ref[r * rows : (r + 1) * rows], wo_ref[...], 1, 0), kept, core_out)
        core_copy(0, r, core_out, core_in).start()

    def out_fold(r):
        core_copy(0, r, core_out, core_in).wait()
        fold(r, kept, core_in, far_out)
        far_copy(1, r, far_out, far_in).start()

    block = 256
    lane = lax.broadcasted_iota(jnp.int32, (block, 128), 1)

    def attention(r):
        long = (r + 1) * rows

        def part(step, carry):
            here = pl.ds(pl.multiple_of(r * rows + (step % 2) * block, block), block)
            pair = pl.ds(pl.multiple_of((step // 2) * 128, 128), 128)
            inside = pl.ds(pl.multiple_of((step % 2) * block, block), block)
            queries = q_ref[here, pair]
            parts = []
            for head in range(2):
                masked = jnp.where((lane // HD) == head, queries, 0) * jnp.asarray(HD**-0.5, LOW)
                scores = contract(masked, k_ref[:long, pair], 1, 1) + key_bias_ref[:, :long]
                last = scores[:, long - rows :] + causal_ref[inside]
                scores = last if r == 0 else jnp.concatenate([scores[:, : long - rows], last], axis=1)
                highest = jnp.max(scores, axis=1, keepdims=True)
                weights = jnp.exp(scores - highest)
                total = jnp.sum(weights, axis=1, keepdims=True)
                parts.append(contract(weights.astype(LOW), v_ref[:long, pair], 1, 0) / total)
                flat = jnp.broadcast_to(highest + jnp.log(total), (block, 128))
                lse_ref[step // 2, r, head : head + 1, inside] = flat.T[:1]
            att_ref[here, pair] = jnp.where(lane < HD, parts[0], parts[1]).astype(LOW)
            return carry

        lax.fori_loop(0, 4, part, 0)
        out_projection(r)

    greet_all(core, far)
    spread.trade()
    up.pump(0)
    down.pump(0)
    spread.first(row, True)
    attention(0)
    spread.first(near, False)
    attention(1)
    out_fold(0)
    spread.relay(row)
    up.pump(1)
    attention(2)
    out_fold(1)
    spread.first(halfway, False)
    spread.relay(near)
    down.pump(1)
    up.pump(2)
    attention(3)
    out_fold(2)
    spread.first(distant, False)
    down.pump(2)
    out_fold(3)
    up.pump(3)

    def norm(r):
        far_copy(1, r, far_out, far_in).wait()
        values = tok_ref[r].astype(F32) + (kept[r, 0] + far_in[r].astype(F32) + vec_ref[0:1])
        middle[r] = values
        second[r, 0] = (norm_parts(values)[0] * vec_ref[1:2] + vec_ref[2:3]).astype(LOW)
        spread_core(2, r, second).start()
        spread_far(3, r, second).start()

    each(norm)
    down.pump(3)
    spread.relay(halfway)
    spread.relay(distant)
    up.arrive()
    down.arrive()
    for r in range(chunks):
        spread.done(r)

    sum_up_ref[...] = jnp.zeros_like(sum_up_ref)

    def feed(r):
        spread_far(3, r, second).wait()
        spread_relay(4, r, second).start()
        spread_core(2, r, second).wait()
        spread_relay(4, r, second).wait()
        pre = contract(second[r].reshape(rows, width), wu_ref[...], 1, 0) + bias_up_ref[...]
        activated, slope = gelu_parts(pre)
        act[r] = activated.astype(LOW).reshape(blocks, own, hidden)
        grads = contract(g_all[r].reshape(rows, width), wd_ref[...], 1, 1) * slope
        grads_low = grads.astype(LOW)
        gpre[r] = grads_low.reshape(blocks, own, hidden)
        sum_up_ref[...] += jnp.sum(grads_low.astype(F32), axis=0, keepdims=True)
        split(r, contract(grads_low, wu_ref[...], 1, 1), kept, core_out)
        core_copy(5, r, core_out, core_in).start()
        core_copy(5, r, core_out, core_in).wait()
        fold(r, kept, core_in, far_out)
        far_copy(6, r, far_out, far_in).start()
        split(r, contract(act[r].reshape(rows, hidden), wd_ref[...], 1, 0), kept_q, core_out)
        core_copy(7, r, core_out, core_in_q).start()

    each(feed)
    sums_ref[...] = jnp.zeros_like(sums_ref)

    def norm_grad(r):
        far_copy(6, r, far_out, far_in).wait()
        grads = kept[r, 0] + far_in[r].astype(F32)
        unit, scale = norm_parts(middle[r])
        place = g_all[r, 0].astype(F32)
        total = place + norm_back(grads, vec_ref[1:2], unit, scale)
        low = total.astype(LOW)
        gmid_ref[r] = low
        branch[r, 0] = low
        spread_core(9, r, branch).start()
        spread_far(10, r, branch).start()
        sums_ref[0:1] += jnp.sum(low.astype(F32), axis=0, keepdims=True)
        sums_ref[1:2] += jnp.sum(grads * unit, axis=0, keepdims=True)
        sums_ref[2:3] += jnp.sum(grads, axis=0, keepdims=True)
        sums_ref[3:4] += jnp.sum(place, axis=0, keepdims=True)

    each(norm_grad)

    def result_fold(r):
        core_copy(7, r, core_out, core_in_q).wait()
        fold(r, kept_q, core_in_q, far_out_q)
        far_copy(8, r, far_out_q, far_in_q).start()

    each(result_fold)

    wide = 256
    flat_second = second.reshape(chunks * rows, width)
    flat_act = act.reshape(chunks * rows, hidden)
    flat_gpre = gpre.reshape(chunks * rows, hidden)
    flat_g = g_all.reshape(chunks * rows, width)
    flat_branch = branch.reshape(chunks * rows, width)

    def down_grad(t):
        part = pl.ds(pl.multiple_of(t * wide, wide), wide)
        total = contract(flat_act[:, part], flat_g[...], 0, 0).astype(LOW)
        for b in range(8):
            stage[b] = total[:, b * own : (b + 1) * own]
        copy = pltpu.make_async_copy(stage, gdown_ref.at[:, part], stage_sems.at[0])
        copy.start()
        copy.wait()

    lax.fori_loop(0, hidden // wide, lambda t, c: (down_grad(t), c)[1], 0)

    def attended_grad(r):
        spread_far(10, r, branch).wait()
        spread_relay(11, r, branch).start()
        spread_core(9, r, branch).wait()
        spread_relay(11, r, branch).wait()
        rows_here = pl.ds(pl.multiple_of(r * rows, rows), rows)
        gatt_ref[rows_here] = contract(branch[r].reshape(rows, width), wo_ref[...], 1, 1).astype(LOW)

    each(attended_grad)

    def up_grad(t):
        part = pl.ds(pl.multiple_of(t * wide, wide), wide)
        total = contract(flat_second[:, part], flat_gpre[...], 0, 0).astype(LOW)
        for b in range(2):
            stage_up[b] = total[b * own : (b + 1) * own]
        copy = pltpu.make_async_copy(stage_up, gup_ref.at[pl.ds(2 * t, 2)], stage_sems.at[1])
        copy.start()
        copy.wait()

    lax.fori_loop(0, width // wide, lambda t, c: (up_grad(t), c)[1], 0)
    total_out = contract(att_ref[...], flat_branch[...], 0, 0).astype(LOW)
    for b in range(8):
        gout_ref[b] = total_out[:, b * own : (b + 1) * own]

    def finish(r):
        far_copy(8, r, far_out_q, far_in_q).wait()
        total = kept_q[r, 0].astype(F32) + far_in_q[r].astype(F32)
        result_ref[r] = (middle[r] + (total + vec_ref[3:4])).astype(LOW)

    each(finish)
    spread.traded()
    up.sent()
    down.sent()


def feed_block(queries, keys, values, key_bias, causal, w_output, w_up, w_down, own_tokens, grads, vectors, bias_up):
    chunks, own, width = own_tokens.shape
    rows = chunks * 4 * own
    head_width = w_output.shape[0]
    hidden = w_up.shape[1]
    half = (chunks, 2, own, width)
    one = (chunks, own, width)
    all_rows = (chunks, 4, own, width)
    vmem = pl.BlockSpec(memory_space=pltpu.VMEM)
    hbm = pl.BlockSpec(memory_space=pl.ANY)
    dma = pltpu.SemaphoreType.DMA
    gather_sems = [dma((2, 3)), dma((2, 3)), dma((4,)), dma((4,))]
    return pl.pallas_call(
        feed_kernel,
        in_specs=[vmem] * 12,
        out_specs=[vmem] * 6 + [hbm] * 2 + [vmem] * 2,
        out_shape=[
            jax.ShapeDtypeStruct((rows, head_width), LOW),
            jax.ShapeDtypeStruct((head_width // 128, chunks, 2, rows // chunks), F32),
            jax.ShapeDtypeStruct(one, LOW),
            jax.ShapeDtypeStruct((rows, head_width), LOW),
            jax.ShapeDtypeStruct(one, LOW),
            jax.ShapeDtypeStruct((8, head_width, width // 8), LOW),
            jax.ShapeDtypeStruct((8, width // 8, hidden), LOW),
            jax.ShapeDtypeStruct((8, hidden, width // 8), LOW),
            jax.ShapeDtypeStruct((8, width), F32),
            jax.ShapeDtypeStruct((1, hidden), F32),
        ],
        scratch_shapes=[
            pltpu.VMEM((8, own, hidden), LOW),
            pltpu.VMEM((hidden, width), LOW),
            pltpu.VMEM(all_rows, LOW),
            pltpu.VMEM(half, F32),
            pltpu.VMEM(half, LOW),
            pltpu.VMEM(half, LOW),
            pltpu.VMEM(half, LOW),
            pltpu.VMEM(half, LOW),
            pltpu.VMEM(one, LOW),
            pltpu.VMEM(one, LOW),
            pltpu.VMEM(one, LOW),
            pltpu.VMEM(one, LOW),
            pltpu.VMEM(one, F32),
            pltpu.VMEM(all_rows, LOW),
            pltpu.VMEM((chunks, 4, own, hidden), LOW),
            pltpu.VMEM((chunks, 4, own, hidden), LOW),
            pltpu.VMEM(all_rows, LOW),
            pltpu.VMEM((8, 256, width // 8), LOW),
            pltpu.VMEM((2, width // 8, hidden), LOW),
            dma((2,)),
            dma((12, chunks)),
            dma((12, chunks)),
            dma((4,)),
            dma((4,)),
            dma((3, 4)),
            dma((3, 4)),
        ]
        + gather_sems
        + gather_sems,
        compiler_params=pltpu.CompilerParams(
            collective_id=1, has_side_effects=True, vmem_limit_bytes=61 * 1024 * 1024
        ),
        cost_estimate=pl.CostEstimate(flops=100_000_000_000, bytes_accessed=30_000_000, transcendentals=0),
        name="feed_block",
    )(queries, keys, values, key_bias, causal, w_output, w_up, w_down, own_tokens, grads, vectors, bias_up)


def back_kernel(
    q_ref,
    k_ref,
    v_ref,
    do_ref,
    o_ref,
    lse_ref,
    key_bias_ref,
    causal_ref,
    w_ref,
    tok_ref,
    gmid_ref,
    res_ref,
    gdown_ref,
    gup_ref,
    gout_ref,
    gain_ref,
    sums_ref,
    sum_up_ref,
    normed_ref,
    res_out,
    gtok_out,
    down_out,
    up_out,
    out_out,
    proj_out,
    shared_out,
    by_col_out,
    dk_sum,
    dv_sum,
    dproj,
    gproj,
    kept,
    core_out,
    core_in,
    far_out,
    far_in,
    gtok,
    norm_tile,
    x_down,
    x_up,
    x_out,
    x_proj,
    z_down,
    z_up,
    z_out,
    z_proj,
    vec,
    vec_in,
    res_send,
    res_recv,
    tok_send,
    tok_recv,
    fold_send,
    fold_recv,
    x_send,
    x_recv,
    z_send,
    z_recv,
    vec_send,
    vec_recv,
    tile_sem,
):
    chunks, own, width = tok_ref.shape
    rows = 4 * own
    head_width = q_ref.shape[1]
    core, far = peers()
    row = lax.axis_index("row")
    dp = lax.axis_index("dp")
    cross = {"dp": 1 - dp}
    other = lambda r: {"row": r}
    sets = (
        (gdown_ref, x_down, z_down, down_out),
        (gup_ref, x_up, z_up, up_out),
        (gout_ref, x_out, z_out, out_out),
        (gproj, x_proj, z_proj, proj_out),
    )

    barrier = pltpu.get_barrier_semaphore()
    for device in (core, far, cross, other((row + 1) % 4), other((row + 2) % 4), other((row + 3) % 4)):
        pl.semaphore_signal(barrier, inc=1, device_id=device, device_id_type=pl.DeviceIdType.MESH)
    pl.semaphore_wait(barrier, 6)

    def trade(r, source, target, send, recv):
        return remote(source.at[r], target.at[row], send.at[r], recv.at[row], other(r))

    def trade_start(r, source, target, send, recv):
        @pl.when(row != r)
        def _():
            trade(r, source, target, send, recv).start()

        @pl.when(row == r)
        def _():
            target[r] = source[r]

    def trade_wait(source, target, send, recv):
        for r in range(4):

            @pl.when(row != r)
            def _():
                trade(r, source, target, send, recv).wait_send()
                remote(source.at[r], target.at[r], send.at[r], recv.at[r], other(r)).wait_recv()

    def x_copy(i):
        grads, arrived, _, _ = sets[i]
        return remote(grads.at[pl.ds((1 - dp) * 4, 4)], arrived, x_send.at[i], x_recv.at[i], cross)

    def x_add(i):
        grads, arrived, _, _ = sets[i]
        x_copy(i).wait()
        for b in range(4):
            arrived[b] = (arrived[b].astype(F32) + grads[dp * 4 + b].astype(F32)).astype(LOW)

    def lanes(d):
        place = row if d == 0 else 3 - row
        following = {"row": jnp.minimum(row + 1, 3)} if d == 0 else {"row": jnp.maximum(row - 1, 0)}
        return place, following

    def z_first(i, d, k):
        _, sums, moving, _ = sets[i]
        place, following = lanes(d)
        block = 3 - k if d == 0 else k
        return remote(sums.at[block], moving.at[d, k], z_send.at[i, d, k], z_recv.at[i, d, k], following)

    def z_next(i, d, k):
        _, sums, moving, _ = sets[i]
        place, following = lanes(d)
        return remote(moving.at[d, k - 1], moving.at[d, k], z_send.at[i, d, k], z_recv.at[i, d, k], following)

    def z_pump(i, k):
        _, sums, moving, _ = sets[i]
        for d in range(2):
            place, following = lanes(d)

            @pl.when(place == 0)
            def _():
                z_first(i, d, k).start()

            if k >= 1:

                @pl.when((place >= 1) & (place <= k))
                def _():
                    block = 3 - k + place if d == 0 else k - place
                    z_first(i, d, k - 1).wait_recv()
                    moving[d, k - 1] = (moving[d, k - 1].astype(F32) + sums[block].astype(F32)).astype(LOW)
                    z_next(i, d, k).start()

    def z_finish(i):
        _, sums, moving, out = sets[i]
        out[...] = sums[row].astype(F32)
        for d in range(2):
            place, following = lanes(d)

            @pl.when(place >= 1)
            def _():
                z_first(i, d, 2).wait_recv()
                out[...] += moving[d, 2].astype(F32)

        for d in range(2):
            place, following = lanes(d)
            for k in range(3):

                @pl.when(place <= k)
                def _():
                    z_first(i, d, k).wait_send()

    for i in range(3):
        x_copy(i).start()
    for r in range(4):
        trade_start(r, res_ref, res_out, res_send, res_recv)

    block = 256
    lane = lax.broadcasted_iota(jnp.int32, (block, 128), 1)

    def attention(r):
        wide = (r + 1) * rows

        def part(step, carry):
            here = pl.ds(pl.multiple_of(r * rows + (step % 2) * block, block), block)
            pair = pl.ds(pl.multiple_of((step // 2) * 128, 128), 128)
            inside = pl.ds(pl.multiple_of((step % 2) * block, block), block)
            queries = q_ref[here, pair]
            grads = do_ref[here, pair]
            inner = (grads.astype(F32) * o_ref[here, pair].astype(F32)).T
            parts = []
            for head in range(2):
                mine = (lane // HD) == head
                masked = jnp.where(mine, queries, 0) * jnp.asarray(HD**-0.5, LOW)
                masked_grads = jnp.where(mine, grads, 0)
                inner_row = jnp.sum(inner[head * HD : (head + 1) * HD], axis=0, keepdims=True)
                scores = contract(k_ref[:wide, pair], masked, 1, 1) + key_bias_ref[:wide]
                last = scores[wide - rows :] + causal_ref[:, inside]
                scores = last if r == 0 else jnp.concatenate([scores[: wide - rows], last], axis=0)
                weights = jnp.exp(scores - lse_ref[step // 2, r, head : head + 1, inside])
                grad_weights = contract(v_ref[:wide, pair], masked_grads, 1, 1)
                grad_scores = (weights * (grad_weights - inner_row)).astype(LOW)
                dv_sum[:wide, pair] += contract(weights.astype(LOW), masked_grads, 1, 0)
                dk_sum[:wide, pair] += contract(grad_scores, masked, 1, 0)
                parts.append(contract(grad_scores, k_ref[:wide, pair], 0, 0))
            dproj[here, pair] = (jnp.where(lane < HD, parts[0], parts[1]) * HD**-0.5).astype(LOW)
            return carry

        lax.fori_loop(0, 4, part, 0)
        end = slice(wide - rows, wide)
        dproj[end, head_width : 2 * head_width] = dk_sum[end].astype(LOW)
        dproj[end, 2 * head_width :] = dv_sum[end].astype(LOW)

    def core_copy(r):
        return remote(core_out.at[r], core_in.at[r], fold_send.at[0, r], fold_recv.at[0, r], core)

    def far_copy(r):
        return remote(far_out.at[r], far_in.at[r], fold_send.at[1, r], fold_recv.at[1, r], far)

    def project(r):
        total = contract(dproj[r * rows : (r + 1) * rows], w_ref[...], 1, 1)
        kept[r, 0] = total[:own]
        core_out[r, 0] = total[own : 2 * own].astype(LOW)
        kept[r, 1] = total[2 * own : 3 * own]
        core_out[r, 1] = total[3 * own :].astype(LOW)
        core_copy(r).start()

    def fold(r):
        core_copy(r).wait()
        far_out[r] = (kept[r, 1] + core_in[r, 1].astype(F32)).astype(LOW)
        kept[r, 0] = kept[r, 0] + core_in[r, 0].astype(F32)
        far_copy(r).start()

    vec[...] = jnp.zeros_like(vec)

    def norm_grad(r):
        far_copy(r).wait()
        grads = kept[r, 0] + far_in[r].astype(F32)
        unit, scale = norm_parts(tok_ref[r].astype(F32))
        gtok[r] = (gmid_ref[r].astype(F32) + norm_back(grads, gain_ref[...], unit, scale)).astype(LOW)
        trade_start(r, gtok, gtok_out, tok_send, tok_recv)
        vec[0:1] += jnp.sum(grads * unit, axis=0, keepdims=True)
        vec[1:2] += jnp.sum(grads, axis=0, keepdims=True)

    def tile_copy(t):
        part = slice(t * 256, (t + 1) * 256)
        return pltpu.make_async_copy(normed_ref.at[:, part], norm_tile.at[t % 2], tile_sem.at[t % 2])

    dk_sum[...] = jnp.zeros_like(dk_sum)
    dv_sum[...] = jnp.zeros_like(dv_sum)
    tile_copy(0).start()
    tile_copy(1).start()
    attention(3)
    project(3)
    fold(3)
    attention(2)
    project(2)
    fold(2)
    x_add(0)
    z_pump(0, 0)
    attention(1)
    project(1)
    fold(1)
    norm_grad(3)
    z_pump(0, 1)
    attention(0)
    project(0)
    fold(0)
    for t in range(width // 256):
        tile_copy(t).wait()
        total = contract(norm_tile[t % 2], dproj[...], 0, 0).astype(LOW)
        gproj[2 * t] = total[:own]
        gproj[2 * t + 1] = total[own:]
        if t + 2 < width // 256:
            tile_copy(t + 2).start()
    x_copy(3).start()
    norm_grad(2)
    z_pump(0, 2)
    x_add(1)
    z_pump(1, 0)
    norm_grad(1)
    z_pump(1, 1)
    norm_grad(0)
    x_add(2)
    z_pump(2, 0)
    z_pump(1, 2)
    x_add(3)
    z_pump(3, 0)
    z_pump(2, 1)
    z_pump(3, 1)
    z_pump(2, 2)
    z_pump(3, 2)

    vec[2:6] = sums_ref[0:4]
    vec[8:9] = sum_up_ref[...]
    low_sum = jnp.sum(dproj[:, :head_width].astype(F32), axis=0, keepdims=True)
    value_sum = jnp.sum(dproj[:, 2 * head_width :].astype(F32), axis=0, keepdims=True)
    vec[9:10, :head_width] = low_sum
    vec[9:10, head_width : 2 * head_width] = value_sum
    steps = (cross, other(row + 1 - 2 * (row % 2)), other((row + 2) % 4), core, far)
    for step, device in enumerate(steps):
        size = 16 if step < 3 else 8
        copy = remote(vec.at[:size], vec_in.at[step, :size], vec_send.at[step], vec_recv.at[step], device)
        copy.start()
        copy.wait()
        vec[:size] = vec[:size] + vec_in[step, :size]
    shared_out[...] = vec[:8]
    by_col_out[...] = vec[8:]

    for i in range(4):
        z_finish(i)
    trade_wait(res_ref, res_out, res_send, res_recv)
    trade_wait(gtok, gtok_out, tok_send, tok_recv)


def back_block(
    queries, keys, values, grads, attended, lse, key_bias, causal, w_proj, tokens, gmid, result, gdown, gup, gout, gain, sums, sum_up, normed
):
    chunks, own, width = tokens.shape
    rows, head_width = queries.shape
    half = (chunks, 2, own, width)
    one = (chunks, own, width)
    blocks = ((gdown.shape[1], gdown.shape[2]), (gup.shape[1], gup.shape[2]), (gout.shape[1], gout.shape[2]), (own, 3 * head_width))
    vmem = pl.BlockSpec(memory_space=pltpu.VMEM)
    hbm = pl.BlockSpec(memory_space=pl.ANY)
    dma = pltpu.SemaphoreType.DMA
    return pl.pallas_call(
        back_kernel,
        in_specs=[vmem] * 18 + [hbm],
        out_specs=[vmem] * 8,
        out_shape=[jax.ShapeDtypeStruct(one, LOW), jax.ShapeDtypeStruct(one, LOW)]
        + [jax.ShapeDtypeStruct(shape, F32) for shape in blocks]
        + [jax.ShapeDtypeStruct((8, width), F32)] * 2,
        scratch_shapes=[
            pltpu.VMEM((rows, head_width), F32),
            pltpu.VMEM((rows, head_width), F32),
            pltpu.VMEM((rows, 3 * head_width), LOW),
            pltpu.VMEM((8, own, 3 * head_width), LOW),
            pltpu.VMEM(half, F32),
            pltpu.VMEM(half, LOW),
            pltpu.VMEM(half, LOW),
            pltpu.VMEM(one, LOW),
            pltpu.VMEM(one, LOW),
            pltpu.VMEM(one, LOW),
            pltpu.VMEM((2, rows, 256), LOW),
        ]
        + [pltpu.VMEM((4,) + shape, LOW) for shape in blocks]
        + [pltpu.VMEM((2, 3) + shape, LOW) for shape in blocks]
        + [
            pltpu.VMEM((16, width), F32),
            pltpu.VMEM((5, 16, width), F32),
            dma((4,)),
            dma((4,)),
            dma((4,)),
            dma((4,)),
            dma((2, 4)),
            dma((2, 4)),
            dma((4,)),
            dma((4,)),
            dma((4, 2, 3)),
            dma((4, 2, 3)),
            dma((5,)),
            dma((5,)),
            dma((2,)),
        ],
        compiler_params=pltpu.CompilerParams(
            collective_id=2, has_side_effects=True, vmem_limit_bytes=61 * 1024 * 1024
        ),
        cost_estimate=pl.CostEstimate(flops=100_000_000_000, bytes_accessed=30_000_000, transcendentals=0),
        name="back_block",
    )(
        queries, keys, values, grads, attended, lse, key_bias, causal, w_proj, tokens, gmid, result, gdown, gup, gout, gain, sums, sum_up, normed
    )


def local_sequence(
    tokens,
    lengths,
    first_gain,
    first_shift,
    w_query,
    w_key,
    w_value,
    bias_query,
    bias_value,
    w_output,
    bias_output,
    second_gain,
    second_shift,
    w_up,
    bias_up,
    w_down,
    bias_down,
    cotangent,
):
    micro_count, own_rows, width = tokens.shape
    col_count = lax.axis_size("col")
    row_place = lax.axis_index("row")
    col_place = lax.axis_index("col")
    chunk = own_rows * col_count
    seq_rows = chunk * micro_count
    head_width = w_query.shape[1]
    hidden_width = w_up.shape[1]
    length = lax.dynamic_slice_in_dim(lengths[0], row_place, 1)[0]

    inside = (col_place ^ jnp.arange(col_count, dtype=jnp.int32))[:, None] * own_rows + jnp.arange(
        own_rows, dtype=jnp.int32
    )
    inside = inside.reshape(-1)
    positions = (jnp.arange(micro_count, dtype=jnp.int32)[:, None] * chunk + inside).reshape(-1)
    key_bias = jnp.where(positions < length, 0.0, MASKED).astype(F32)
    causal = jnp.where(inside[None, :] <= inside[:, None], 0.0, MASKED).astype(F32)
    all_positions = (
        jnp.arange(own_rows, dtype=jnp.int32) + (row_place * chunk + col_place * own_rows)
    )
    valid = all_positions[None, :] < lengths[0][:, None]
    grads_low = jnp.where(valid[:, :, None], cotangent, jnp.zeros((), LOW))

    queries, keys, values, inputs_low, w_projection, output_full, normed_all = front_block(
        tokens,
        w_query,
        w_key,
        w_value,
        w_output,
        first_gain.reshape(1, width),
        first_shift.reshape(1, width),
        bias_query.reshape(1, -1),
        bias_value.reshape(1, -1),
    )
    vectors = jnp.concatenate(
        [jnp.stack([bias_output, second_gain, second_shift, bias_down]), jnp.zeros((4, width), F32)]
    )
    attended, lse, result, grad_attended, grad_middle, grad_output, grad_up, grad_down, sums, sum_up = feed_block(
        queries,
        keys,
        values,
        key_bias.reshape(1, seq_rows),
        causal,
        output_full,
        w_up,
        w_down,
        inputs_low,
        grads_low,
        vectors,
        bias_up.reshape(1, -1),
    )
    result, grad_tokens, grad_down, grad_up, grad_output, grad_w, shared, by_col = back_block(
        queries,
        keys,
        values,
        grad_attended,
        attended,
        lse,
        key_bias.reshape(seq_rows, 1),
        causal.T,
        w_projection.reshape(width, 3 * head_width),
        inputs_low,
        grad_middle,
        result,
        grad_down,
        grad_up,
        grad_output,
        first_gain.reshape(1, width),
        sums,
        sum_up,
        normed_all,
    )
    return (
        result,
        grad_tokens,
        shared[0],
        shared[1],
        grad_w[:, :head_width],
        grad_w[:, head_width : 2 * head_width],
        grad_w[:, 2 * head_width :],
        by_col[1, :head_width],
        by_col[1, head_width : 2 * head_width],
        grad_output,
        shared[2],
        shared[3],
        shared[4],
        grad_up,
        by_col[0],
        grad_down,
        shared[5],
    )


def solution(mesh):
    return jax.shard_map(
        local_sequence if fits(mesh) else local_general,
        mesh=mesh,
        in_specs=(
            P(None, ("dp", "row", "col"), None),
            P("dp", None),
            P(),
            P(),
            P(("dp", "row"), "col"),
            P(("dp", "row"), "col"),
            P(("dp", "row"), "col"),
            P("col"),
            P("col"),
            P("col", ("dp", "row")),
            P(),
            P(),
            P(),
            P(("dp", "row"), "col"),
            P("col"),
            P("col", ("dp", "row")),
            P(),
            P(None, ("dp", "row", "col"), None),
        ),
        out_specs=(
            P(None, ("dp", "row", "col"), None),
            P(None, ("dp", "row", "col"), None),
            P(),
            P(),
            P(("dp", "row"), "col"),
            P(("dp", "row"), "col"),
            P(("dp", "row"), "col"),
            P("col"),
            P("col"),
            P("col", ("dp", "row")),
            P(),
            P(),
            P(),
            P(("dp", "row"), "col"),
            P("col"),
            P("col", ("dp", "row")),
            P(),
        ),
        check_vma=False,
    )
```

```python
import functools

import jax
import jax.numpy as jnp
from jax import lax
from jax.experimental import pallas as pl
from jax.experimental.pallas import tpu as pltpu
from jax.sharding import PartitionSpec as P

HD = 64


EPSILON = 1e-05
MASKED = -1e30


def layer_norm(values, norm_gain, norm_shift):
    centered = values - jnp.mean(values, axis=-1, keepdims=True)
    variance = jnp.mean(centered * centered, axis=-1, keepdims=True)
    return centered * lax.rsqrt(variance + EPSILON) * norm_gain + norm_shift


def gelu_tanh(values):
    return jax.nn.gelu(values, approximate=True)


def product(former, latter):
    return jnp.dot(former, latter, preferred_element_type=jnp.float32)


def transposed_left(former, latter):
    return lax.dot_general(
        former, latter, (((0,), (0,)), ((), ())), preferred_element_type=jnp.float32
    )


def transposed_right(former, latter):
    return lax.dot_general(
        former, latter, (((1,), (1,)), ((), ())), preferred_element_type=jnp.float32
    )


def spread_rows(rows_block):
    return lax.all_gather(rows_block, "col", axis=0, tiled=True)


def fold_rows(partial_sum):
    return lax.psum_scatter(partial_sum, "col", scatter_dimension=0, tiled=True)


def fetch_weights(w_query, w_key, w_value, w_up, w_output, w_down):
    leading = (
        lax.all_gather(w_query, ("dp", "row"), axis=0, tiled=True),
        lax.all_gather(w_key, ("dp", "row"), axis=0, tiled=True),
        lax.all_gather(w_value, ("dp", "row"), axis=0, tiled=True),
        lax.all_gather(w_up, ("dp", "row"), axis=0, tiled=True),
    )
    trailing = (
        lax.all_gather(w_output, ("dp", "row"), axis=1, tiled=True),
        lax.all_gather(w_down, ("dp", "row"), axis=1, tiled=True),
    )
    return tuple(leading) + tuple(trailing)


def reduce_blocks(gradients):
    leading = (
        lax.psum_scatter(gradients[0], ("dp", "row"), scatter_dimension=0, tiled=True),
        lax.psum_scatter(gradients[1], ("dp", "row"), scatter_dimension=0, tiled=True),
        lax.psum_scatter(gradients[2], ("dp", "row"), scatter_dimension=0, tiled=True),
        lax.psum_scatter(gradients[3], ("dp", "row"), scatter_dimension=0, tiled=True),
    )
    trailing = (
        lax.psum_scatter(gradients[4], ("dp", "row"), scatter_dimension=1, tiled=True),
        lax.psum_scatter(gradients[5], ("dp", "row"), scatter_dimension=1, tiled=True),
    )
    return tuple(leading) + tuple(trailing)


def heads_of(rows_block):
    return rows_block.reshape(rows_block.shape[0], -1, HD)


def block_of(rows_all, start, block_rows):
    return heads_of(lax.dynamic_slice_in_dim(rows_all, start, block_rows, 0))


def block_scores(query_heads, key_heads, query_start, key_start, length):
    block_rows = query_heads.shape[0]
    scores = jnp.einsum(
        "qhd,khd->hqk", query_heads, key_heads, preferred_element_type=jnp.float32
    ) * HD ** (-0.5)
    query_pos = query_start + jnp.arange(block_rows, dtype=jnp.int32)
    key_pos = key_start + jnp.arange(key_heads.shape[0], dtype=jnp.int32)
    allowed = (key_pos[None, :] <= query_pos[:, None]) & (key_pos[None, :] < length)
    return jnp.where(allowed[None], scores, MASKED)


def key_block_count(row_place, length, block_rows):
    return jnp.minimum(row_place + 1, (length + block_rows - 1) // block_rows)


def attention_forward(queries, key_rows, value_rows, row_place, length):
    block_rows = queries.shape[0]
    query_heads = heads_of(queries)
    head_count = query_heads.shape[1]
    query_start = row_place * block_rows
    count = key_block_count(row_place, length, block_rows)

    def stats_step(block_index, carry):
        highest, partition = carry
        start = block_index * block_rows
        scores = block_scores(
            query_heads, block_of(key_rows, start, block_rows), query_start, start, length
        )
        newest = jnp.maximum(highest, jnp.max(scores, axis=-1, keepdims=True))
        partition = partition * jnp.exp(highest - newest) + jnp.sum(
            jnp.exp(scores - newest), axis=-1, keepdims=True
        )
        return (newest, partition)

    start_stats = (
        jnp.full((head_count, block_rows, 1), MASKED, jnp.float32),
        jnp.zeros((head_count, block_rows, 1), jnp.float32),
    )
    highest, partition = lax.fori_loop(0, count, stats_step, start_stats)

    def output_step(block_index, total):
        start = block_index * block_rows
        scores = block_scores(
            query_heads, block_of(key_rows, start, block_rows), query_start, start, length
        )
        weights_low = (jnp.exp(scores - highest) / partition).astype(jnp.bfloat16)
        return total + jnp.einsum(
            "hqk,khd->qhd",
            weights_low,
            block_of(value_rows, start, block_rows),
            preferred_element_type=jnp.float32,
        )

    total = lax.fori_loop(0, count, output_step, jnp.zeros(query_heads.shape, jnp.float32))
    return (total.reshape(block_rows, -1), highest, partition)


def attention_query_side(
    queries, key_rows, value_rows, grad_attended, highest, partition, row_place, length
):
    block_rows = queries.shape[0]
    seq_rows = key_rows.shape[0]
    query_heads = heads_of(queries)
    grad_heads = heads_of(grad_attended)
    head_count = query_heads.shape[1]
    query_start = row_place * block_rows
    count = key_block_count(row_place, length, block_rows)

    def inner_step(block_index, total):
        start = block_index * block_rows
        scores = block_scores(
            query_heads, block_of(key_rows, start, block_rows), query_start, start, length
        )
        weights = jnp.exp(scores - highest) / partition
        grad_weights = jnp.einsum(
            "qhd,khd->hqk",
            grad_heads,
            block_of(value_rows, start, block_rows),
            preferred_element_type=jnp.float32,
        )
        return total + jnp.sum(weights * grad_weights, axis=-1, keepdims=True)

    inner = lax.fori_loop(0, count, inner_step, jnp.zeros((head_count, block_rows, 1), jnp.float32))

    def grad_step(block_index, carry):
        start = block_index * block_rows
        key_heads = block_of(key_rows, start, block_rows)
        scores = block_scores(query_heads, key_heads, query_start, start, length)
        weights = jnp.exp(scores - highest) / partition
        grad_weights = jnp.einsum(
            "qhd,khd->hqk",
            grad_heads,
            block_of(value_rows, start, block_rows),
            preferred_element_type=jnp.float32,
        )
        grad_scores = (weights * (grad_weights - inner)).astype(jnp.bfloat16)
        query_total = carry[0] + jnp.einsum(
            "hqk,khd->qhd", grad_scores, key_heads, preferred_element_type=jnp.float32
        )
        weights_low = weights.astype(jnp.bfloat16)
        key_part = jnp.einsum(
            "hqk,qhd->khd", grad_scores, query_heads, preferred_element_type=jnp.float32
        )
        value_part = jnp.einsum(
            "hqk,qhd->khd", weights_low, grad_heads, preferred_element_type=jnp.float32
        )
        key_total = lax.dynamic_update_slice_in_dim(
            carry[1], lax.dynamic_slice_in_dim(carry[1], start, block_rows, 0) + key_part, start, 0
        )
        value_total = lax.dynamic_update_slice_in_dim(
            carry[2],
            lax.dynamic_slice_in_dim(carry[2], start, block_rows, 0) + value_part,
            start,
            0,
        )
        return (query_total, key_total, value_total)

    start_carry = (jnp.zeros(query_heads.shape, jnp.float32),)
    start_carry = start_carry + (
        jnp.zeros((seq_rows, head_count, HD), jnp.float32),
        jnp.zeros((seq_rows, head_count, HD), jnp.float32),
    )
    totals = lax.fori_loop(0, count, grad_step, start_carry)
    query_terms = totals[0].reshape(block_rows, -1) * HD ** (-0.5)
    return (
        query_terms,
        totals[1].reshape(seq_rows, -1) * HD ** (-0.5),
        totals[2].reshape(seq_rows, -1),
        inner,
    )


def local_general(
    tokens,
    lengths,
    first_gain,
    first_shift,
    w_query,
    w_key,
    w_value,
    bias_query,
    bias_value,
    w_output,
    bias_output,
    second_gain,
    second_shift,
    w_up,
    bias_up,
    w_down,
    bias_down,
    cotangent,
):
    micro_count, own_rows, width = tokens.shape
    col_count = lax.axis_size("col")
    group_rows = own_rows * col_count
    row_place = lax.axis_index("row")
    col_place = lax.axis_index("col")
    head_width = w_query.shape[1]
    hidden_width = w_up.shape[1]
    own_positions = (
        row_place * group_rows + col_place * own_rows + jnp.arange(own_rows, dtype=jnp.int32)
    )
    weight_totals = (
        jnp.zeros((width, head_width), jnp.float32),
        jnp.zeros((width, head_width), jnp.float32),
        jnp.zeros((width, head_width), jnp.float32),
        jnp.zeros((width, hidden_width), jnp.float32),
        jnp.zeros((head_width, width), jnp.float32),
        jnp.zeros((hidden_width, width), jnp.float32),
    )
    vector_totals = (
        jnp.zeros((width,), jnp.float32),
        jnp.zeros((width,), jnp.float32),
        jnp.zeros((head_width,), jnp.float32),
        jnp.zeros((head_width,), jnp.float32),
        jnp.zeros((width,), jnp.float32),
        jnp.zeros((width,), jnp.float32),
        jnp.zeros((width,), jnp.float32),
        jnp.zeros((hidden_width,), jnp.float32),
        jnp.zeros((width,), jnp.float32),
    )
    results = []
    input_grads = []
    for micro_index in range(micro_count):
        gathered = fetch_weights(w_query, w_key, w_value, w_up, w_output, w_down)
        query_full, key_full, value_full, up_full, output_full, down_full = gathered
        length = lengths[0, micro_index]
        inputs = tokens[micro_index].astype(jnp.float32)
        normed = layer_norm(inputs, first_gain, first_shift).astype(jnp.bfloat16)
        normed_all = spread_rows(normed)
        queries = (product(normed_all, query_full) + bias_query).astype(jnp.bfloat16)
        keys_local = product(normed_all, key_full).astype(jnp.bfloat16)
        values_local = (product(normed_all, value_full) + bias_value).astype(jnp.bfloat16)
        keys_all, values_all = (
            lax.all_gather(keys_local, "row", axis=0, tiled=True),
            lax.all_gather(values_local, "row", axis=0, tiled=True),
        )
        attended, maxima, partitions = attention_forward(
            queries, keys_all, values_all, row_place, length
        )
        attended_low = attended.astype(jnp.bfloat16)
        branch = fold_rows(product(attended_low, output_full)) + bias_output
        middle = inputs + branch
        second_normed = layer_norm(middle, second_gain, second_shift).astype(jnp.bfloat16)
        second_all = spread_rows(second_normed)
        pre_activation = product(second_all, up_full) + bias_up
        activated = gelu_tanh(pre_activation).astype(jnp.bfloat16)
        result = middle + (fold_rows(product(activated, down_full)) + bias_down)
        results.append(result.astype(jnp.bfloat16))
        query_full, key_full, value_full, up_full, output_full, down_full = fetch_weights(
            w_query, w_key, w_value, w_up, w_output, w_down
        )
        validity = (own_positions < length).astype(jnp.float32)
        grad_result = cotangent[micro_index].astype(jnp.float32) * validity[:, None]
        grad_result_all = spread_rows(grad_result.astype(jnp.bfloat16))
        grad_down = transposed_left(activated, grad_result_all)
        grad_activated = transposed_right(grad_result_all, down_full)
        gelu_back = jax.vjp(gelu_tanh, pre_activation)[1]
        grad_pre = gelu_back(grad_activated)[0].astype(jnp.bfloat16)
        grad_up = transposed_left(second_all, grad_pre)
        grad_second_normed = fold_rows(transposed_right(grad_pre, up_full))
        second_back = jax.vjp(layer_norm, middle, second_gain, second_shift)[1]
        grad_middle_norm, grad_second_gain, grad_second_shift = second_back(grad_second_normed)
        grad_middle = grad_result + grad_middle_norm
        grad_branch = grad_middle.astype(jnp.bfloat16)
        grad_branch_all = spread_rows(grad_branch)
        grad_output = transposed_left(attended_low, grad_branch_all)
        grad_attended = transposed_right(grad_branch_all, output_full).astype(jnp.bfloat16)
        query_terms, key_terms, value_terms, inner = attention_query_side(
            queries, keys_all, values_all, grad_attended, maxima, partitions, row_place, length
        )
        key_sums, value_sums = (
            lax.psum_scatter(key_terms, "row", scatter_dimension=0, tiled=True),
            lax.psum_scatter(value_terms, "row", scatter_dimension=0, tiled=True),
        )
        grad_queries = query_terms.astype(jnp.bfloat16)
        grad_keys = key_sums.astype(jnp.bfloat16)
        grad_values = value_sums.astype(jnp.bfloat16)
        grad_query = transposed_left(normed_all, grad_queries)
        grad_key = transposed_left(normed_all, grad_keys)
        grad_value = transposed_left(normed_all, grad_values)
        grad_normed = fold_rows(
            transposed_right(grad_queries, query_full)
            + transposed_right(grad_keys, key_full)
            + transposed_right(grad_values, value_full)
        )
        first_back = jax.vjp(layer_norm, inputs, first_gain, first_shift)[1]
        grad_inputs_norm, grad_first_gain, grad_first_shift = first_back(grad_normed)
        input_grads.append((grad_middle + grad_inputs_norm).astype(jnp.bfloat16))
        local_grads = (grad_query, grad_key, grad_value, grad_up, grad_output, grad_down)
        weight_totals = tuple(
            (former + latter for former, latter in zip(weight_totals, local_grads))
        )
        local_vectors = (
            grad_first_gain,
            grad_first_shift,
            jnp.sum(grad_queries.astype(jnp.float32), axis=0),
            jnp.sum(grad_values.astype(jnp.float32), axis=0),
            jnp.sum(grad_branch.astype(jnp.float32), axis=0),
            grad_second_gain,
            grad_second_shift,
            jnp.sum(grad_pre.astype(jnp.float32), axis=0),
            jnp.sum(grad_result, axis=0),
        )
        vector_totals = tuple(
            (former + latter for former, latter in zip(vector_totals, local_vectors))
        )
    weight_totals = reduce_blocks(weight_totals)

    def widen(vector_part):
        blank = jnp.zeros((vector_part.shape[0] * col_count,), jnp.float32)
        return lax.dynamic_update_slice(blank, vector_part, (col_place * vector_part.shape[0],))

    def narrow(whole_vector, piece_width):
        return lax.dynamic_slice_in_dim(whole_vector, col_place * piece_width, piece_width)

    (
        sum_first_gain,
        sum_first_shift,
        sum_bias_query,
        sum_bias_value,
        sum_bias_output,
        sum_second_gain,
        sum_second_shift,
        sum_bias_up,
        sum_bias_down,
    ) = lax.psum(
        (
            vector_totals[0],
            vector_totals[1],
            widen(vector_totals[2]),
            widen(vector_totals[3]),
            vector_totals[4],
            vector_totals[5],
            vector_totals[6],
            widen(vector_totals[7]),
            vector_totals[8],
        ),
        ("dp", "row", "col"),
    )
    grad_w_query, grad_w_key, grad_w_value, grad_w_up, grad_w_output, grad_w_down = weight_totals
    return (
        jnp.stack(results, axis=0),
        jnp.stack(input_grads, axis=0),
        sum_first_gain,
        sum_first_shift,
        grad_w_query,
        grad_w_key,
        grad_w_value,
        narrow(sum_bias_query, head_width),
        narrow(sum_bias_value, head_width),
        grad_w_output,
        sum_bias_output,
        sum_second_gain,
        sum_second_shift,
        grad_w_up,
        narrow(sum_bias_up, hidden_width),
        grad_w_down,
        sum_bias_down,
    )


F32 = jnp.float32
LOW = jnp.bfloat16
VMEM_LIMIT = 56 * 1024 * 1024


def fits(mesh):
    return mesh.shape["row"] == 4 and mesh.shape["col"] == 4 and mesh.shape["dp"] == 2


def contract(former, latter, former_dim, latter_dim):
    return lax.dot_general(
        former,
        latter,
        (((former_dim,), (latter_dim,)), ((), ())),
        preferred_element_type=jnp.float32,
    )


def norm_parts(values):
    centered = values - jnp.mean(values, axis=-1, keepdims=True)
    scale = lax.rsqrt(jnp.mean(centered * centered, axis=-1, keepdims=True) + EPSILON)
    return centered * scale, scale


def norm_back(grads, gain, unit, scale):
    inner = grads * gain
    mean_inner = jnp.mean(inner, axis=-1, keepdims=True)
    mean_unit = jnp.mean(inner * unit, axis=-1, keepdims=True)
    return scale * (inner - mean_inner - unit * mean_unit)


GELU_SCALE = 0.7978845608028654
GELU_CUBE = 0.044715


def gelu_parts(values):
    square = values * values
    curve = jnp.tanh(GELU_SCALE * values * (1.0 + GELU_CUBE * square))
    half = 0.5 + 0.5 * curve
    slope = half + 0.5 * values * (1.0 - curve * curve) * (GELU_SCALE * (1.0 + 3.0 * GELU_CUBE * square))
    return values * half, slope


def peers():
    place = lax.axis_index("col")
    return {"col": place + 1 - 2 * (place % 2)}, {"col": (place + 2) % 4}


def remote(source, target, send_sem, recv_sem, device):
    return pltpu.make_async_remote_copy(
        src_ref=source,
        dst_ref=target,
        send_sem=send_sem,
        recv_sem=recv_sem,
        device_id=device,
        device_id_type=pl.DeviceIdType.MESH,
    )


def row_peers():
    row = lax.axis_index("row")
    return row + 1 - 2 * (row % 2), (row + 2) % 4, 3 - row


def greet_all(core, far):
    row = lax.axis_index("row")
    cross = {"dp": 1 - lax.axis_index("dp")}
    barrier = pltpu.get_barrier_semaphore()
    rows = [{"row": (row + step) % 4} for step in (1, 2, 3)]
    for device in [core, far, cross] + rows:
        pl.semaphore_signal(barrier, inc=1, device_id=device, device_id_type=pl.DeviceIdType.MESH)
    pl.semaphore_wait(barrier, 6)


class Gather:
    def __init__(self, slot, z_send, z_recv, x_send, x_recv):
        self.slot, self.z_send, self.z_recv, self.x_send, self.x_recv = slot, z_send, z_recv, x_send, x_recv
        self.row, self.dp = lax.axis_index("row"), lax.axis_index("dp")

    def lane(self, d):
        if d == 0:
            return self.row, {"row": jnp.minimum(self.row + 1, 3)}
        return 3 - self.row, {"row": jnp.maximum(self.row - 1, 0)}

    def z_copy(self, d, k, block):
        view = self.slot(self.dp * 4 + block)
        return remote(view, view, self.z_send.at[d, k], self.z_recv.at[d, k], self.lane(d)[1])

    def x_copy(self, block):
        view = self.slot(self.dp * 4 + block)
        return remote(view, view, self.x_send.at[block], self.x_recv.at[block], {"dp": 1 - self.dp})

    def pump(self, k):
        for d in range(2):
            place, _ = self.lane(d)
            block = self.row - k if d == 0 else self.row + k
            if k == 0:
                if d == 0:
                    self.x_copy(block).start()

                @pl.when(place <= 2)
                def _():
                    self.z_copy(d, 0, block).start()
            else:

                @pl.when(place >= k)
                def _():
                    self.z_copy(d, k - 1, block).wait_recv()
                    if k < 3:

                        @pl.when(place <= 2)
                        def _():
                            self.z_copy(d, k, block).start()

                    self.x_copy(block).start()

    def arrive(self):
        for block in range(4):
            view = self.slot((1 - self.dp) * 4 + block)
            remote(view, view, self.x_send.at[block], self.x_recv.at[block], {"dp": 1 - self.dp}).wait_recv()

    def sent(self):
        for block in range(4):
            self.x_copy(block).wait_send()
        for d in range(2):
            place, _ = self.lane(d)
            for k in range(3):

                @pl.when((place >= k) & (place <= 2))
                def _():
                    self.z_copy(d, k, self.row - k if d == 0 else self.row + k).wait_send()


class Spread:
    def __init__(self, source, target, trade_send, trade_recv, send, recv):
        self.source, self.target = source, target
        self.trade_send, self.trade_recv, self.send, self.recv = trade_send, trade_recv, send, recv
        self.core, self.far = peers()
        self.row = lax.axis_index("row")

    def trade_copy(self, place):
        return remote(
            self.source.at[place],
            self.target.at[self.row, 0],
            self.trade_send.at[place],
            self.trade_recv.at[self.row],
            {"row": place},
        )

    def trade(self):
        for place in row_peers():
            self.trade_copy(place).start()

    def traded(self):
        for place in row_peers():
            self.trade_copy(place).wait_send()

    def hop(self, step, r):
        source, target, device = ((0, 1, self.core), (0, 2, self.far), (2, 3, self.core))[step]
        return remote(
            self.target.at[r, source], self.target.at[r, target], self.send.at[step, r], self.recv.at[step, r], device
        )

    def arrive(self, r):
        remote(
            self.source.at[r], self.target.at[r, 0], self.trade_send.at[r], self.trade_recv.at[r], {"row": r}
        ).wait_recv()

    def first(self, r):
        self.hop(1, r).start()
        self.hop(0, r).start()

    def relay(self, r):
        self.hop(1, r).wait()
        self.hop(2, r).start()

    def done(self, r):
        self.hop(0, r).wait()
        self.hop(2, r).wait()


class Reduce:
    def __init__(self, grads, sums, moving, x_send, x_recv, z_send, z_recv):
        self.grads, self.sums, self.moving = grads, sums, moving
        self.x_send, self.x_recv, self.z_send, self.z_recv = x_send, x_recv, z_send, z_recv
        self.row, self.dp = lax.axis_index("row"), lax.axis_index("dp")

    def x_copy(self):
        half = self.grads.at[pl.ds((1 - self.dp) * 4, 4)]
        return remote(half, self.sums, self.x_send, self.x_recv, {"dp": 1 - self.dp})

    def start(self):
        self.x_copy().start()

    def add(self):
        self.x_copy().wait()
        for b in range(4):
            self.sums[b] = (self.sums[b].astype(F32) + self.grads[self.dp * 4 + b].astype(F32)).astype(LOW)

    def lane(self, d):
        if d == 0:
            return self.row, {"row": jnp.minimum(self.row + 1, 3)}
        return 3 - self.row, {"row": jnp.maximum(self.row - 1, 0)}

    def z_copy(self, d, k, source):
        return remote(source, self.moving.at[d, k], self.z_send.at[d, k], self.z_recv.at[d, k], self.lane(d)[1])

    def pump(self, k):
        for d in range(2):
            place, _ = self.lane(d)

            @pl.when(place == 0)
            def _():
                self.z_copy(d, k, self.sums.at[3 - k if d == 0 else k]).start()

            if k >= 1:

                @pl.when((place >= 1) & (place <= k))
                def _():
                    block = 3 - k + place if d == 0 else k - place
                    self.z_copy(d, k - 1, self.sums.at[0]).wait_recv()
                    self.moving[d, k - 1] = (
                        self.moving[d, k - 1].astype(F32) + self.sums[block].astype(F32)
                    ).astype(LOW)
                    self.z_copy(d, k, self.moving.at[d, k - 1]).start()

    def finish(self, out):
        out[...] = self.sums[self.row].astype(F32)
        for d in range(2):
            place, _ = self.lane(d)

            @pl.when(place >= 1)
            def _():
                self.z_copy(d, 2, self.sums.at[0]).wait_recv()
                out[...] += self.moving[d, 2].astype(F32)

            for k in range(3):

                @pl.when(place <= k)
                def _():
                    self.z_copy(d, k, self.sums.at[0]).wait_send()


def positions_row(shape, place):
    own = shape // 4
    lane = lax.broadcasted_iota(jnp.int32, (1, own), 1)
    places = (place, place + 1 - 2 * (place % 2), (place + 2) % 4, 3 - place)
    return jnp.concatenate([lane + other * own for other in places], axis=1)


def positions_column(shape, place):
    own = shape // 4
    line = lax.broadcasted_iota(jnp.int32, (own, 1), 0)
    places = (place, place + 1 - 2 * (place % 2), (place + 2) % 4, 3 - place)
    return jnp.concatenate([line + other * own for other in places], axis=0)


def feed_kernel(
    lengths_ref,
    tokens_ref,
    cot_ref,
    wq_ref,
    wk_ref,
    wv_ref,
    wo_shard,
    wu_shard,
    wd_shard,
    vec_ref,
    bias_up_ref,
    bias_q_ref,
    bias_v_ref,
    q_ref,
    k_ref,
    v_ref,
    tok_ref,
    proj_out,
    att_ref,
    lse_ref,
    middle,
    far_out_q,
    gatt_ref,
    gout_ref,
    x_down,
    sums_ref,
    sum_up_ref,
    normed_out,
    gmid_ref,
    gup_ref,
    wo_ref,
    wu_all,
    wd_ref,
    g_all,
    kept,
    kept_q,
    core_out,
    core_in,
    core_in_q,
    far_out,
    far_in,
    second,
    act,
    gpre,
    branch,
    key_bias,
    causal,
    gdown,
    stage_sems,
    send_sems,
    recv_sems,
    trade_send,
    trade_recv,
    row_send,
    row_recv,
    grad_send,
    grad_recv,
    g_send,
    g_recv,
    za_send,
    za_recv,
    xa_send,
    xa_recv,
    zo_send,
    zo_recv,
    xo_send,
    xo_recv,
    zu_send,
    zu_recv,
    xu_send,
    xu_recv,
    zd_send,
    zd_recv,
    xd_send,
    xd_recv,
    rx_send,
    rx_recv,
    out_sems,
    load_sems,
):
    chunks, blocks, own, width = second.shape
    rows = blocks * own
    hidden = wu_all.shape[2]
    core, far = peers()
    row = lax.axis_index("row")
    mine = lax.axis_index("dp") * 4 + row
    wu_ref = wu_all.reshape(width, hidden)

    def wd_slot(block):
        return wd_ref.at[:, pl.ds(pl.multiple_of(block * own, own), own)]

    down = Gather(wd_slot, zd_send, zd_recv, xd_send, xd_recv)
    near, halfway, distant = row_peers()
    head_width = wq_ref.shape[1]
    rows_all = branch
    normed = gpre.reshape(chunks * rows, width)

    def wo_slot(block):
        return wo_ref.at[:, pl.ds(pl.multiple_of(block * own, own), own)]

    up = Gather(lambda block: wu_all.at[block], zu_send, zu_recv, xu_send, xu_recv)
    output = Gather(wo_slot, zo_send, zo_recv, xo_send, xo_recv)
    spread = Spread(tokens_ref, rows_all, trade_send, trade_recv, row_send, row_recv)
    cots = Spread(cot_ref, g_all, grad_send, grad_recv, g_send, g_recv)
    projs = [
        Gather(
            lambda block, n=n: proj_out.at[block, :, n * head_width : (n + 1) * head_width],
            za_send.at[n],
            za_recv.at[n],
            xa_send.at[n],
            xa_recv.at[n],
        )
        for n in range(3)
    ]
    loads = [
        pltpu.make_async_copy(source, target, load_sems.at[n])
        for n, (source, target) in enumerate(
            (
                (wq_ref, projs[0].slot(mine)),
                (wk_ref, projs[1].slot(mine)),
                (wv_ref, projs[2].slot(mine)),
                (tokens_ref.at[row], rows_all.at[row, 0]),
                (cot_ref.at[row], g_all.at[row, 0]),
                (wo_shard, wo_slot(mine)),
                (wu_shard, wu_all.at[mine]),
                (wd_shard, wd_slot(mine)),
            )
        )
    ]
    for load in loads:
        load.start()
    reduces = [
        Reduce(gdown.at[h], x_down.at[h], None, rx_send.at[h], rx_recv.at[h], None, None)
        for h in range(2)
    ]
    place = lax.axis_index("col")
    length = lengths_ref[0, row]
    key_row, query_column = positions_row(rows, place), positions_column(rows, place)
    causal[...] = jnp.where(key_row <= query_column, 0.0, MASKED).astype(LOW)
    for r in range(chunks):
        key_bias[:, r * rows : (r + 1) * rows] = jnp.where(key_row + r * rows < length, 0.0, MASKED)

    def core_copy(step, r, source, target):
        return remote(source.at[r], target.at[r], send_sems.at[step, r], recv_sems.at[step, r], core)

    def far_copy(step, r, source, target):
        return remote(source.at[r], target.at[r], send_sems.at[step, r], recv_sems.at[step, r], far)

    def spread_core(step, r, rows_ref):
        return remote(rows_ref.at[r, 0], rows_ref.at[r, 1], send_sems.at[step, r], recv_sems.at[step, r], core)

    def spread_far(step, r, rows_ref):
        return remote(rows_ref.at[r, 0], rows_ref.at[r, 2], send_sems.at[step, r], recv_sems.at[step, r], far)

    def spread_relay(step, r, rows_ref):
        return remote(rows_ref.at[r, 2], rows_ref.at[r, 3], send_sems.at[step, r], recv_sems.at[step, r], core)

    def split(r, total, kept_ref, out_ref):
        kept_ref[r, 0] = total[:own].astype(kept_ref.dtype)
        out_ref[r, 0] = total[own : 2 * own].astype(LOW)
        kept_ref[r, 1] = total[2 * own : 3 * own].astype(kept_ref.dtype)
        out_ref[r, 1] = total[3 * own :].astype(LOW)

    def fold(r, kept_ref, in_ref, out_ref):
        out_ref[r] = (kept_ref[r, 1].astype(F32) + in_ref[r, 1].astype(F32)).astype(LOW)
        kept_ref[r, 0] = (kept_ref[r, 0].astype(F32) + in_ref[r, 0].astype(F32)).astype(kept_ref.dtype)

    def each(body):
        lax.fori_loop(0, chunks, lambda r, carry: (body(r), carry)[1], 0)

    def out_projection(r):
        split(r, contract(att_ref[r * rows : (r + 1) * rows], wo_ref[...], 1, 0), kept, core_out)
        core_copy(0, r, core_out, core_in).start()

    def out_fold(r):
        core_copy(0, r, core_out, core_in).wait()
        fold(r, kept, core_in, far_out)
        far_copy(1, r, far_out, far_in).start()

    block = 256
    lane = lax.broadcasted_iota(jnp.int32, (block, 128), 1)

    def attention(r):
        long = (r + 1) * rows

        def part(step, carry):
            here = pl.ds(pl.multiple_of(r * rows + (step % 2) * block, block), block)
            pair = pl.ds(pl.multiple_of((step // 2) * 128, 128), 128)
            inside = pl.ds(pl.multiple_of((step % 2) * block, block), block)
            queries = q_ref[here, pair]
            parts = []
            for head in range(2):
                masked = jnp.where((lane // HD) == head, queries, 0) * jnp.asarray(HD**-0.5, LOW)
                scores = contract(masked, k_ref[:long, pair], 1, 1) + key_bias[:, :long]
                last = scores[:, long - rows :] + causal[inside].astype(F32)
                scores = last if r == 0 else jnp.concatenate([scores[:, : long - rows], last], axis=1)
                highest = jnp.max(scores, axis=1, keepdims=True)
                weights = jnp.exp(scores - highest)
                total = jnp.sum(weights, axis=1, keepdims=True)
                parts.append(contract(weights.astype(LOW), v_ref[:long, pair], 1, 0) / total)
                flat = jnp.broadcast_to(highest + jnp.log(total), (block, 128))
                lse_ref[step // 2, r, head : head + 1, inside] = flat.T[:1]
            att_ref[here, pair] = jnp.where(lane < HD, parts[0], parts[1]).astype(LOW)
            return carry

        lax.fori_loop(0, 4, part, 0)

    def norm(r):
        far_copy(1, r, far_out, far_in).wait()
        values = tok_ref[r].astype(F32) + (kept[r, 0] + far_in[r].astype(F32) + vec_ref[0:1])
        middle[r] = values
        second[r, 0] = (norm_parts(values)[0] * vec_ref[1:2] + vec_ref[2:3]).astype(LOW)
        spread_core(2, r, second).start()
        spread_far(3, r, second).start()

    def norm(r):
        far_copy(1, r, far_out, far_in).wait()
        values = tok_ref[r].astype(F32) + (kept[r, 0] + far_in[r].astype(F32) + vec_ref[0:1])
        middle[r] = values
        second[r, 0] = (norm_parts(values)[0] * vec_ref[1:2] + vec_ref[2:3]).astype(LOW)
        spread_core(2, r, second).start()
        spread_far(3, r, second).start()

    def pump(step):
        for proj in projs:
            proj.pump(step)

    def give_cot(r):
        line = lax.broadcasted_iota(jnp.int32, (own, width), 0) + (r * rows + place * own)
        g_all[r, 0] = jnp.where(line < length, g_all[r, 0], jnp.zeros((), LOW))
        cots.first(r)

    def norm_rows(r):
        spread.done(r)
        here = pl.ds(pl.multiple_of(r * rows, rows), rows)
        values = rows_all[r].reshape(rows, width).astype(F32)
        low = (norm_parts(values)[0] * vec_ref[4:5] + vec_ref[5:6]).astype(LOW)
        gpre[r] = low.reshape(blocks, own, width)
        pltpu.make_async_copy(normed.at[here], normed_out.at[here], out_sems.at[r]).start()
        tok_ref[r] = rows_all[r, 0]

    def project(r):
        here = pl.ds(pl.multiple_of(r * rows, rows), rows)
        total = contract(normed[here], proj_out.reshape(8 * own, 3 * head_width)[...], 1, 0)
        q_ref[here] = (total[:, :head_width] + bias_q_ref[...]).astype(LOW)
        k_ref[here] = total[:, head_width : 2 * head_width].astype(LOW)
        v_ref[here] = (total[:, 2 * head_width :] + bias_v_ref[...]).astype(LOW)

    greet_all(core, far)
    for load in loads[:3]:
        load.wait()
    pump(0)
    spread.trade()
    loads[3].wait()
    spread.first(row)
    loads[4].wait()
    give_cot(row)
    for load in loads[5:]:
        load.wait()
    spread.arrive(near)
    spread.first(near)
    pump(1)
    spread.relay(row)
    cots.relay(row)
    norm_rows(row)
    spread.arrive(halfway)
    spread.first(halfway)
    spread.relay(near)
    spread.arrive(distant)
    spread.first(distant)
    output.pump(0)
    cots.trade()
    norm_rows(near)
    pump(2)
    spread.relay(halfway)
    norm_rows(halfway)
    spread.relay(distant)
    pump(3)
    output.pump(1)
    norm_rows(distant)
    for proj in projs:
        proj.arrive()
    each(project)
    up.pump(0)
    down.pump(0)
    output.pump(2)
    attention(0)
    output.pump(3)
    cots.arrive(near)
    give_cot(near)
    attention(1)
    output.arrive()
    out_projection(0)
    out_projection(1)
    out_fold(0)
    cots.relay(near)
    attention(2)
    out_projection(2)
    out_fold(1)
    norm(0)
    up.pump(1)
    down.pump(1)
    cots.arrive(halfway)
    give_cot(halfway)
    attention(3)
    out_projection(3)
    out_fold(2)
    norm(1)
    out_fold(3)
    cots.arrive(distant)
    give_cot(distant)
    up.pump(2)
    norm(2)
    cots.relay(halfway)
    down.pump(2)
    up.pump(3)
    down.pump(3)
    cots.relay(distant)
    for r in range(chunks):
        here = slice(r * rows, (r + 1) * rows)
        pltpu.make_async_copy(normed.at[here], normed_out.at[here], out_sems.at[r]).wait()
    up.arrive()
    down.arrive()

    sum_up_ref[...] = jnp.zeros_like(sum_up_ref)

    def relay_start(r):
        spread_far(3, r, second).wait()
        spread_relay(4, r, second).start()

    def feed(r):
        spread_core(2, r, second).wait()
        spread_relay(4, r, second).wait()
        cots.done(r)
        pre = contract(second[r].reshape(rows, width), wu_ref[...], 1, 0) + bias_up_ref[...]
        activated, slope = gelu_parts(pre)
        act[r] = activated.astype(LOW).reshape(blocks, own, hidden)
        grads = contract(g_all[r].reshape(rows, width), wd_ref[...], 1, 1) * slope
        grads_low = grads.astype(LOW)
        gpre[r] = grads_low.reshape(blocks, own, hidden)
        sum_up_ref[...] += jnp.sum(grads_low.astype(F32), axis=0, keepdims=True)
        split(r, contract(grads_low, wu_ref[...], 1, 1), kept, core_out)
        core_copy(5, r, core_out, core_in).start()
        total = contract(act[r].reshape(rows, hidden), wd_ref[...], 1, 0)
        core_copy(5, r, core_out, core_in).wait()
        fold(r, kept, core_in, far_out)
        far_copy(6, r, far_out, far_in).start()
        kept_q[r] = total[:own].astype(LOW)
        core_out[r, 0] = total[own : 2 * own].astype(LOW)
        far_out_q[r] = total[2 * own : 3 * own].astype(LOW)
        core_out[r, 1] = total[3 * own :].astype(LOW)
        core_copy(7, r, core_out, core_in_q).start()

    wide = 256
    flat_second = second.reshape(chunks * rows, width)
    flat_act = act.reshape(chunks * rows, hidden)
    flat_gpre = gpre.reshape(chunks * rows, hidden)
    flat_g = g_all.reshape(chunks * rows, width)
    flat_branch = branch.reshape(chunks * rows, width)

    def some(first, last, body):
        lax.fori_loop(first, last, lambda t, carry: (body(t), carry)[1], 0)

    def down_grad(t):
        part = pl.ds(pl.multiple_of(t * wide, wide), wide)
        here = pl.ds(pl.multiple_of((t % 2) * wide, wide), wide)
        total = contract(flat_act[:, part], flat_g[...], 0, 0).astype(LOW)
        for b in range(8):
            gdown[t // 2, b, here] = total[:, b * own : (b + 1) * own]

    sums_ref[...] = jnp.zeros_like(sums_ref)

    def norm_grad(r):
        far_copy(6, r, far_out, far_in).wait()
        grads = kept[r, 0] + far_in[r].astype(F32)
        unit, scale = norm_parts(middle[r])
        own_grads = g_all[r, 0].astype(F32)
        total = own_grads + norm_back(grads, vec_ref[1:2], unit, scale)
        low = total.astype(LOW)
        branch[r, 0] = low
        spread_core(9, r, branch).start()
        spread_far(10, r, branch).start()
        sums_ref[0:1] += jnp.sum(low.astype(F32), axis=0, keepdims=True)
        sums_ref[1:2] += jnp.sum(grads * unit, axis=0, keepdims=True)
        sums_ref[2:3] += jnp.sum(grads, axis=0, keepdims=True)
        sums_ref[3:4] += jnp.sum(own_grads, axis=0, keepdims=True)

    relay_start(0)
    feed(0)
    norm(3)
    relay_start(1)

    def step(r):
        feed(r)
        norm_grad(r - 1)

        @pl.when(r < chunks - 1)
        def _():
            relay_start(r + 1)

    some(1, chunks, step)
    some(0, 2, down_grad)
    reduces[0].start()
    some(2, 4, down_grad)
    reduces[1].start()
    norm_grad(chunks - 1)
    given = pltpu.make_async_copy(branch.at[:, 0], gmid_ref, stage_sems.at[0])
    given.start()

    def result_fold(r):
        core_copy(7, r, core_out, core_in_q).wait()
        far_out_q[r] = (far_out_q[r].astype(F32) + core_in_q[r, 1].astype(F32)).astype(LOW)
        own_part = kept_q[r].astype(F32) + core_in_q[r, 0].astype(F32)
        middle[r] = middle[r] + (own_part + vec_ref[3:4])

    each(result_fold)

    def late(r):
        spread_far(10, r, branch).wait()
        spread_relay(11, r, branch).start()
        part = pl.ds(pl.multiple_of(r * wide, wide), wide)
        total = contract(flat_second[:, part], flat_gpre[...], 0, 0).astype(LOW)
        for b in range(2):
            core_out[0, b] = total[b * own : (b + 1) * own]
        copy = pltpu.make_async_copy(core_out.at[0], gup_ref.at[pl.ds(2 * r, 2)], stage_sems.at[1])
        copy.start()
        spread_core(9, r, branch).wait()
        spread_relay(11, r, branch).wait()
        rows_here = pl.ds(pl.multiple_of(r * rows, rows), rows)
        gatt_ref[rows_here] = contract(branch[r].reshape(rows, width), wo_ref[...], 1, 1).astype(LOW)
        copy.wait()

    some(0, 4, late)
    total_out = contract(att_ref[...], flat_branch[...], 0, 0).astype(LOW)
    for b in range(8):
        gout_ref[b] = total_out[:, b * own : (b + 1) * own]
    for h in range(2):
        reduces[h].add()
    given.wait()
    spread.traded()
    cots.traded()
    for gather in projs + [output, up, down]:
        gather.sent()


def feed_block(
    lengths, tokens, cotangent, w_query, w_key, w_value, w_output, w_up, w_down, vectors, bias_up, bias_query, bias_value
):
    chunks, own, width = tokens.shape
    rows = chunks * 4 * own
    head_width = w_query.shape[1]
    hidden = w_up.shape[1]
    half = (chunks, 2, own, width)
    one = (chunks, own, width)
    all_rows = (chunks, 4, own, width)
    vmem = pl.BlockSpec(memory_space=pltpu.VMEM)
    hbm = pl.BlockSpec(memory_space=pl.ANY)
    dma = pltpu.SemaphoreType.DMA
    gather_sems = [dma((2, 3)), dma((2, 3)), dma((4,)), dma((4,))]
    spread_sems = [dma((4,)), dma((4,)), dma((3, 4)), dma((3, 4))]
    return pl.pallas_call(
        feed_kernel,
        in_specs=[pl.BlockSpec(memory_space=pltpu.SMEM)] + [hbm] * 8 + [vmem] * 4,
        out_specs=[vmem] * 14 + [hbm] * 3,
        out_shape=[
            jax.ShapeDtypeStruct((rows, head_width), LOW),
            jax.ShapeDtypeStruct((rows, head_width), LOW),
            jax.ShapeDtypeStruct((rows, head_width), LOW),
            jax.ShapeDtypeStruct(one, LOW),
            jax.ShapeDtypeStruct((8, own, 3 * head_width), LOW),
            jax.ShapeDtypeStruct((rows, head_width), LOW),
            jax.ShapeDtypeStruct((head_width // 128, chunks, 2, rows // chunks), F32),
            jax.ShapeDtypeStruct(one, F32),
            jax.ShapeDtypeStruct(one, LOW),
            jax.ShapeDtypeStruct((rows, head_width), LOW),
            jax.ShapeDtypeStruct((8, head_width, width // 8), LOW),
            jax.ShapeDtypeStruct((2, 4, hidden // 2, width // 8), LOW),
            jax.ShapeDtypeStruct((8, width), F32),
            jax.ShapeDtypeStruct((1, hidden), F32),
            jax.ShapeDtypeStruct((rows, width), LOW),
            jax.ShapeDtypeStruct(one, LOW),
            jax.ShapeDtypeStruct((8, width // 8, hidden), LOW),
        ],
        scratch_shapes=[
            pltpu.VMEM((head_width, width), LOW),
            pltpu.VMEM((8, own, hidden), LOW),
            pltpu.VMEM((hidden, width), LOW),
            pltpu.VMEM(all_rows, LOW),
            pltpu.VMEM(half, F32),
            pltpu.VMEM(one, LOW),
            pltpu.VMEM(half, LOW),
            pltpu.VMEM(half, LOW),
            pltpu.VMEM(half, LOW),
            pltpu.VMEM(one, LOW),
            pltpu.VMEM(one, LOW),
            pltpu.VMEM(all_rows, LOW),
            pltpu.VMEM((chunks, 4, own, hidden), LOW),
            pltpu.VMEM((chunks, 4, own, hidden), LOW),
            pltpu.VMEM(all_rows, LOW),
            pltpu.VMEM((1, rows), F32),
            pltpu.VMEM((rows // chunks, rows // chunks), LOW),
            pltpu.VMEM((2, 8, hidden // 2, width // 8), LOW),
            dma((2,)),
            dma((12, chunks)),
            dma((12, chunks)),
        ]
        + spread_sems
        + spread_sems
        + [dma((3, 2, 3)), dma((3, 2, 3)), dma((3, 4)), dma((3, 4))]
        + gather_sems
        + gather_sems
        + gather_sems
        + [dma((2,)), dma((2,)), dma((4,)), dma((8,))],
        compiler_params=pltpu.CompilerParams(
            collective_id=1, has_side_effects=True, vmem_limit_bytes=62 * 1024 * 1024
        ),
        cost_estimate=pl.CostEstimate(flops=100_000_000_000, bytes_accessed=30_000_000, transcendentals=0),
        name="feed_block",
    )(lengths, tokens, cotangent, w_query, w_key, w_value, w_output, w_up, w_down, vectors, bias_up, bias_query, bias_value)


def back_kernel(
    q_ref,
    k_ref,
    v_ref,
    do_ref,
    o_ref,
    lse_ref,
    lengths_ref,
    w_ref,
    tok_ref,
    gmid_ref,
    base_ref,
    far_q_ref,
    sum_down_ref,
    gup_ref,
    gout_ref,
    gain_ref,
    sums_ref,
    sum_up_ref,
    normed_ref,
    res_out,
    gtok_out,
    down_out,
    up_out,
    out_out,
    query_out,
    key_out,
    value_out,
    shared_out,
    by_col_out,
    dk_sum,
    dv_sum,
    dproj,
    gproj,
    kept,
    core_out,
    core_in,
    far_out,
    far_in,
    gtok,
    norm_tile,
    key_bias,
    causal,
    far_q_in,
    result,
    x_up,
    x_out,
    x_proj,
    z_down,
    z_up,
    z_out,
    z_proj,
    proj_sum,
    vec,
    vec_in,
    q_send,
    q_recv,
    res_send,
    res_recv,
    tok_send,
    tok_recv,
    fold_send,
    fold_recv,
    x_send,
    x_recv,
    z_send,
    z_recv,
    d_send,
    d_recv,
    vec_send,
    vec_recv,
    tile_sem,
):
    chunks, own, width = tok_ref.shape
    rows = 4 * own
    head_width = q_ref.shape[1]
    core, far = peers()
    row = lax.axis_index("row")
    dp = lax.axis_index("dp")
    cross = {"dp": 1 - dp}
    other = lambda r: {"row": r}
    quarters = own // 2

    def reduce_of(n, grads, sums, moving):
        return Reduce(grads, sums, moving, x_send.at[n], x_recv.at[n], z_send.at[n], z_recv.at[n])

    ups = [
        reduce_of(h, gup_ref.at[:, h * quarters : (h + 1) * quarters], x_up.at[h], z_up.at[h]) for h in range(2)
    ]
    outs = reduce_of(2, gout_ref, x_out, z_out)
    projs = [
        reduce_of(3 + h, gproj.at[:, h * quarters : (h + 1) * quarters], x_proj.at[h], z_proj.at[h]) for h in range(2)
    ]
    downs = [
        Reduce(None, sum_down_ref.at[h], z_down.at[h], None, None, d_send.at[h], d_recv.at[h]) for h in range(2)
    ]
    place = lax.axis_index("col")
    length = lengths_ref[0, row]
    query_row, key_column = positions_row(rows, place), positions_column(rows, place)
    causal[...] = jnp.where(key_column <= query_row, 0.0, MASKED)
    for r in range(chunks):
        key_bias[r * rows : (r + 1) * rows] = jnp.where(key_column + r * rows < length, 0.0, MASKED)

    barrier = pltpu.get_barrier_semaphore()
    for device in (core, far, cross, other((row + 1) % 4), other((row + 2) % 4), other((row + 3) % 4)):
        pl.semaphore_signal(barrier, inc=1, device_id=device, device_id_type=pl.DeviceIdType.MESH)
    pl.semaphore_wait(barrier, 6)

    def trade(r, source, target, send, recv):
        return remote(source.at[r], target.at[row], send.at[r], recv.at[row], other(r))

    def trade_start(r, source, target, send, recv):
        @pl.when(row != r)
        def _():
            trade(r, source, target, send, recv).start()

        @pl.when(row == r)
        def _():
            target[r] = source[r]

    def trade_wait(source, target, send, recv):
        for r in range(4):

            @pl.when(row != r)
            def _():
                trade(r, source, target, send, recv).wait_send()
                remote(source.at[r], target.at[r], send.at[r], recv.at[r], other(r)).wait_recv()

    def far_q_copy(r):
        return remote(far_q_ref.at[r], far_q_in.at[r], q_send.at[r], q_recv.at[r], far)

    ups[0].start()
    ups[1].start()
    outs.start()
    for r in range(4):
        far_q_copy(r).start()

    def give_result(r):
        far_q_copy(r).wait()
        result[r] = (base_ref[r] + far_q_in[r].astype(F32)).astype(LOW)
        trade_start(r, result, res_out, res_send, res_recv)

    block = 256
    lane = lax.broadcasted_iota(jnp.int32, (block, 128), 1)

    def attention(r):
        wide = (r + 1) * rows

        def part(step, carry):
            here = pl.ds(pl.multiple_of(r * rows + (step % 2) * block, block), block)
            pair = pl.ds(pl.multiple_of((step // 2) * 128, 128), 128)
            inside = pl.ds(pl.multiple_of((step % 2) * block, block), block)
            queries = q_ref[here, pair]
            grads = do_ref[here, pair]
            inner = (grads.astype(F32) * o_ref[here, pair].astype(F32)).T
            parts = []
            for head in range(2):
                mine = (lane // HD) == head
                masked = jnp.where(mine, queries, 0) * jnp.asarray(HD**-0.5, LOW)
                masked_grads = jnp.where(mine, grads, 0)
                inner_row = jnp.sum(inner[head * HD : (head + 1) * HD], axis=0, keepdims=True)
                scores = contract(k_ref[:wide, pair], masked, 1, 1) + key_bias[:wide]
                last = scores[wide - rows :] + causal[:, inside]
                scores = last if r == 0 else jnp.concatenate([scores[: wide - rows], last], axis=0)
                weights = jnp.exp(scores - lse_ref[step // 2, r, head : head + 1, inside])
                grad_weights = contract(v_ref[:wide, pair], masked_grads, 1, 1)
                grad_scores = (weights * (grad_weights - inner_row)).astype(LOW)
                dv_sum[:wide, pair] += contract(weights.astype(LOW), masked_grads, 1, 0)
                dk_sum[:wide, pair] += contract(grad_scores, masked, 1, 0)
                parts.append(contract(grad_scores, k_ref[:wide, pair], 0, 0))
            dproj[here, pair] = (jnp.where(lane < HD, parts[0], parts[1]) * HD**-0.5).astype(LOW)
            return carry

        lax.fori_loop(0, 4, part, 0)
        end = slice(wide - rows, wide)
        dproj[end, head_width : 2 * head_width] = dk_sum[end].astype(LOW)
        dproj[end, 2 * head_width :] = dv_sum[end].astype(LOW)

    def core_copy(r):
        return remote(core_out.at[r], core_in.at[r], fold_send.at[0, r], fold_recv.at[0, r], core)

    def far_copy(r):
        return remote(far_out.at[r], far_in.at[r], fold_send.at[1, r], fold_recv.at[1, r], far)

    def project(r):
        total = contract(dproj[r * rows : (r + 1) * rows], w_ref[...], 1, 1)
        kept[r, 0] = total[:own]
        core_out[r, 0] = total[own : 2 * own].astype(LOW)
        kept[r, 1] = total[2 * own : 3 * own]
        core_out[r, 1] = total[3 * own :].astype(LOW)
        core_copy(r).start()

    def fold(r):
        core_copy(r).wait()
        far_out[r] = (kept[r, 1] + core_in[r, 1].astype(F32)).astype(LOW)
        kept[r, 0] = kept[r, 0] + core_in[r, 0].astype(F32)
        far_copy(r).start()

    vec[...] = jnp.zeros_like(vec)

    def norm_grad(r):
        far_copy(r).wait()
        grads = kept[r, 0] + far_in[r].astype(F32)
        unit, scale = norm_parts(tok_ref[r].astype(F32))
        gtok[r] = (gmid_ref[r].astype(F32) + norm_back(grads, gain_ref[...], unit, scale)).astype(LOW)
        trade_start(r, gtok, gtok_out, tok_send, tok_recv)
        vec[0:1] += jnp.sum(grads * unit, axis=0, keepdims=True)
        vec[1:2] += jnp.sum(grads, axis=0, keepdims=True)

    def tile_copy(t):
        tile = (2 * (1 - dp) + t) % 4
        part = pl.ds(pl.multiple_of(tile * 256, 256), 256)
        return pltpu.make_async_copy(normed_ref.at[:, part], norm_tile.at[t % 2], tile_sem.at[t % 2])

    dk_sum[...] = jnp.zeros_like(dk_sum)
    dv_sum[...] = jnp.zeros_like(dv_sum)
    tile_copy(0).start()
    tile_copy(1).start()
    downs[0].pump(0)
    downs[1].pump(0)
    attention(3)
    project(3)
    fold(3)
    downs[0].pump(1)
    downs[1].pump(1)
    attention(2)
    project(2)
    fold(2)
    downs[0].pump(2)
    downs[1].pump(2)
    for part in (ups[0], ups[1], outs):
        part.add()
        part.pump(0)
    for r in range(4):
        give_result(r)
    attention(1)
    project(1)
    fold(1)
    norm_grad(3)
    attention(0)
    project(0)
    fold(0)
    for t in range(width // 256):
        tile_copy(t).wait()
        tile = (2 * (1 - dp) + t) % 4
        total = contract(norm_tile[t % 2], dproj[...], 0, 0).astype(LOW)
        gproj[2 * tile] = total[:own]
        gproj[2 * tile + 1] = total[own:]
        if t + 2 < width // 256:
            tile_copy(t + 2).start()
        if t == 1:
            projs[0].start()
            projs[1].start()
    for part in (ups[0], ups[1], outs):
        part.pump(1)
    norm_grad(2)
    norm_grad(1)
    norm_grad(0)
    projs[0].add()
    projs[0].pump(0)
    projs[1].add()
    projs[1].pump(0)
    for part in (ups[0], ups[1], outs):
        part.pump(2)

    vec[2:6] = sums_ref[0:4]
    vec[8:9] = sum_up_ref[...]
    low_sum = jnp.sum(dproj[:, :head_width].astype(F32), axis=0, keepdims=True)
    value_sum = jnp.sum(dproj[:, 2 * head_width :].astype(F32), axis=0, keepdims=True)
    vec[9:10, :head_width] = low_sum
    vec[9:10, head_width : 2 * head_width] = value_sum
    steps = (cross, other(row + 1 - 2 * (row % 2)), other((row + 2) % 4), core, far)
    for step, device in enumerate(steps):
        size = 16 if step < 3 else 8
        copy = remote(vec.at[:size], vec_in.at[step, :size], vec_send.at[step], vec_recv.at[step], device)
        copy.start()
        copy.wait()
        vec[:size] = vec[:size] + vec_in[step, :size]
    shared_out[...] = vec[:8]
    by_col_out[...] = vec[8:]

    for h in range(2):
        ups[h].finish(up_out.at[h * quarters : (h + 1) * quarters])
    outs.finish(out_out)
    wide = down_out.shape[0] // 2
    for h in range(2):
        downs[h].finish(down_out.at[h * wide : (h + 1) * wide])
    projs[0].pump(1)
    projs[1].pump(1)
    projs[0].pump(2)
    projs[1].pump(2)
    for h in range(2):
        here = slice(h * quarters, (h + 1) * quarters)
        projs[h].finish(proj_sum.at[here])
    query_out[...] = proj_sum[:, :head_width]
    key_out[...] = proj_sum[:, head_width : 2 * head_width]
    value_out[...] = proj_sum[:, 2 * head_width :]
    trade_wait(result, res_out, res_send, res_recv)
    trade_wait(gtok, gtok_out, tok_send, tok_recv)


def back_block(
    queries, keys, values, grads, attended, lse, lengths, w_proj, tokens, gmid, base, far_q, sum_down, gup, gout, gain, sums, sum_up, normed
):
    chunks, own, width = tokens.shape
    rows, head_width = queries.shape
    half = (chunks, 2, own, width)
    one = (chunks, own, width)
    hidden = gup.shape[2]
    quarters = own // 2
    out_block = (gout.shape[1], gout.shape[2])
    down_rows = sum_down.shape[2]
    outputs = ((2 * down_rows, own), (own, hidden), out_block, (own, head_width), (own, head_width), (own, head_width))
    vmem = pl.BlockSpec(memory_space=pltpu.VMEM)
    hbm = pl.BlockSpec(memory_space=pl.ANY)
    dma = pltpu.SemaphoreType.DMA
    return pl.pallas_call(
        back_kernel,
        in_specs=[vmem] * 6 + [pl.BlockSpec(memory_space=pltpu.SMEM)] + [vmem] * 11 + [hbm],
        out_specs=[vmem] * 10,
        out_shape=[jax.ShapeDtypeStruct(one, LOW), jax.ShapeDtypeStruct(one, LOW)]
        + [jax.ShapeDtypeStruct(shape, F32) for shape in outputs]
        + [jax.ShapeDtypeStruct((8, width), F32)] * 2,
        scratch_shapes=[
            pltpu.VMEM((rows, head_width), F32),
            pltpu.VMEM((rows, head_width), F32),
            pltpu.VMEM((rows, 3 * head_width), LOW),
            pltpu.VMEM((8, own, 3 * head_width), LOW),
            pltpu.VMEM(half, F32),
            pltpu.VMEM(half, LOW),
            pltpu.VMEM(half, LOW),
            pltpu.VMEM(one, LOW),
            pltpu.VMEM(one, LOW),
            pltpu.VMEM(one, LOW),
            pltpu.VMEM((2, rows, 256), LOW),
        ]
        + [
            pltpu.VMEM((rows, 1), F32),
            pltpu.VMEM((rows // chunks, rows // chunks), F32),
            pltpu.VMEM(one, LOW),
            pltpu.VMEM(one, LOW),
            pltpu.VMEM((2, 4, quarters, hidden), LOW),
            pltpu.VMEM((4,) + out_block, LOW),
            pltpu.VMEM((2, 4, quarters, 3 * head_width), LOW),
            pltpu.VMEM((2, 2, 3, down_rows, own), LOW),
            pltpu.VMEM((2, 2, 3, quarters, hidden), LOW),
            pltpu.VMEM((2, 3) + out_block, LOW),
            pltpu.VMEM((2, 2, 3, quarters, 3 * head_width), LOW),
            pltpu.VMEM((own, 3 * head_width), F32),
            pltpu.VMEM((16, width), F32),
            pltpu.VMEM((5, 16, width), F32),
            dma((4,)),
            dma((4,)),
            dma((4,)),
            dma((4,)),
            dma((4,)),
            dma((4,)),
            dma((2, 4)),
            dma((2, 4)),
            dma((5,)),
            dma((5,)),
            dma((5, 2, 3)),
            dma((5, 2, 3)),
            dma((2, 2, 3)),
            dma((2, 2, 3)),
            dma((5,)),
            dma((5,)),
            dma((2,)),
        ],
        compiler_params=pltpu.CompilerParams(
            collective_id=2, has_side_effects=True, vmem_limit_bytes=61 * 1024 * 1024
        ),
        cost_estimate=pl.CostEstimate(flops=100_000_000_000, bytes_accessed=30_000_000, transcendentals=0),
        name="back_block",
    )(
        queries, keys, values, grads, attended, lse, lengths, w_proj, tokens, gmid, base, far_q, sum_down, gup, gout, gain, sums, sum_up, normed
    )


def local_sequence(
    tokens,
    lengths,
    first_gain,
    first_shift,
    w_query,
    w_key,
    w_value,
    bias_query,
    bias_value,
    w_output,
    bias_output,
    second_gain,
    second_shift,
    w_up,
    bias_up,
    w_down,
    bias_down,
    cotangent,
):
    micro_count, own_rows, width = tokens.shape
    head_width = w_query.shape[1]
    vectors = jnp.stack(
        [bias_output, second_gain, second_shift, bias_down, first_gain, first_shift, bias_down, bias_down]
    )
    (
        queries,
        keys,
        values,
        inputs_low,
        w_projection,
        attended,
        lse,
        base,
        far_part,
        grad_attended,
        grad_output,
        sum_down,
        sums,
        sum_up,
        normed_all,
        grad_middle,
        grad_up,
    ) = feed_block(
        lengths,
        tokens,
        cotangent,
        w_query,
        w_key,
        w_value,
        w_output,
        w_up,
        w_down,
        vectors,
        bias_up.reshape(1, -1),
        bias_query.reshape(1, -1),
        bias_value.reshape(1, -1),
    )
    result, grad_tokens, grad_down, grad_up, grad_output, grad_query, grad_key, grad_value, shared, by_col = back_block(
        queries,
        keys,
        values,
        grad_attended,
        attended,
        lse,
        lengths,
        w_projection.reshape(width, 3 * head_width),
        inputs_low,
        grad_middle,
        base,
        far_part,
        sum_down,
        grad_up,
        grad_output,
        first_gain.reshape(1, width),
        sums,
        sum_up,
        normed_all,
    )
    return (
        result,
        grad_tokens,
        shared[0],
        shared[1],
        grad_query,
        grad_key,
        grad_value,
        by_col[1, :head_width],
        by_col[1, head_width : 2 * head_width],
        grad_output,
        shared[2],
        shared[3],
        shared[4],
        grad_up,
        by_col[0],
        grad_down,
        shared[5],
    )


def solution(mesh):
    return jax.shard_map(
        local_sequence if fits(mesh) else local_general,
        mesh=mesh,
        in_specs=(
            P(None, ("dp", "row", "col"), None),
            P("dp", None),
            P(),
            P(),
            P(("dp", "row"), "col"),
            P(("dp", "row"), "col"),
            P(("dp", "row"), "col"),
            P("col"),
            P("col"),
            P("col", ("dp", "row")),
            P(),
            P(),
            P(),
            P(("dp", "row"), "col"),
            P("col"),
            P("col", ("dp", "row")),
            P(),
            P(None, ("dp", "row", "col"), None),
        ),
        out_specs=(
            P(None, ("dp", "row", "col"), None),
            P(None, ("dp", "row", "col"), None),
            P(),
            P(),
            P(("dp", "row"), "col"),
            P(("dp", "row"), "col"),
            P(("dp", "row"), "col"),
            P("col"),
            P("col"),
            P("col", ("dp", "row")),
            P(),
            P(),
            P(),
            P(("dp", "row"), "col"),
            P("col"),
            P("col", ("dp", "row")),
            P(),
        ),
        check_vma=False,
    )
```

```python
import functools

import jax
import jax.numpy as jnp
from jax import lax
from jax.experimental import pallas as pl
from jax.experimental.pallas import tpu as pltpu
from jax.sharding import PartitionSpec as P

HD = 64


EPSILON = 1e-05
MASKED = -1e30


def layer_norm(values, norm_gain, norm_shift):
    centered = values - jnp.mean(values, axis=-1, keepdims=True)
    variance = jnp.mean(centered * centered, axis=-1, keepdims=True)
    return centered * lax.rsqrt(variance + EPSILON) * norm_gain + norm_shift


def gelu_tanh(values):
    return jax.nn.gelu(values, approximate=True)


def product(former, latter):
    return jnp.dot(former, latter, preferred_element_type=jnp.float32)


def transposed_left(former, latter):
    return lax.dot_general(
        former, latter, (((0,), (0,)), ((), ())), preferred_element_type=jnp.float32
    )


def transposed_right(former, latter):
    return lax.dot_general(
        former, latter, (((1,), (1,)), ((), ())), preferred_element_type=jnp.float32
    )


def spread_rows(rows_block):
    return lax.all_gather(rows_block, "col", axis=0, tiled=True)


def fold_rows(partial_sum):
    return lax.psum_scatter(partial_sum, "col", scatter_dimension=0, tiled=True)


def fetch_weights(w_query, w_key, w_value, w_up, w_output, w_down):
    leading = (
        lax.all_gather(w_query, ("dp", "row"), axis=0, tiled=True),
        lax.all_gather(w_key, ("dp", "row"), axis=0, tiled=True),
        lax.all_gather(w_value, ("dp", "row"), axis=0, tiled=True),
        lax.all_gather(w_up, ("dp", "row"), axis=0, tiled=True),
    )
    trailing = (
        lax.all_gather(w_output, ("dp", "row"), axis=1, tiled=True),
        lax.all_gather(w_down, ("dp", "row"), axis=1, tiled=True),
    )
    return tuple(leading) + tuple(trailing)


def reduce_blocks(gradients):
    leading = (
        lax.psum_scatter(gradients[0], ("dp", "row"), scatter_dimension=0, tiled=True),
        lax.psum_scatter(gradients[1], ("dp", "row"), scatter_dimension=0, tiled=True),
        lax.psum_scatter(gradients[2], ("dp", "row"), scatter_dimension=0, tiled=True),
        lax.psum_scatter(gradients[3], ("dp", "row"), scatter_dimension=0, tiled=True),
    )
    trailing = (
        lax.psum_scatter(gradients[4], ("dp", "row"), scatter_dimension=1, tiled=True),
        lax.psum_scatter(gradients[5], ("dp", "row"), scatter_dimension=1, tiled=True),
    )
    return tuple(leading) + tuple(trailing)


def heads_of(rows_block):
    return rows_block.reshape(rows_block.shape[0], -1, HD)


def block_of(rows_all, start, block_rows):
    return heads_of(lax.dynamic_slice_in_dim(rows_all, start, block_rows, 0))


def block_scores(query_heads, key_heads, query_start, key_start, length):
    block_rows = query_heads.shape[0]
    scores = jnp.einsum(
        "qhd,khd->hqk", query_heads, key_heads, preferred_element_type=jnp.float32
    ) * HD ** (-0.5)
    query_pos = query_start + jnp.arange(block_rows, dtype=jnp.int32)
    key_pos = key_start + jnp.arange(key_heads.shape[0], dtype=jnp.int32)
    allowed = (key_pos[None, :] <= query_pos[:, None]) & (key_pos[None, :] < length)
    return jnp.where(allowed[None], scores, MASKED)


def key_block_count(row_place, length, block_rows):
    return jnp.minimum(row_place + 1, (length + block_rows - 1) // block_rows)


def attention_forward(queries, key_rows, value_rows, row_place, length):
    block_rows = queries.shape[0]
    query_heads = heads_of(queries)
    head_count = query_heads.shape[1]
    query_start = row_place * block_rows
    count = key_block_count(row_place, length, block_rows)

    def stats_step(block_index, carry):
        highest, partition = carry
        start = block_index * block_rows
        scores = block_scores(
            query_heads, block_of(key_rows, start, block_rows), query_start, start, length
        )
        newest = jnp.maximum(highest, jnp.max(scores, axis=-1, keepdims=True))
        partition = partition * jnp.exp(highest - newest) + jnp.sum(
            jnp.exp(scores - newest), axis=-1, keepdims=True
        )
        return (newest, partition)

    start_stats = (
        jnp.full((head_count, block_rows, 1), MASKED, jnp.float32),
        jnp.zeros((head_count, block_rows, 1), jnp.float32),
    )
    highest, partition = lax.fori_loop(0, count, stats_step, start_stats)

    def output_step(block_index, total):
        start = block_index * block_rows
        scores = block_scores(
            query_heads, block_of(key_rows, start, block_rows), query_start, start, length
        )
        weights_low = (jnp.exp(scores - highest) / partition).astype(jnp.bfloat16)
        return total + jnp.einsum(
            "hqk,khd->qhd",
            weights_low,
            block_of(value_rows, start, block_rows),
            preferred_element_type=jnp.float32,
        )

    total = lax.fori_loop(0, count, output_step, jnp.zeros(query_heads.shape, jnp.float32))
    return (total.reshape(block_rows, -1), highest, partition)


def attention_query_side(
    queries, key_rows, value_rows, grad_attended, highest, partition, row_place, length
):
    block_rows = queries.shape[0]
    seq_rows = key_rows.shape[0]
    query_heads = heads_of(queries)
    grad_heads = heads_of(grad_attended)
    head_count = query_heads.shape[1]
    query_start = row_place * block_rows
    count = key_block_count(row_place, length, block_rows)

    def inner_step(block_index, total):
        start = block_index * block_rows
        scores = block_scores(
            query_heads, block_of(key_rows, start, block_rows), query_start, start, length
        )
        weights = jnp.exp(scores - highest) / partition
        grad_weights = jnp.einsum(
            "qhd,khd->hqk",
            grad_heads,
            block_of(value_rows, start, block_rows),
            preferred_element_type=jnp.float32,
        )
        return total + jnp.sum(weights * grad_weights, axis=-1, keepdims=True)

    inner = lax.fori_loop(0, count, inner_step, jnp.zeros((head_count, block_rows, 1), jnp.float32))

    def grad_step(block_index, carry):
        start = block_index * block_rows
        key_heads = block_of(key_rows, start, block_rows)
        scores = block_scores(query_heads, key_heads, query_start, start, length)
        weights = jnp.exp(scores - highest) / partition
        grad_weights = jnp.einsum(
            "qhd,khd->hqk",
            grad_heads,
            block_of(value_rows, start, block_rows),
            preferred_element_type=jnp.float32,
        )
        grad_scores = (weights * (grad_weights - inner)).astype(jnp.bfloat16)
        query_total = carry[0] + jnp.einsum(
            "hqk,khd->qhd", grad_scores, key_heads, preferred_element_type=jnp.float32
        )
        weights_low = weights.astype(jnp.bfloat16)
        key_part = jnp.einsum(
            "hqk,qhd->khd", grad_scores, query_heads, preferred_element_type=jnp.float32
        )
        value_part = jnp.einsum(
            "hqk,qhd->khd", weights_low, grad_heads, preferred_element_type=jnp.float32
        )
        key_total = lax.dynamic_update_slice_in_dim(
            carry[1], lax.dynamic_slice_in_dim(carry[1], start, block_rows, 0) + key_part, start, 0
        )
        value_total = lax.dynamic_update_slice_in_dim(
            carry[2],
            lax.dynamic_slice_in_dim(carry[2], start, block_rows, 0) + value_part,
            start,
            0,
        )
        return (query_total, key_total, value_total)

    start_carry = (jnp.zeros(query_heads.shape, jnp.float32),)
    start_carry = start_carry + (
        jnp.zeros((seq_rows, head_count, HD), jnp.float32),
        jnp.zeros((seq_rows, head_count, HD), jnp.float32),
    )
    totals = lax.fori_loop(0, count, grad_step, start_carry)
    query_terms = totals[0].reshape(block_rows, -1) * HD ** (-0.5)
    return (
        query_terms,
        totals[1].reshape(seq_rows, -1) * HD ** (-0.5),
        totals[2].reshape(seq_rows, -1),
        inner,
    )


def local_general(
    tokens,
    lengths,
    first_gain,
    first_shift,
    w_query,
    w_key,
    w_value,
    bias_query,
    bias_value,
    w_output,
    bias_output,
    second_gain,
    second_shift,
    w_up,
    bias_up,
    w_down,
    bias_down,
    cotangent,
):
    micro_count, own_rows, width = tokens.shape
    col_count = lax.axis_size("col")
    group_rows = own_rows * col_count
    row_place = lax.axis_index("row")
    col_place = lax.axis_index("col")
    head_width = w_query.shape[1]
    hidden_width = w_up.shape[1]
    own_positions = (
        row_place * group_rows + col_place * own_rows + jnp.arange(own_rows, dtype=jnp.int32)
    )
    weight_totals = (
        jnp.zeros((width, head_width), jnp.float32),
        jnp.zeros((width, head_width), jnp.float32),
        jnp.zeros((width, head_width), jnp.float32),
        jnp.zeros((width, hidden_width), jnp.float32),
        jnp.zeros((head_width, width), jnp.float32),
        jnp.zeros((hidden_width, width), jnp.float32),
    )
    vector_totals = (
        jnp.zeros((width,), jnp.float32),
        jnp.zeros((width,), jnp.float32),
        jnp.zeros((head_width,), jnp.float32),
        jnp.zeros((head_width,), jnp.float32),
        jnp.zeros((width,), jnp.float32),
        jnp.zeros((width,), jnp.float32),
        jnp.zeros((width,), jnp.float32),
        jnp.zeros((hidden_width,), jnp.float32),
        jnp.zeros((width,), jnp.float32),
    )
    results = []
    input_grads = []
    for micro_index in range(micro_count):
        gathered = fetch_weights(w_query, w_key, w_value, w_up, w_output, w_down)
        query_full, key_full, value_full, up_full, output_full, down_full = gathered
        length = lengths[0, micro_index]
        inputs = tokens[micro_index].astype(jnp.float32)
        normed = layer_norm(inputs, first_gain, first_shift).astype(jnp.bfloat16)
        normed_all = spread_rows(normed)
        queries = (product(normed_all, query_full) + bias_query).astype(jnp.bfloat16)
        keys_local = product(normed_all, key_full).astype(jnp.bfloat16)
        values_local = (product(normed_all, value_full) + bias_value).astype(jnp.bfloat16)
        keys_all, values_all = (
            lax.all_gather(keys_local, "row", axis=0, tiled=True),
            lax.all_gather(values_local, "row", axis=0, tiled=True),
        )
        attended, maxima, partitions = attention_forward(
            queries, keys_all, values_all, row_place, length
        )
        attended_low = attended.astype(jnp.bfloat16)
        branch = fold_rows(product(attended_low, output_full)) + bias_output
        middle = inputs + branch
        second_normed = layer_norm(middle, second_gain, second_shift).astype(jnp.bfloat16)
        second_all = spread_rows(second_normed)
        pre_activation = product(second_all, up_full) + bias_up
        activated = gelu_tanh(pre_activation).astype(jnp.bfloat16)
        result = middle + (fold_rows(product(activated, down_full)) + bias_down)
        results.append(result.astype(jnp.bfloat16))
        query_full, key_full, value_full, up_full, output_full, down_full = fetch_weights(
            w_query, w_key, w_value, w_up, w_output, w_down
        )
        validity = (own_positions < length).astype(jnp.float32)
        grad_result = cotangent[micro_index].astype(jnp.float32) * validity[:, None]
        grad_result_all = spread_rows(grad_result.astype(jnp.bfloat16))
        grad_down = transposed_left(activated, grad_result_all)
        grad_activated = transposed_right(grad_result_all, down_full)
        gelu_back = jax.vjp(gelu_tanh, pre_activation)[1]
        grad_pre = gelu_back(grad_activated)[0].astype(jnp.bfloat16)
        grad_up = transposed_left(second_all, grad_pre)
        grad_second_normed = fold_rows(transposed_right(grad_pre, up_full))
        second_back = jax.vjp(layer_norm, middle, second_gain, second_shift)[1]
        grad_middle_norm, grad_second_gain, grad_second_shift = second_back(grad_second_normed)
        grad_middle = grad_result + grad_middle_norm
        grad_branch = grad_middle.astype(jnp.bfloat16)
        grad_branch_all = spread_rows(grad_branch)
        grad_output = transposed_left(attended_low, grad_branch_all)
        grad_attended = transposed_right(grad_branch_all, output_full).astype(jnp.bfloat16)
        query_terms, key_terms, value_terms, inner = attention_query_side(
            queries, keys_all, values_all, grad_attended, maxima, partitions, row_place, length
        )
        key_sums, value_sums = (
            lax.psum_scatter(key_terms, "row", scatter_dimension=0, tiled=True),
            lax.psum_scatter(value_terms, "row", scatter_dimension=0, tiled=True),
        )
        grad_queries = query_terms.astype(jnp.bfloat16)
        grad_keys = key_sums.astype(jnp.bfloat16)
        grad_values = value_sums.astype(jnp.bfloat16)
        grad_query = transposed_left(normed_all, grad_queries)
        grad_key = transposed_left(normed_all, grad_keys)
        grad_value = transposed_left(normed_all, grad_values)
        grad_normed = fold_rows(
            transposed_right(grad_queries, query_full)
            + transposed_right(grad_keys, key_full)
            + transposed_right(grad_values, value_full)
        )
        first_back = jax.vjp(layer_norm, inputs, first_gain, first_shift)[1]
        grad_inputs_norm, grad_first_gain, grad_first_shift = first_back(grad_normed)
        input_grads.append((grad_middle + grad_inputs_norm).astype(jnp.bfloat16))
        local_grads = (grad_query, grad_key, grad_value, grad_up, grad_output, grad_down)
        weight_totals = tuple(
            (former + latter for former, latter in zip(weight_totals, local_grads))
        )
        local_vectors = (
            grad_first_gain,
            grad_first_shift,
            jnp.sum(grad_queries.astype(jnp.float32), axis=0),
            jnp.sum(grad_values.astype(jnp.float32), axis=0),
            jnp.sum(grad_branch.astype(jnp.float32), axis=0),
            grad_second_gain,
            grad_second_shift,
            jnp.sum(grad_pre.astype(jnp.float32), axis=0),
            jnp.sum(grad_result, axis=0),
        )
        vector_totals = tuple(
            (former + latter for former, latter in zip(vector_totals, local_vectors))
        )
    weight_totals = reduce_blocks(weight_totals)

    def widen(vector_part):
        blank = jnp.zeros((vector_part.shape[0] * col_count,), jnp.float32)
        return lax.dynamic_update_slice(blank, vector_part, (col_place * vector_part.shape[0],))

    def narrow(whole_vector, piece_width):
        return lax.dynamic_slice_in_dim(whole_vector, col_place * piece_width, piece_width)

    (
        sum_first_gain,
        sum_first_shift,
        sum_bias_query,
        sum_bias_value,
        sum_bias_output,
        sum_second_gain,
        sum_second_shift,
        sum_bias_up,
        sum_bias_down,
    ) = lax.psum(
        (
            vector_totals[0],
            vector_totals[1],
            widen(vector_totals[2]),
            widen(vector_totals[3]),
            vector_totals[4],
            vector_totals[5],
            vector_totals[6],
            widen(vector_totals[7]),
            vector_totals[8],
        ),
        ("dp", "row", "col"),
    )
    grad_w_query, grad_w_key, grad_w_value, grad_w_up, grad_w_output, grad_w_down = weight_totals
    return (
        jnp.stack(results, axis=0),
        jnp.stack(input_grads, axis=0),
        sum_first_gain,
        sum_first_shift,
        grad_w_query,
        grad_w_key,
        grad_w_value,
        narrow(sum_bias_query, head_width),
        narrow(sum_bias_value, head_width),
        grad_w_output,
        sum_bias_output,
        sum_second_gain,
        sum_second_shift,
        grad_w_up,
        narrow(sum_bias_up, hidden_width),
        grad_w_down,
        sum_bias_down,
    )


F32 = jnp.float32
LOW = jnp.bfloat16
VMEM_LIMIT = 56 * 1024 * 1024


def fits(mesh):
    return mesh.shape["row"] == 4 and mesh.shape["col"] == 4 and mesh.shape["dp"] == 2


def contract(former, latter, former_dim, latter_dim):
    return lax.dot_general(
        former,
        latter,
        (((former_dim,), (latter_dim,)), ((), ())),
        preferred_element_type=jnp.float32,
    )


def norm_parts(values):
    centered = values - jnp.mean(values, axis=-1, keepdims=True)
    scale = lax.rsqrt(jnp.mean(centered * centered, axis=-1, keepdims=True) + EPSILON)
    return centered * scale, scale


def norm_back(grads, gain, unit, scale):
    inner = grads * gain
    mean_inner = jnp.mean(inner, axis=-1, keepdims=True)
    mean_unit = jnp.mean(inner * unit, axis=-1, keepdims=True)
    return scale * (inner - mean_inner - unit * mean_unit)


GELU_SCALE = 0.7978845608028654
GELU_CUBE = 0.044715


def gelu_parts(values):
    square = values * values
    curve = jnp.tanh(GELU_SCALE * values * (1.0 + GELU_CUBE * square))
    half = 0.5 + 0.5 * curve
    slope = half + 0.5 * values * (1.0 - curve * curve) * (GELU_SCALE * (1.0 + 3.0 * GELU_CUBE * square))
    return values * half, slope


def peers():
    place = lax.axis_index("col")
    return {"col": place + 1 - 2 * (place % 2)}, {"col": (place + 2) % 4}


def remote(source, target, send_sem, recv_sem, device):
    return pltpu.make_async_remote_copy(
        src_ref=source,
        dst_ref=target,
        send_sem=send_sem,
        recv_sem=recv_sem,
        device_id=device,
        device_id_type=pl.DeviceIdType.MESH,
    )


def row_peers():
    row = lax.axis_index("row")
    return row + 1 - 2 * (row % 2), (row + 2) % 4, 3 - row


def greet_all(core, far):
    row = lax.axis_index("row")
    cross = {"dp": 1 - lax.axis_index("dp")}
    barrier = pltpu.get_barrier_semaphore()
    rows = [{"row": (row + step) % 4} for step in (1, 2, 3)]
    for device in [core, far, cross] + rows:
        pl.semaphore_signal(barrier, inc=1, device_id=device, device_id_type=pl.DeviceIdType.MESH)
    pl.semaphore_wait(barrier, 6)


class Gather:
    def __init__(self, slot, z_send, z_recv, x_send, x_recv):
        self.slot, self.z_send, self.z_recv, self.x_send, self.x_recv = slot, z_send, z_recv, x_send, x_recv
        self.row, self.dp = lax.axis_index("row"), lax.axis_index("dp")

    def lane(self, d):
        if d == 0:
            return self.row, {"row": jnp.minimum(self.row + 1, 3)}
        return 3 - self.row, {"row": jnp.maximum(self.row - 1, 0)}

    def z_copy(self, d, k, block):
        view = self.slot(self.dp * 4 + block)
        return remote(view, view, self.z_send.at[d, k], self.z_recv.at[d, k], self.lane(d)[1])

    def x_copy(self, block):
        view = self.slot(self.dp * 4 + block)
        return remote(view, view, self.x_send.at[block], self.x_recv.at[block], {"dp": 1 - self.dp})

    def pump(self, k):
        for d in range(2):
            place, _ = self.lane(d)
            block = self.row - k if d == 0 else self.row + k
            if k == 0:
                if d == 0:
                    self.x_copy(block).start()

                @pl.when(place <= 2)
                def _():
                    self.z_copy(d, 0, block).start()
            else:

                @pl.when(place >= k)
                def _():
                    self.z_copy(d, k - 1, block).wait_recv()
                    if k < 3:

                        @pl.when(place <= 2)
                        def _():
                            self.z_copy(d, k, block).start()

                    self.x_copy(block).start()

    def arrive(self):
        for block in range(4):
            view = self.slot((1 - self.dp) * 4 + block)
            remote(view, view, self.x_send.at[block], self.x_recv.at[block], {"dp": 1 - self.dp}).wait_recv()

    def sent(self):
        for block in range(4):
            self.x_copy(block).wait_send()
        for d in range(2):
            place, _ = self.lane(d)
            for k in range(3):

                @pl.when((place >= k) & (place <= 2))
                def _():
                    self.z_copy(d, k, self.row - k if d == 0 else self.row + k).wait_send()


class Spread:
    def __init__(self, source, target, trade_send, trade_recv, send, recv):
        self.source, self.target = source, target
        self.trade_send, self.trade_recv, self.send, self.recv = trade_send, trade_recv, send, recv
        self.core, self.far = peers()
        self.row = lax.axis_index("row")

    def trade_copy(self, place):
        return remote(
            self.source.at[place],
            self.target.at[self.row, 0],
            self.trade_send.at[place],
            self.trade_recv.at[self.row],
            {"row": place},
        )

    def trade(self):
        for place in row_peers():
            self.trade_copy(place).start()

    def traded(self):
        for place in row_peers():
            self.trade_copy(place).wait_send()

    def hop(self, step, r):
        source, target, device = ((0, 1, self.core), (0, 2, self.far), (2, 3, self.core))[step]
        return remote(
            self.target.at[r, source], self.target.at[r, target], self.send.at[step, r], self.recv.at[step, r], device
        )

    def arrive(self, r):
        remote(
            self.source.at[r], self.target.at[r, 0], self.trade_send.at[r], self.trade_recv.at[r], {"row": r}
        ).wait_recv()

    def first(self, r):
        self.hop(1, r).start()
        self.hop(0, r).start()

    def relay(self, r):
        self.hop(1, r).wait()
        self.hop(2, r).start()

    def done(self, r):
        self.hop(0, r).wait()
        self.hop(2, r).wait()


class Reduce:
    def __init__(self, grads, sums, moving, x_send, x_recv, z_send, z_recv):
        self.grads, self.sums, self.moving = grads, sums, moving
        self.x_send, self.x_recv, self.z_send, self.z_recv = x_send, x_recv, z_send, z_recv
        self.row, self.dp = lax.axis_index("row"), lax.axis_index("dp")

    def x_copy(self):
        half = self.grads.at[pl.ds((1 - self.dp) * 4, 4)]
        return remote(half, self.sums, self.x_send, self.x_recv, {"dp": 1 - self.dp})

    def start(self):
        self.x_copy().start()

    def add(self):
        self.x_copy().wait()
        for b in range(4):
            self.sums[b] = (self.sums[b].astype(F32) + self.grads[self.dp * 4 + b].astype(F32)).astype(LOW)

    def lane(self, d):
        if d == 0:
            return self.row, {"row": jnp.minimum(self.row + 1, 3)}
        return 3 - self.row, {"row": jnp.maximum(self.row - 1, 0)}

    def z_copy(self, d, k, source):
        return remote(source, self.moving.at[d, k], self.z_send.at[d, k], self.z_recv.at[d, k], self.lane(d)[1])

    def pump(self, k):
        for d in range(2):
            place, _ = self.lane(d)

            @pl.when(place == 0)
            def _():
                self.z_copy(d, k, self.sums.at[3 - k if d == 0 else k]).start()

            if k >= 1:

                @pl.when((place >= 1) & (place <= k))
                def _():
                    block = 3 - k + place if d == 0 else k - place
                    self.z_copy(d, k - 1, self.sums.at[0]).wait_recv()
                    self.moving[d, k - 1] = (
                        self.moving[d, k - 1].astype(F32) + self.sums[block].astype(F32)
                    ).astype(LOW)
                    self.z_copy(d, k, self.moving.at[d, k - 1]).start()

    def finish(self, out):
        out[...] = self.sums[self.row].astype(F32)
        for d in range(2):
            place, _ = self.lane(d)

            @pl.when(place >= 1)
            def _():
                self.z_copy(d, 2, self.sums.at[0]).wait_recv()
                out[...] += self.moving[d, 2].astype(F32)

            for k in range(3):

                @pl.when(place <= k)
                def _():
                    self.z_copy(d, k, self.sums.at[0]).wait_send()


def positions_row(shape, place):
    own = shape // 4
    lane = lax.broadcasted_iota(jnp.int32, (1, own), 1)
    places = (place, place + 1 - 2 * (place % 2), (place + 2) % 4, 3 - place)
    return jnp.concatenate([lane + other * own for other in places], axis=1)


def positions_column(shape, place):
    own = shape // 4
    line = lax.broadcasted_iota(jnp.int32, (own, 1), 0)
    places = (place, place + 1 - 2 * (place % 2), (place + 2) % 4, 3 - place)
    return jnp.concatenate([line + other * own for other in places], axis=0)


def feed_kernel(
    lengths_ref,
    tokens_ref,
    cot_ref,
    wq_ref,
    wk_ref,
    wv_ref,
    wo_shard,
    wu_shard,
    wd_shard,
    vec_ref,
    bias_up_ref,
    bias_q_ref,
    bias_v_ref,
    q_ref,
    k_ref,
    v_ref,
    tok_ref,
    proj_out,
    att_ref,
    lse_ref,
    middle,
    far_out_q,
    gatt_ref,
    gout_ref,
    x_down,
    sums_ref,
    sum_up_ref,
    normed_out,
    gmid_ref,
    gup_ref,
    wo_ref,
    wu_all,
    wd_ref,
    g_all,
    kept,
    kept_q,
    core_out,
    core_in,
    core_in_q,
    far_out,
    far_in,
    second,
    act,
    gpre,
    branch,
    key_bias,
    causal,
    gdown,
    stage_sems,
    send_sems,
    recv_sems,
    trade_send,
    trade_recv,
    row_send,
    row_recv,
    grad_send,
    grad_recv,
    g_send,
    g_recv,
    za_send,
    za_recv,
    xa_send,
    xa_recv,
    zo_send,
    zo_recv,
    xo_send,
    xo_recv,
    zu_send,
    zu_recv,
    xu_send,
    xu_recv,
    zd_send,
    zd_recv,
    xd_send,
    xd_recv,
    rx_send,
    rx_recv,
    out_sems,
    load_sems,
):
    chunks, blocks, own, width = second.shape
    rows = blocks * own
    hidden = wu_all.shape[2]
    core, far = peers()
    row = lax.axis_index("row")
    mine = lax.axis_index("dp") * 4 + row
    wu_ref = wu_all.reshape(width, hidden)

    def wd_slot(block):
        return wd_ref.at[:, pl.ds(pl.multiple_of(block * own, own), own)]

    down = Gather(wd_slot, zd_send, zd_recv, xd_send, xd_recv)
    near, halfway, distant = row_peers()
    head_width = wq_ref.shape[1]
    rows_all = branch
    normed = gpre.reshape(chunks * rows, width)

    def wo_slot(block):
        return wo_ref.at[:, pl.ds(pl.multiple_of(block * own, own), own)]

    up = Gather(lambda block: wu_all.at[block], zu_send, zu_recv, xu_send, xu_recv)
    output = Gather(wo_slot, zo_send, zo_recv, xo_send, xo_recv)
    spread = Spread(tokens_ref, rows_all, trade_send, trade_recv, row_send, row_recv)
    cots = Spread(cot_ref, g_all, grad_send, grad_recv, g_send, g_recv)
    projs = [
        Gather(
            lambda block, n=n: proj_out.at[block, :, n * head_width : (n + 1) * head_width],
            za_send.at[n],
            za_recv.at[n],
            xa_send.at[n],
            xa_recv.at[n],
        )
        for n in range(3)
    ]
    loads = [
        pltpu.make_async_copy(source, target, load_sems.at[n])
        for n, (source, target) in enumerate(
            (
                (wq_ref, projs[0].slot(mine)),
                (wk_ref, projs[1].slot(mine)),
                (wv_ref, projs[2].slot(mine)),
                (tokens_ref.at[row], rows_all.at[row, 0]),
                (cot_ref.at[row], g_all.at[row, 0]),
                (wo_shard, wo_slot(mine)),
                (wu_shard, wu_all.at[mine]),
                (wd_shard, wd_slot(mine)),
            )
        )
    ]
    for load in loads:
        load.start()
    reduces = [
        Reduce(gdown.at[h], x_down.at[h], None, rx_send.at[h], rx_recv.at[h], None, None)
        for h in range(2)
    ]
    place = lax.axis_index("col")
    length = lengths_ref[0, row]
    key_row, query_column = positions_row(rows, place), positions_column(rows, place)
    causal[...] = jnp.where(key_row <= query_column, 0.0, MASKED).astype(LOW)
    for r in range(chunks):
        key_bias[:, r * rows : (r + 1) * rows] = jnp.where(key_row + r * rows < length, 0.0, MASKED)

    def core_copy(step, r, source, target):
        return remote(source.at[r], target.at[r], send_sems.at[step, r], recv_sems.at[step, r], core)

    def far_copy(step, r, source, target):
        return remote(source.at[r], target.at[r], send_sems.at[step, r], recv_sems.at[step, r], far)

    def spread_core(step, r, rows_ref):
        return remote(rows_ref.at[r, 0], rows_ref.at[r, 1], send_sems.at[step, r], recv_sems.at[step, r], core)

    def spread_far(step, r, rows_ref):
        return remote(rows_ref.at[r, 0], rows_ref.at[r, 2], send_sems.at[step, r], recv_sems.at[step, r], far)

    def spread_relay(step, r, rows_ref):
        return remote(rows_ref.at[r, 2], rows_ref.at[r, 3], send_sems.at[step, r], recv_sems.at[step, r], core)

    def split(r, total, kept_ref, out_ref):
        kept_ref[r, 0] = total[:own].astype(kept_ref.dtype)
        out_ref[r, 0] = total[own : 2 * own].astype(LOW)
        kept_ref[r, 1] = total[2 * own : 3 * own].astype(kept_ref.dtype)
        out_ref[r, 1] = total[3 * own :].astype(LOW)

    def fold(r, kept_ref, in_ref, out_ref):
        out_ref[r] = (kept_ref[r, 1].astype(F32) + in_ref[r, 1].astype(F32)).astype(LOW)
        kept_ref[r, 0] = (kept_ref[r, 0].astype(F32) + in_ref[r, 0].astype(F32)).astype(kept_ref.dtype)

    def each(body):
        lax.fori_loop(0, chunks, lambda r, carry: (body(r), carry)[1], 0)

    def out_projection(r):
        split(r, contract(att_ref[r * rows : (r + 1) * rows], wo_ref[...], 1, 0), kept, core_out)
        core_copy(0, r, core_out, core_in).start()

    def out_fold(r):
        core_copy(0, r, core_out, core_in).wait()
        fold(r, kept, core_in, far_out)
        far_copy(1, r, far_out, far_in).start()

    block = 256
    lane = lax.broadcasted_iota(jnp.int32, (block, 128), 1)

    def attention(r):
        long = (r + 1) * rows

        def part(step, carry):
            here = pl.ds(pl.multiple_of(r * rows + (step % 2) * block, block), block)
            pair = pl.ds(pl.multiple_of((step // 2) * 128, 128), 128)
            inside = pl.ds(pl.multiple_of((step % 2) * block, block), block)
            queries = q_ref[here, pair]
            parts = []
            for head in range(2):
                masked = jnp.where((lane // HD) == head, queries, 0) * jnp.asarray(HD**-0.5, LOW)
                scores = contract(masked, k_ref[:long, pair], 1, 1) + key_bias[:, :long]
                last = scores[:, long - rows :] + causal[inside].astype(F32)
                scores = last if r == 0 else jnp.concatenate([scores[:, : long - rows], last], axis=1)
                highest = jnp.max(scores, axis=1, keepdims=True)
                weights = jnp.exp(scores - highest)
                total = jnp.sum(weights, axis=1, keepdims=True)
                parts.append(contract(weights.astype(LOW), v_ref[:long, pair], 1, 0) / total)
                flat = jnp.broadcast_to(highest + jnp.log(total), (block, 128))
                lse_ref[step // 2, r, head : head + 1, inside] = flat.T[:1]
            att_ref[here, pair] = jnp.where(lane < HD, parts[0], parts[1]).astype(LOW)
            return carry

        lax.fori_loop(0, 4, part, 0)

    def norm(r):
        far_copy(1, r, far_out, far_in).wait()
        values = tok_ref[r].astype(F32) + (kept[r, 0] + far_in[r].astype(F32) + vec_ref[0:1])
        middle[r] = values
        second[r, 0] = (norm_parts(values)[0] * vec_ref[1:2] + vec_ref[2:3]).astype(LOW)
        spread_core(2, r, second).start()
        spread_far(3, r, second).start()

    def norm(r):
        far_copy(1, r, far_out, far_in).wait()
        values = tok_ref[r].astype(F32) + (kept[r, 0] + far_in[r].astype(F32) + vec_ref[0:1])
        middle[r] = values
        second[r, 0] = (norm_parts(values)[0] * vec_ref[1:2] + vec_ref[2:3]).astype(LOW)
        spread_core(2, r, second).start()
        spread_far(3, r, second).start()

    def pump(step):
        for proj in projs:
            proj.pump(step)

    def give_cot(r):
        line = lax.broadcasted_iota(jnp.int32, (own, width), 0) + (r * rows + place * own)
        g_all[r, 0] = jnp.where(line < length, g_all[r, 0], jnp.zeros((), LOW))
        cots.first(r)

    def norm_rows(r):
        spread.done(r)
        here = pl.ds(pl.multiple_of(r * rows, rows), rows)
        values = rows_all[r].reshape(rows, width).astype(F32)
        low = (norm_parts(values)[0] * vec_ref[4:5] + vec_ref[5:6]).astype(LOW)
        gpre[r] = low.reshape(blocks, own, width)
        pltpu.make_async_copy(normed.at[here], normed_out.at[here], out_sems.at[r]).start()
        tok_ref[r] = rows_all[r, 0]

    def project(r):
        here = pl.ds(pl.multiple_of(r * rows, rows), rows)
        total = contract(normed[here], proj_out.reshape(8 * own, 3 * head_width)[...], 1, 0)
        q_ref[here] = (total[:, :head_width] + bias_q_ref[...]).astype(LOW)
        k_ref[here] = total[:, head_width : 2 * head_width].astype(LOW)
        v_ref[here] = (total[:, 2 * head_width :] + bias_v_ref[...]).astype(LOW)

    greet_all(core, far)
    for load in loads[:3]:
        load.wait()
    pump(0)
    spread.trade()
    loads[3].wait()
    spread.first(row)
    loads[4].wait()
    give_cot(row)
    for load in loads[5:]:
        load.wait()
    spread.arrive(near)
    spread.first(near)
    pump(1)
    spread.relay(row)
    cots.relay(row)
    norm_rows(row)
    spread.arrive(halfway)
    spread.first(halfway)
    spread.relay(near)
    spread.arrive(distant)
    spread.first(distant)
    output.pump(0)
    cots.trade()
    norm_rows(near)
    pump(2)
    spread.relay(halfway)
    norm_rows(halfway)
    spread.relay(distant)
    pump(3)
    output.pump(1)
    norm_rows(distant)
    for proj in projs:
        proj.arrive()
    each(project)
    up.pump(0)
    down.pump(0)
    output.pump(2)
    attention(0)
    output.pump(3)
    cots.arrive(near)
    give_cot(near)
    attention(1)
    output.arrive()
    out_projection(0)
    out_projection(1)
    out_fold(0)
    cots.relay(near)
    attention(2)
    out_projection(2)
    out_fold(1)
    norm(0)
    up.pump(1)
    down.pump(1)
    cots.arrive(halfway)
    give_cot(halfway)
    attention(3)
    out_projection(3)
    out_fold(2)
    norm(1)
    out_fold(3)
    cots.arrive(distant)
    give_cot(distant)
    up.pump(2)
    norm(2)
    cots.relay(halfway)
    down.pump(2)
    up.pump(3)
    down.pump(3)
    cots.relay(distant)
    for r in range(chunks):
        here = slice(r * rows, (r + 1) * rows)
        pltpu.make_async_copy(normed.at[here], normed_out.at[here], out_sems.at[r]).wait()
    up.arrive()
    down.arrive()

    sum_up_ref[...] = jnp.zeros_like(sum_up_ref)

    def relay_start(r):
        spread_far(3, r, second).wait()
        spread_relay(4, r, second).start()

    def feed(r):
        spread_core(2, r, second).wait()
        spread_relay(4, r, second).wait()
        cots.done(r)
        pre = contract(second[r].reshape(rows, width), wu_ref[...], 1, 0) + bias_up_ref[...]
        activated, slope = gelu_parts(pre)
        act[r] = activated.astype(LOW).reshape(blocks, own, hidden)
        grads = contract(g_all[r].reshape(rows, width), wd_ref[...], 1, 1) * slope
        grads_low = grads.astype(LOW)
        gpre[r] = grads_low.reshape(blocks, own, hidden)
        sum_up_ref[...] += jnp.sum(grads_low.astype(F32), axis=0, keepdims=True)
        split(r, contract(grads_low, wu_ref[...], 1, 1), kept, core_out)
        core_copy(5, r, core_out, core_in).start()
        total = contract(act[r].reshape(rows, hidden), wd_ref[...], 1, 0)
        core_copy(5, r, core_out, core_in).wait()
        fold(r, kept, core_in, far_out)
        far_copy(6, r, far_out, far_in).start()
        kept_q[r] = total[:own].astype(LOW)
        core_out[r, 0] = total[own : 2 * own].astype(LOW)
        far_out_q[r] = total[2 * own : 3 * own].astype(LOW)
        core_out[r, 1] = total[3 * own :].astype(LOW)
        core_copy(7, r, core_out, core_in_q).start()

    wide = 256
    flat_second = second.reshape(chunks * rows, width)
    flat_act = act.reshape(chunks * rows, hidden)
    flat_gpre = gpre.reshape(chunks * rows, hidden)
    flat_g = g_all.reshape(chunks * rows, width)
    flat_branch = branch.reshape(chunks * rows, width)

    def some(first, last, body):
        lax.fori_loop(first, last, lambda t, carry: (body(t), carry)[1], 0)

    def down_grad(t):
        part = pl.ds(pl.multiple_of(t * wide, wide), wide)
        here = pl.ds(pl.multiple_of((t % 2) * wide, wide), wide)
        total = contract(flat_act[:, part], flat_g[...], 0, 0).astype(LOW)
        for b in range(8):
            gdown[t // 2, b, here] = total[:, b * own : (b + 1) * own]

    sums_ref[...] = jnp.zeros_like(sums_ref)

    def norm_grad(r):
        far_copy(6, r, far_out, far_in).wait()
        grads = kept[r, 0] + far_in[r].astype(F32)
        unit, scale = norm_parts(middle[r])
        own_grads = g_all[r, 0].astype(F32)
        total = own_grads + norm_back(grads, vec_ref[1:2], unit, scale)
        low = total.astype(LOW)
        branch[r, 0] = low
        spread_core(9, r, branch).start()
        spread_far(10, r, branch).start()
        sums_ref[0:1] += jnp.sum(low.astype(F32), axis=0, keepdims=True)
        sums_ref[1:2] += jnp.sum(grads * unit, axis=0, keepdims=True)
        sums_ref[2:3] += jnp.sum(grads, axis=0, keepdims=True)
        sums_ref[3:4] += jnp.sum(own_grads, axis=0, keepdims=True)

    relay_start(0)
    feed(0)
    norm(3)
    relay_start(1)

    def step(r):
        feed(r)
        norm_grad(r - 1)

        @pl.when(r < chunks - 1)
        def _():
            relay_start(r + 1)

    some(1, chunks, step)
    some(0, 2, down_grad)
    reduces[0].start()
    some(2, 4, down_grad)
    reduces[1].start()
    norm_grad(chunks - 1)
    given = pltpu.make_async_copy(branch.at[:, 0], gmid_ref, stage_sems.at[0])
    given.start()

    def result_fold(r):
        core_copy(7, r, core_out, core_in_q).wait()
        far_out_q[r] = (far_out_q[r].astype(F32) + core_in_q[r, 1].astype(F32)).astype(LOW)
        own_part = kept_q[r].astype(F32) + core_in_q[r, 0].astype(F32)
        middle[r] = middle[r] + (own_part + vec_ref[3:4])

    each(result_fold)

    def late(r):
        spread_far(10, r, branch).wait()
        spread_relay(11, r, branch).start()
        part = pl.ds(pl.multiple_of(r * wide, wide), wide)
        total = contract(flat_second[:, part], flat_gpre[...], 0, 0).astype(LOW)
        for b in range(2):
            core_out[0, b] = total[b * own : (b + 1) * own]
        copy = pltpu.make_async_copy(core_out.at[0], gup_ref.at[pl.ds(2 * r, 2)], stage_sems.at[1])
        copy.start()
        spread_core(9, r, branch).wait()
        spread_relay(11, r, branch).wait()
        rows_here = pl.ds(pl.multiple_of(r * rows, rows), rows)
        gatt_ref[rows_here] = contract(branch[r].reshape(rows, width), wo_ref[...], 1, 1).astype(LOW)
        copy.wait()

    some(0, 4, late)
    total_out = contract(att_ref[...], flat_branch[...], 0, 0).astype(LOW)
    for b in range(8):
        gout_ref[b] = total_out[:, b * own : (b + 1) * own]
    for h in range(2):
        reduces[h].add()
    given.wait()
    spread.traded()
    cots.traded()
    for gather in projs + [output, up, down]:
        gather.sent()


def feed_block(
    lengths, tokens, cotangent, w_query, w_key, w_value, w_output, w_up, w_down, vectors, bias_up, bias_query, bias_value
):
    chunks, own, width = tokens.shape
    rows = chunks * 4 * own
    head_width = w_query.shape[1]
    hidden = w_up.shape[1]
    half = (chunks, 2, own, width)
    one = (chunks, own, width)
    all_rows = (chunks, 4, own, width)
    vmem = pl.BlockSpec(memory_space=pltpu.VMEM)
    hbm = pl.BlockSpec(memory_space=pl.ANY)
    dma = pltpu.SemaphoreType.DMA
    gather_sems = [dma((2, 3)), dma((2, 3)), dma((4,)), dma((4,))]
    spread_sems = [dma((4,)), dma((4,)), dma((3, 4)), dma((3, 4))]
    return pl.pallas_call(
        feed_kernel,
        in_specs=[pl.BlockSpec(memory_space=pltpu.SMEM)] + [hbm] * 8 + [vmem] * 4,
        out_specs=[vmem] * 14 + [hbm] * 3,
        out_shape=[
            jax.ShapeDtypeStruct((rows, head_width), LOW),
            jax.ShapeDtypeStruct((rows, head_width), LOW),
            jax.ShapeDtypeStruct((rows, head_width), LOW),
            jax.ShapeDtypeStruct(one, LOW),
            jax.ShapeDtypeStruct((8, own, 3 * head_width), LOW),
            jax.ShapeDtypeStruct((rows, head_width), LOW),
            jax.ShapeDtypeStruct((head_width // 128, chunks, 2, rows // chunks), F32),
            jax.ShapeDtypeStruct(one, F32),
            jax.ShapeDtypeStruct(one, LOW),
            jax.ShapeDtypeStruct((rows, head_width), LOW),
            jax.ShapeDtypeStruct((8, head_width, width // 8), LOW),
            jax.ShapeDtypeStruct((2, 4, hidden // 2, width // 8), LOW),
            jax.ShapeDtypeStruct((8, width), F32),
            jax.ShapeDtypeStruct((1, hidden), F32),
            jax.ShapeDtypeStruct((rows, width), LOW),
            jax.ShapeDtypeStruct(one, LOW),
            jax.ShapeDtypeStruct((8, width // 8, hidden), LOW),
        ],
        scratch_shapes=[
            pltpu.VMEM((head_width, width), LOW),
            pltpu.VMEM((8, own, hidden), LOW),
            pltpu.VMEM((hidden, width), LOW),
            pltpu.VMEM(all_rows, LOW),
            pltpu.VMEM(half, F32),
            pltpu.VMEM(one, LOW),
            pltpu.VMEM(half, LOW),
            pltpu.VMEM(half, LOW),
            pltpu.VMEM(half, LOW),
            pltpu.VMEM(one, LOW),
            pltpu.VMEM(one, LOW),
            pltpu.VMEM(all_rows, LOW),
            pltpu.VMEM((chunks, 4, own, hidden), LOW),
            pltpu.VMEM((chunks, 4, own, hidden), LOW),
            pltpu.VMEM(all_rows, LOW),
            pltpu.VMEM((1, rows), F32),
            pltpu.VMEM((rows // chunks, rows // chunks), LOW),
            pltpu.VMEM((2, 8, hidden // 2, width // 8), LOW),
            dma((2,)),
            dma((12, chunks)),
            dma((12, chunks)),
        ]
        + spread_sems
        + spread_sems
        + [dma((3, 2, 3)), dma((3, 2, 3)), dma((3, 4)), dma((3, 4))]
        + gather_sems
        + gather_sems
        + gather_sems
        + [dma((2,)), dma((2,)), dma((4,)), dma((8,))],
        compiler_params=pltpu.CompilerParams(
            collective_id=1, has_side_effects=True, vmem_limit_bytes=62 * 1024 * 1024
        ),
        cost_estimate=pl.CostEstimate(flops=100_000_000_000, bytes_accessed=30_000_000, transcendentals=0),
        name="feed_block",
    )(lengths, tokens, cotangent, w_query, w_key, w_value, w_output, w_up, w_down, vectors, bias_up, bias_query, bias_value)


def back_kernel(
    q_ref,
    k_ref,
    v_ref,
    do_ref,
    o_ref,
    lse_ref,
    lengths_ref,
    w_ref,
    tok_ref,
    gmid_ref,
    base_ref,
    far_q_ref,
    sum_down_ref,
    gup_ref,
    gout_ref,
    gain_ref,
    sums_ref,
    sum_up_ref,
    normed_ref,
    res_out,
    gtok_out,
    down_out,
    up_out,
    out_out,
    query_out,
    key_out,
    value_out,
    shared_out,
    by_col_out,
    dk_sum,
    dv_sum,
    dproj,
    gproj,
    kept,
    core_out,
    core_in,
    far_out,
    far_in,
    gtok,
    norm_tile,
    key_bias,
    causal,
    far_q_in,
    result,
    x_up,
    x_out,
    x_proj,
    z_down,
    z_up,
    z_out,
    z_proj,
    proj_sum,
    vec,
    vec_in,
    q_send,
    q_recv,
    res_send,
    res_recv,
    tok_send,
    tok_recv,
    fold_send,
    fold_recv,
    x_send,
    x_recv,
    z_send,
    z_recv,
    d_send,
    d_recv,
    vec_send,
    vec_recv,
    tile_sem,
):
    chunks, own, width = tok_ref.shape
    rows = 4 * own
    head_width = q_ref.shape[1]
    core, far = peers()
    row = lax.axis_index("row")
    dp = lax.axis_index("dp")
    cross = {"dp": 1 - dp}
    other = lambda r: {"row": r}
    quarters = own // 2

    def reduce_of(n, grads, sums, moving):
        return Reduce(grads, sums, moving, x_send.at[n], x_recv.at[n], z_send.at[n], z_recv.at[n])

    ups = [
        reduce_of(h, gup_ref.at[:, h * quarters : (h + 1) * quarters], x_up.at[h], z_up.at[h]) for h in range(2)
    ]
    outs = reduce_of(2, gout_ref, x_out, z_out)
    projs = [
        reduce_of(3 + p, gproj.at[p], x_proj.at[p], z_proj.at[p]) for p in range(2)
    ]
    downs = [
        Reduce(None, sum_down_ref.at[h], z_down.at[h], None, None, d_send.at[h], d_recv.at[h]) for h in range(2)
    ]
    place = lax.axis_index("col")
    length = lengths_ref[0, row]
    query_row, key_column = positions_row(rows, place), positions_column(rows, place)
    causal[...] = jnp.where(key_column <= query_row, 0.0, MASKED)
    for r in range(chunks):
        key_bias[r * rows : (r + 1) * rows] = jnp.where(key_column + r * rows < length, 0.0, MASKED)

    barrier = pltpu.get_barrier_semaphore()
    for device in (core, far, cross, other((row + 1) % 4), other((row + 2) % 4), other((row + 3) % 4)):
        pl.semaphore_signal(barrier, inc=1, device_id=device, device_id_type=pl.DeviceIdType.MESH)
    pl.semaphore_wait(barrier, 6)

    def trade(r, source, target, send, recv):
        return remote(source.at[r], target.at[row], send.at[r], recv.at[row], other(r))

    def trade_start(r, source, target, send, recv):
        @pl.when(row != r)
        def _():
            trade(r, source, target, send, recv).start()

        @pl.when(row == r)
        def _():
            target[r] = source[r]

    def trade_wait(source, target, send, recv):
        for r in range(4):

            @pl.when(row != r)
            def _():
                trade(r, source, target, send, recv).wait_send()
                remote(source.at[r], target.at[r], send.at[r], recv.at[r], other(r)).wait_recv()

    def far_q_copy(r):
        return remote(far_q_ref.at[r], far_q_in.at[r], q_send.at[r], q_recv.at[r], far)

    ups[0].start()
    ups[1].start()
    outs.start()
    for r in range(4):
        far_q_copy(r).start()

    def give_result(r):
        far_q_copy(r).wait()
        result[r] = (base_ref[r] + far_q_in[r].astype(F32)).astype(LOW)
        trade_start(r, result, res_out, res_send, res_recv)

    block = 256
    lane = lax.broadcasted_iota(jnp.int32, (block, 128), 1)

    def attention(r, p):
        wide = (r + 1) * rows
        pair = slice(p * 128, (p + 1) * 128)

        def part(step, carry):
            here = pl.ds(pl.multiple_of(r * rows + step * block, block), block)
            inside = pl.ds(pl.multiple_of(step * block, block), block)
            queries = q_ref[here, pair]
            grads = do_ref[here, pair]
            inner = (grads.astype(F32) * o_ref[here, pair].astype(F32)).T
            parts = []
            for head in range(2):
                mine = (lane // HD) == head
                masked = jnp.where(mine, queries, 0) * jnp.asarray(HD**-0.5, LOW)
                masked_grads = jnp.where(mine, grads, 0)
                inner_row = jnp.sum(inner[head * HD : (head + 1) * HD], axis=0, keepdims=True)
                scores = contract(k_ref[:wide, pair], masked, 1, 1) + key_bias[:wide]
                last = scores[wide - rows :] + causal[:, inside]
                scores = last if r == 0 else jnp.concatenate([scores[: wide - rows], last], axis=0)
                weights = jnp.exp(scores - lse_ref[p, r, head : head + 1, inside])
                grad_weights = contract(v_ref[:wide, pair], masked_grads, 1, 1)
                grad_scores = (weights * (grad_weights - inner_row)).astype(LOW)
                dv_sum[:wide, pair] += contract(weights.astype(LOW), masked_grads, 1, 0)
                dk_sum[:wide, pair] += contract(grad_scores, masked, 1, 0)
                parts.append(contract(grad_scores, k_ref[:wide, pair], 0, 0))
            dproj[p, here, :128] = (jnp.where(lane < HD, parts[0], parts[1]) * HD**-0.5).astype(LOW)
            return carry

        lax.fori_loop(0, 2, part, 0)
        end = slice(wide - rows, wide)
        dproj[p, end, 128:256] = dk_sum[end, pair].astype(LOW)
        dproj[p, end, 256:] = dv_sum[end, pair].astype(LOW)

    def core_copy(r):
        return remote(core_out.at[r], core_in.at[r], fold_send.at[0, r], fold_recv.at[0, r], core)

    def far_copy(r):
        return remote(far_out.at[r], far_in.at[r], fold_send.at[1, r], fold_recv.at[1, r], far)

    def project(r):
        here = slice(r * rows, (r + 1) * rows)
        grads = jnp.concatenate(
            [dproj[p, here, n * 128 : (n + 1) * 128] for n in range(3) for p in range(2)], axis=1
        )
        total = contract(grads, w_ref[...], 1, 1)
        kept[r, 0] = total[:own]
        core_out[r, 0] = total[own : 2 * own].astype(LOW)
        kept[r, 1] = total[2 * own : 3 * own]
        core_out[r, 1] = total[3 * own :].astype(LOW)
        core_copy(r).start()

    def fold(r):
        core_copy(r).wait()
        far_out[r] = (kept[r, 1] + core_in[r, 1].astype(F32)).astype(LOW)
        kept[r, 0] = kept[r, 0] + core_in[r, 0].astype(F32)
        far_copy(r).start()

    vec[...] = jnp.zeros_like(vec)

    def norm_grad(r):
        far_copy(r).wait()
        grads = kept[r, 0] + far_in[r].astype(F32)
        unit, scale = norm_parts(tok_ref[r].astype(F32))
        gtok[r] = (gmid_ref[r].astype(F32) + norm_back(grads, gain_ref[...], unit, scale)).astype(LOW)
        trade_start(r, gtok, gtok_out, tok_send, tok_recv)
        vec[0:1] += jnp.sum(grads * unit, axis=0, keepdims=True)
        vec[1:2] += jnp.sum(grads, axis=0, keepdims=True)

    def tile_copy(t):
        tile = (2 * (1 - dp) + t) % 4
        part = pl.ds(pl.multiple_of(tile * 256, 256), 256)
        return pltpu.make_async_copy(normed_ref.at[:, part], norm_tile.at[t % 2], tile_sem.at[t % 2])

    dk_sum[...] = jnp.zeros_like(dk_sum)
    dv_sum[...] = jnp.zeros_like(dv_sum)
    tile_copy(0).start()
    tile_copy(1).start()
    def projection_grad(p):
        for t in range(width // 256):
            tile_copy(t).wait()
            tile = (2 * (1 - dp) + t) % 4
            total = contract(norm_tile[t % 2], dproj[p], 0, 0).astype(LOW)
            gproj[p, 2 * tile] = total[:own]
            gproj[p, 2 * tile + 1] = total[own:]
            if t + 2 < width // 256:
                tile_copy(t + 2).start()
            elif p == 0:
                tile_copy(t - 2).start()
            if t == 1:
                projs[p].start()

    def pump(parts, step):
        for part in parts:
            part.pump(step)

    pump(downs, 0)
    attention(3, 0)
    pump(downs, 1)
    attention(2, 0)
    give_result(0)
    give_result(1)
    ups[0].add()
    ups[0].pump(0)
    attention(1, 0)
    pump(downs, 2)
    attention(0, 0)
    give_result(2)
    give_result(3)
    ups[1].add()
    ups[1].pump(0)
    projection_grad(0)
    outs.add()
    outs.pump(0)
    attention(3, 1)
    project(3)
    fold(3)
    pump(ups + [outs], 1)
    attention(2, 1)
    project(2)
    projs[0].add()
    projs[0].pump(0)
    fold(2)
    norm_grad(3)
    attention(1, 1)
    project(1)
    fold(1)
    norm_grad(2)
    pump(ups + [outs], 2)
    attention(0, 1)
    project(0)
    fold(0)
    projs[0].pump(1)
    projection_grad(1)
    norm_grad(1)
    norm_grad(0)

    vec[2:6] = sums_ref[0:4]
    vec[8:9] = sum_up_ref[...]
    for p in range(2):
        part = slice(p * 128, (p + 1) * 128)
        vec[9:10, part] = jnp.sum(dproj[p, :, :128].astype(F32), axis=0, keepdims=True)
        vec[9:10, head_width + p * 128 : head_width + (p + 1) * 128] = jnp.sum(
            dproj[p, :, 256:].astype(F32), axis=0, keepdims=True
        )
    steps = (other(row + 1 - 2 * (row % 2)), other((row + 2) % 4), core, far, cross)

    def sum_copy(step):
        size = 8 if step in (2, 3) else 16
        return size, remote(
            vec.at[:size], vec_in.at[step, :size], vec_send.at[step], vec_recv.at[step], steps[step]
        )

    def sum_start(step):
        sum_copy(step)[1].start()

    def sum_finish(step):
        size, copy = sum_copy(step)
        copy.wait()
        vec[:size] = vec[:size] + vec_in[step, :size]

    sum_start(0)
    projs[0].pump(2)
    projs[1].add()
    projs[1].pump(0)
    sum_finish(0)
    sum_start(1)
    wide = down_out.shape[0] // 2
    for h in range(2):
        downs[h].finish(down_out.at[h * wide : (h + 1) * wide])
        ups[h].finish(up_out.at[h * quarters : (h + 1) * quarters])
    sum_finish(1)
    sum_start(2)
    projs[1].pump(1)
    sum_finish(2)
    sum_start(3)
    outs.finish(out_out)
    sum_finish(3)
    sum_start(4)
    projs[1].pump(2)
    for p in range(2):
        projs[p].finish(proj_sum.at[p])
        part = slice(p * 128, (p + 1) * 128)
        query_out[:, part] = proj_sum[p, :, :128]
        key_out[:, part] = proj_sum[p, :, 128:256]
        value_out[:, part] = proj_sum[p, :, 256:]
    sum_finish(4)
    shared_out[...] = vec[:8]
    by_col_out[...] = vec[8:]
    trade_wait(result, res_out, res_send, res_recv)
    trade_wait(gtok, gtok_out, tok_send, tok_recv)


def back_block(
    queries, keys, values, grads, attended, lse, lengths, w_proj, tokens, gmid, base, far_q, sum_down, gup, gout, gain, sums, sum_up, normed
):
    chunks, own, width = tokens.shape
    rows, head_width = queries.shape
    half = (chunks, 2, own, width)
    one = (chunks, own, width)
    hidden = gup.shape[2]
    quarters = own // 2
    out_block = (gout.shape[1], gout.shape[2])
    down_rows = sum_down.shape[2]
    outputs = ((2 * down_rows, own), (own, hidden), out_block, (own, head_width), (own, head_width), (own, head_width))
    vmem = pl.BlockSpec(memory_space=pltpu.VMEM)
    hbm = pl.BlockSpec(memory_space=pl.ANY)
    dma = pltpu.SemaphoreType.DMA
    return pl.pallas_call(
        back_kernel,
        in_specs=[vmem] * 6 + [pl.BlockSpec(memory_space=pltpu.SMEM)] + [vmem] * 11 + [hbm],
        out_specs=[vmem] * 10,
        out_shape=[jax.ShapeDtypeStruct(one, LOW), jax.ShapeDtypeStruct(one, LOW)]
        + [jax.ShapeDtypeStruct(shape, F32) for shape in outputs]
        + [jax.ShapeDtypeStruct((8, width), F32)] * 2,
        scratch_shapes=[
            pltpu.VMEM((rows, head_width), F32),
            pltpu.VMEM((rows, head_width), F32),
            pltpu.VMEM((2, rows, 384), LOW),
            pltpu.VMEM((2, 8, own, 384), LOW),
            pltpu.VMEM(half, F32),
            pltpu.VMEM(half, LOW),
            pltpu.VMEM(half, LOW),
            pltpu.VMEM(one, LOW),
            pltpu.VMEM(one, LOW),
            pltpu.VMEM(one, LOW),
            pltpu.VMEM((2, rows, 256), LOW),
        ]
        + [
            pltpu.VMEM((rows, 1), F32),
            pltpu.VMEM((rows // chunks, rows // chunks), F32),
            pltpu.VMEM(one, LOW),
            pltpu.VMEM(one, LOW),
            pltpu.VMEM((2, 4, quarters, hidden), LOW),
            pltpu.VMEM((4,) + out_block, LOW),
            pltpu.VMEM((2, 4, own, 384), LOW),
            pltpu.VMEM((2, 2, 3, down_rows, own), LOW),
            pltpu.VMEM((2, 2, 3, quarters, hidden), LOW),
            pltpu.VMEM((2, 3) + out_block, LOW),
            pltpu.VMEM((2, 2, 3, own, 384), LOW),
            pltpu.VMEM((2, own, 384), F32),
            pltpu.VMEM((16, width), F32),
            pltpu.VMEM((5, 16, width), F32),
            dma((4,)),
            dma((4,)),
            dma((4,)),
            dma((4,)),
            dma((4,)),
            dma((4,)),
            dma((2, 4)),
            dma((2, 4)),
            dma((5,)),
            dma((5,)),
            dma((5, 2, 3)),
            dma((5, 2, 3)),
            dma((2, 2, 3)),
            dma((2, 2, 3)),
            dma((5,)),
            dma((5,)),
            dma((2,)),
        ],
        compiler_params=pltpu.CompilerParams(
            collective_id=2, has_side_effects=True, vmem_limit_bytes=61 * 1024 * 1024
        ),
        cost_estimate=pl.CostEstimate(flops=100_000_000_000, bytes_accessed=30_000_000, transcendentals=0),
        name="back_block",
    )(
        queries, keys, values, grads, attended, lse, lengths, w_proj, tokens, gmid, base, far_q, sum_down, gup, gout, gain, sums, sum_up, normed
    )


def local_sequence(
    tokens,
    lengths,
    first_gain,
    first_shift,
    w_query,
    w_key,
    w_value,
    bias_query,
    bias_value,
    w_output,
    bias_output,
    second_gain,
    second_shift,
    w_up,
    bias_up,
    w_down,
    bias_down,
    cotangent,
):
    micro_count, own_rows, width = tokens.shape
    head_width = w_query.shape[1]
    vectors = jnp.stack(
        [bias_output, second_gain, second_shift, bias_down, first_gain, first_shift, bias_down, bias_down]
    )
    (
        queries,
        keys,
        values,
        inputs_low,
        w_projection,
        attended,
        lse,
        base,
        far_part,
        grad_attended,
        grad_output,
        sum_down,
        sums,
        sum_up,
        normed_all,
        grad_middle,
        grad_up,
    ) = feed_block(
        lengths,
        tokens,
        cotangent,
        w_query,
        w_key,
        w_value,
        w_output,
        w_up,
        w_down,
        vectors,
        bias_up.reshape(1, -1),
        bias_query.reshape(1, -1),
        bias_value.reshape(1, -1),
    )
    result, grad_tokens, grad_down, grad_up, grad_output, grad_query, grad_key, grad_value, shared, by_col = back_block(
        queries,
        keys,
        values,
        grad_attended,
        attended,
        lse,
        lengths,
        w_projection.reshape(width, 3 * head_width),
        inputs_low,
        grad_middle,
        base,
        far_part,
        sum_down,
        grad_up,
        grad_output,
        first_gain.reshape(1, width),
        sums,
        sum_up,
        normed_all,
    )
    return (
        result,
        grad_tokens,
        shared[0],
        shared[1],
        grad_query,
        grad_key,
        grad_value,
        by_col[1, :head_width],
        by_col[1, head_width : 2 * head_width],
        grad_output,
        shared[2],
        shared[3],
        shared[4],
        grad_up,
        by_col[0],
        grad_down,
        shared[5],
    )


def solution(mesh):
    return jax.shard_map(
        local_sequence if fits(mesh) else local_general,
        mesh=mesh,
        in_specs=(
            P(None, ("dp", "row", "col"), None),
            P("dp", None),
            P(),
            P(),
            P(("dp", "row"), "col"),
            P(("dp", "row"), "col"),
            P(("dp", "row"), "col"),
            P("col"),
            P("col"),
            P("col", ("dp", "row")),
            P(),
            P(),
            P(),
            P(("dp", "row"), "col"),
            P("col"),
            P("col", ("dp", "row")),
            P(),
            P(None, ("dp", "row", "col"), None),
        ),
        out_specs=(
            P(None, ("dp", "row", "col"), None),
            P(None, ("dp", "row", "col"), None),
            P(),
            P(),
            P(("dp", "row"), "col"),
            P(("dp", "row"), "col"),
            P(("dp", "row"), "col"),
            P("col"),
            P("col"),
            P("col", ("dp", "row")),
            P(),
            P(),
            P(),
            P(("dp", "row"), "col"),
            P("col"),
            P("col", ("dp", "row")),
            P(),
        ),
        check_vma=False,
    )
```

```python
import functools

import jax
import jax.numpy as jnp
from jax import lax
from jax.experimental import pallas as pl
from jax.experimental.pallas import tpu as pltpu
from jax.sharding import PartitionSpec as P

HD = 64


EPSILON = 1e-05
MASKED = -1e30


def layer_norm(values, norm_gain, norm_shift):
    centered = values - jnp.mean(values, axis=-1, keepdims=True)
    variance = jnp.mean(centered * centered, axis=-1, keepdims=True)
    return centered * lax.rsqrt(variance + EPSILON) * norm_gain + norm_shift


def gelu_tanh(values):
    return jax.nn.gelu(values, approximate=True)


def product(former, latter):
    return jnp.dot(former, latter, preferred_element_type=jnp.float32)


def transposed_left(former, latter):
    return lax.dot_general(
        former, latter, (((0,), (0,)), ((), ())), preferred_element_type=jnp.float32
    )


def transposed_right(former, latter):
    return lax.dot_general(
        former, latter, (((1,), (1,)), ((), ())), preferred_element_type=jnp.float32
    )


def spread_rows(rows_block):
    return lax.all_gather(rows_block, "col", axis=0, tiled=True)


def fold_rows(partial_sum):
    return lax.psum_scatter(partial_sum, "col", scatter_dimension=0, tiled=True)


def fetch_weights(w_query, w_key, w_value, w_up, w_output, w_down):
    leading = (
        lax.all_gather(w_query, ("dp", "row"), axis=0, tiled=True),
        lax.all_gather(w_key, ("dp", "row"), axis=0, tiled=True),
        lax.all_gather(w_value, ("dp", "row"), axis=0, tiled=True),
        lax.all_gather(w_up, ("dp", "row"), axis=0, tiled=True),
    )
    trailing = (
        lax.all_gather(w_output, ("dp", "row"), axis=1, tiled=True),
        lax.all_gather(w_down, ("dp", "row"), axis=1, tiled=True),
    )
    return tuple(leading) + tuple(trailing)


def reduce_blocks(gradients):
    leading = (
        lax.psum_scatter(gradients[0], ("dp", "row"), scatter_dimension=0, tiled=True),
        lax.psum_scatter(gradients[1], ("dp", "row"), scatter_dimension=0, tiled=True),
        lax.psum_scatter(gradients[2], ("dp", "row"), scatter_dimension=0, tiled=True),
        lax.psum_scatter(gradients[3], ("dp", "row"), scatter_dimension=0, tiled=True),
    )
    trailing = (
        lax.psum_scatter(gradients[4], ("dp", "row"), scatter_dimension=1, tiled=True),
        lax.psum_scatter(gradients[5], ("dp", "row"), scatter_dimension=1, tiled=True),
    )
    return tuple(leading) + tuple(trailing)


def heads_of(rows_block):
    return rows_block.reshape(rows_block.shape[0], -1, HD)


def block_of(rows_all, start, block_rows):
    return heads_of(lax.dynamic_slice_in_dim(rows_all, start, block_rows, 0))


def block_scores(query_heads, key_heads, query_start, key_start, length):
    block_rows = query_heads.shape[0]
    scores = jnp.einsum(
        "qhd,khd->hqk", query_heads, key_heads, preferred_element_type=jnp.float32
    ) * HD ** (-0.5)
    query_pos = query_start + jnp.arange(block_rows, dtype=jnp.int32)
    key_pos = key_start + jnp.arange(key_heads.shape[0], dtype=jnp.int32)
    allowed = (key_pos[None, :] <= query_pos[:, None]) & (key_pos[None, :] < length)
    return jnp.where(allowed[None], scores, MASKED)


def key_block_count(row_place, length, block_rows):
    return jnp.minimum(row_place + 1, (length + block_rows - 1) // block_rows)


def attention_forward(queries, key_rows, value_rows, row_place, length):
    block_rows = queries.shape[0]
    query_heads = heads_of(queries)
    head_count = query_heads.shape[1]
    query_start = row_place * block_rows
    count = key_block_count(row_place, length, block_rows)

    def stats_step(block_index, carry):
        highest, partition = carry
        start = block_index * block_rows
        scores = block_scores(
            query_heads, block_of(key_rows, start, block_rows), query_start, start, length
        )
        newest = jnp.maximum(highest, jnp.max(scores, axis=-1, keepdims=True))
        partition = partition * jnp.exp(highest - newest) + jnp.sum(
            jnp.exp(scores - newest), axis=-1, keepdims=True
        )
        return (newest, partition)

    start_stats = (
        jnp.full((head_count, block_rows, 1), MASKED, jnp.float32),
        jnp.zeros((head_count, block_rows, 1), jnp.float32),
    )
    highest, partition = lax.fori_loop(0, count, stats_step, start_stats)

    def output_step(block_index, total):
        start = block_index * block_rows
        scores = block_scores(
            query_heads, block_of(key_rows, start, block_rows), query_start, start, length
        )
        weights_low = (jnp.exp(scores - highest) / partition).astype(jnp.bfloat16)
        return total + jnp.einsum(
            "hqk,khd->qhd",
            weights_low,
            block_of(value_rows, start, block_rows),
            preferred_element_type=jnp.float32,
        )

    total = lax.fori_loop(0, count, output_step, jnp.zeros(query_heads.shape, jnp.float32))
    return (total.reshape(block_rows, -1), highest, partition)


def attention_query_side(
    queries, key_rows, value_rows, grad_attended, highest, partition, row_place, length
):
    block_rows = queries.shape[0]
    seq_rows = key_rows.shape[0]
    query_heads = heads_of(queries)
    grad_heads = heads_of(grad_attended)
    head_count = query_heads.shape[1]
    query_start = row_place * block_rows
    count = key_block_count(row_place, length, block_rows)

    def inner_step(block_index, total):
        start = block_index * block_rows
        scores = block_scores(
            query_heads, block_of(key_rows, start, block_rows), query_start, start, length
        )
        weights = jnp.exp(scores - highest) / partition
        grad_weights = jnp.einsum(
            "qhd,khd->hqk",
            grad_heads,
            block_of(value_rows, start, block_rows),
            preferred_element_type=jnp.float32,
        )
        return total + jnp.sum(weights * grad_weights, axis=-1, keepdims=True)

    inner = lax.fori_loop(0, count, inner_step, jnp.zeros((head_count, block_rows, 1), jnp.float32))

    def grad_step(block_index, carry):
        start = block_index * block_rows
        key_heads = block_of(key_rows, start, block_rows)
        scores = block_scores(query_heads, key_heads, query_start, start, length)
        weights = jnp.exp(scores - highest) / partition
        grad_weights = jnp.einsum(
            "qhd,khd->hqk",
            grad_heads,
            block_of(value_rows, start, block_rows),
            preferred_element_type=jnp.float32,
        )
        grad_scores = (weights * (grad_weights - inner)).astype(jnp.bfloat16)
        query_total = carry[0] + jnp.einsum(
            "hqk,khd->qhd", grad_scores, key_heads, preferred_element_type=jnp.float32
        )
        weights_low = weights.astype(jnp.bfloat16)
        key_part = jnp.einsum(
            "hqk,qhd->khd", grad_scores, query_heads, preferred_element_type=jnp.float32
        )
        value_part = jnp.einsum(
            "hqk,qhd->khd", weights_low, grad_heads, preferred_element_type=jnp.float32
        )
        key_total = lax.dynamic_update_slice_in_dim(
            carry[1], lax.dynamic_slice_in_dim(carry[1], start, block_rows, 0) + key_part, start, 0
        )
        value_total = lax.dynamic_update_slice_in_dim(
            carry[2],
            lax.dynamic_slice_in_dim(carry[2], start, block_rows, 0) + value_part,
            start,
            0,
        )
        return (query_total, key_total, value_total)

    start_carry = (jnp.zeros(query_heads.shape, jnp.float32),)
    start_carry = start_carry + (
        jnp.zeros((seq_rows, head_count, HD), jnp.float32),
        jnp.zeros((seq_rows, head_count, HD), jnp.float32),
    )
    totals = lax.fori_loop(0, count, grad_step, start_carry)
    query_terms = totals[0].reshape(block_rows, -1) * HD ** (-0.5)
    return (
        query_terms,
        totals[1].reshape(seq_rows, -1) * HD ** (-0.5),
        totals[2].reshape(seq_rows, -1),
        inner,
    )


def local_general(
    tokens,
    lengths,
    first_gain,
    first_shift,
    w_query,
    w_key,
    w_value,
    bias_query,
    bias_value,
    w_output,
    bias_output,
    second_gain,
    second_shift,
    w_up,
    bias_up,
    w_down,
    bias_down,
    cotangent,
):
    micro_count, own_rows, width = tokens.shape
    col_count = lax.axis_size("col")
    group_rows = own_rows * col_count
    row_place = lax.axis_index("row")
    col_place = lax.axis_index("col")
    head_width = w_query.shape[1]
    hidden_width = w_up.shape[1]
    own_positions = (
        row_place * group_rows + col_place * own_rows + jnp.arange(own_rows, dtype=jnp.int32)
    )
    weight_totals = (
        jnp.zeros((width, head_width), jnp.float32),
        jnp.zeros((width, head_width), jnp.float32),
        jnp.zeros((width, head_width), jnp.float32),
        jnp.zeros((width, hidden_width), jnp.float32),
        jnp.zeros((head_width, width), jnp.float32),
        jnp.zeros((hidden_width, width), jnp.float32),
    )
    vector_totals = (
        jnp.zeros((width,), jnp.float32),
        jnp.zeros((width,), jnp.float32),
        jnp.zeros((head_width,), jnp.float32),
        jnp.zeros((head_width,), jnp.float32),
        jnp.zeros((width,), jnp.float32),
        jnp.zeros((width,), jnp.float32),
        jnp.zeros((width,), jnp.float32),
        jnp.zeros((hidden_width,), jnp.float32),
        jnp.zeros((width,), jnp.float32),
    )
    results = []
    input_grads = []
    for micro_index in range(micro_count):
        gathered = fetch_weights(w_query, w_key, w_value, w_up, w_output, w_down)
        query_full, key_full, value_full, up_full, output_full, down_full = gathered
        length = lengths[0, micro_index]
        inputs = tokens[micro_index].astype(jnp.float32)
        normed = layer_norm(inputs, first_gain, first_shift).astype(jnp.bfloat16)
        normed_all = spread_rows(normed)
        queries = (product(normed_all, query_full) + bias_query).astype(jnp.bfloat16)
        keys_local = product(normed_all, key_full).astype(jnp.bfloat16)
        values_local = (product(normed_all, value_full) + bias_value).astype(jnp.bfloat16)
        keys_all, values_all = (
            lax.all_gather(keys_local, "row", axis=0, tiled=True),
            lax.all_gather(values_local, "row", axis=0, tiled=True),
        )
        attended, maxima, partitions = attention_forward(
            queries, keys_all, values_all, row_place, length
        )
        attended_low = attended.astype(jnp.bfloat16)
        branch = fold_rows(product(attended_low, output_full)) + bias_output
        middle = inputs + branch
        second_normed = layer_norm(middle, second_gain, second_shift).astype(jnp.bfloat16)
        second_all = spread_rows(second_normed)
        pre_activation = product(second_all, up_full) + bias_up
        activated = gelu_tanh(pre_activation).astype(jnp.bfloat16)
        result = middle + (fold_rows(product(activated, down_full)) + bias_down)
        results.append(result.astype(jnp.bfloat16))
        query_full, key_full, value_full, up_full, output_full, down_full = fetch_weights(
            w_query, w_key, w_value, w_up, w_output, w_down
        )
        validity = (own_positions < length).astype(jnp.float32)
        grad_result = cotangent[micro_index].astype(jnp.float32) * validity[:, None]
        grad_result_all = spread_rows(grad_result.astype(jnp.bfloat16))
        grad_down = transposed_left(activated, grad_result_all)
        grad_activated = transposed_right(grad_result_all, down_full)
        gelu_back = jax.vjp(gelu_tanh, pre_activation)[1]
        grad_pre = gelu_back(grad_activated)[0].astype(jnp.bfloat16)
        grad_up = transposed_left(second_all, grad_pre)
        grad_second_normed = fold_rows(transposed_right(grad_pre, up_full))
        second_back = jax.vjp(layer_norm, middle, second_gain, second_shift)[1]
        grad_middle_norm, grad_second_gain, grad_second_shift = second_back(grad_second_normed)
        grad_middle = grad_result + grad_middle_norm
        grad_branch = grad_middle.astype(jnp.bfloat16)
        grad_branch_all = spread_rows(grad_branch)
        grad_output = transposed_left(attended_low, grad_branch_all)
        grad_attended = transposed_right(grad_branch_all, output_full).astype(jnp.bfloat16)
        query_terms, key_terms, value_terms, inner = attention_query_side(
            queries, keys_all, values_all, grad_attended, maxima, partitions, row_place, length
        )
        key_sums, value_sums = (
            lax.psum_scatter(key_terms, "row", scatter_dimension=0, tiled=True),
            lax.psum_scatter(value_terms, "row", scatter_dimension=0, tiled=True),
        )
        grad_queries = query_terms.astype(jnp.bfloat16)
        grad_keys = key_sums.astype(jnp.bfloat16)
        grad_values = value_sums.astype(jnp.bfloat16)
        grad_query = transposed_left(normed_all, grad_queries)
        grad_key = transposed_left(normed_all, grad_keys)
        grad_value = transposed_left(normed_all, grad_values)
        grad_normed = fold_rows(
            transposed_right(grad_queries, query_full)
            + transposed_right(grad_keys, key_full)
            + transposed_right(grad_values, value_full)
        )
        first_back = jax.vjp(layer_norm, inputs, first_gain, first_shift)[1]
        grad_inputs_norm, grad_first_gain, grad_first_shift = first_back(grad_normed)
        input_grads.append((grad_middle + grad_inputs_norm).astype(jnp.bfloat16))
        local_grads = (grad_query, grad_key, grad_value, grad_up, grad_output, grad_down)
        weight_totals = tuple(
            (former + latter for former, latter in zip(weight_totals, local_grads))
        )
        local_vectors = (
            grad_first_gain,
            grad_first_shift,
            jnp.sum(grad_queries.astype(jnp.float32), axis=0),
            jnp.sum(grad_values.astype(jnp.float32), axis=0),
            jnp.sum(grad_branch.astype(jnp.float32), axis=0),
            grad_second_gain,
            grad_second_shift,
            jnp.sum(grad_pre.astype(jnp.float32), axis=0),
            jnp.sum(grad_result, axis=0),
        )
        vector_totals = tuple(
            (former + latter for former, latter in zip(vector_totals, local_vectors))
        )
    weight_totals = reduce_blocks(weight_totals)

    def widen(vector_part):
        blank = jnp.zeros((vector_part.shape[0] * col_count,), jnp.float32)
        return lax.dynamic_update_slice(blank, vector_part, (col_place * vector_part.shape[0],))

    def narrow(whole_vector, piece_width):
        return lax.dynamic_slice_in_dim(whole_vector, col_place * piece_width, piece_width)

    (
        sum_first_gain,
        sum_first_shift,
        sum_bias_query,
        sum_bias_value,
        sum_bias_output,
        sum_second_gain,
        sum_second_shift,
        sum_bias_up,
        sum_bias_down,
    ) = lax.psum(
        (
            vector_totals[0],
            vector_totals[1],
            widen(vector_totals[2]),
            widen(vector_totals[3]),
            vector_totals[4],
            vector_totals[5],
            vector_totals[6],
            widen(vector_totals[7]),
            vector_totals[8],
        ),
        ("dp", "row", "col"),
    )
    grad_w_query, grad_w_key, grad_w_value, grad_w_up, grad_w_output, grad_w_down = weight_totals
    return (
        jnp.stack(results, axis=0),
        jnp.stack(input_grads, axis=0),
        sum_first_gain,
        sum_first_shift,
        grad_w_query,
        grad_w_key,
        grad_w_value,
        narrow(sum_bias_query, head_width),
        narrow(sum_bias_value, head_width),
        grad_w_output,
        sum_bias_output,
        sum_second_gain,
        sum_second_shift,
        grad_w_up,
        narrow(sum_bias_up, hidden_width),
        grad_w_down,
        sum_bias_down,
    )


F32 = jnp.float32
LOW = jnp.bfloat16
VMEM_LIMIT = 56 * 1024 * 1024


def fits(mesh):
    return mesh.shape["row"] == 4 and mesh.shape["col"] == 4 and mesh.shape["dp"] == 2


def contract(former, latter, former_dim, latter_dim):
    return lax.dot_general(
        former,
        latter,
        (((former_dim,), (latter_dim,)), ((), ())),
        preferred_element_type=jnp.float32,
    )


def norm_parts(values):
    centered = values - jnp.mean(values, axis=-1, keepdims=True)
    scale = lax.rsqrt(jnp.mean(centered * centered, axis=-1, keepdims=True) + EPSILON)
    return centered * scale, scale


def norm_back(grads, gain, unit, scale):
    inner = grads * gain
    mean_inner = jnp.mean(inner, axis=-1, keepdims=True)
    mean_unit = jnp.mean(inner * unit, axis=-1, keepdims=True)
    return scale * (inner - mean_inner - unit * mean_unit)


GELU_SCALE = 0.7978845608028654
GELU_CUBE = 0.044715


def gelu_parts(values):
    square = values * values
    curve = jnp.tanh(GELU_SCALE * values * (1.0 + GELU_CUBE * square))
    half = 0.5 + 0.5 * curve
    slope = half + 0.5 * values * (1.0 - curve * curve) * (GELU_SCALE * (1.0 + 3.0 * GELU_CUBE * square))
    return values * half, slope


def peers():
    place = lax.axis_index("col")
    return {"col": place + 1 - 2 * (place % 2)}, {"col": (place + 2) % 4}


def remote(source, target, send_sem, recv_sem, device):
    return pltpu.make_async_remote_copy(
        src_ref=source,
        dst_ref=target,
        send_sem=send_sem,
        recv_sem=recv_sem,
        device_id=device,
        device_id_type=pl.DeviceIdType.MESH,
    )


def row_peers():
    row = lax.axis_index("row")
    return row + 1 - 2 * (row % 2), (row + 2) % 4, 3 - row


def greet_all(core, far):
    row = lax.axis_index("row")
    cross = {"dp": 1 - lax.axis_index("dp")}
    barrier = pltpu.get_barrier_semaphore()
    rows = [{"row": (row + step) % 4} for step in (1, 2, 3)]
    for device in [core, far, cross] + rows:
        pl.semaphore_signal(barrier, inc=1, device_id=device, device_id_type=pl.DeviceIdType.MESH)
    pl.semaphore_wait(barrier, 6)


class Gather:
    def __init__(self, slot, z_send, z_recv, x_send, x_recv):
        self.slot, self.z_send, self.z_recv, self.x_send, self.x_recv = slot, z_send, z_recv, x_send, x_recv
        self.row, self.dp = lax.axis_index("row"), lax.axis_index("dp")

    def lane(self, d):
        if d == 0:
            return self.row, {"row": jnp.minimum(self.row + 1, 3)}
        return 3 - self.row, {"row": jnp.maximum(self.row - 1, 0)}

    def z_copy(self, d, k, block):
        view = self.slot(self.dp * 4 + block)
        return remote(view, view, self.z_send.at[d, k], self.z_recv.at[d, k], self.lane(d)[1])

    def x_copy(self, block):
        view = self.slot(self.dp * 4 + block)
        return remote(view, view, self.x_send.at[block], self.x_recv.at[block], {"dp": 1 - self.dp})

    def pump(self, k):
        for d in range(2):
            place, _ = self.lane(d)
            block = self.row - k if d == 0 else self.row + k
            if k == 0:
                if d == 0:
                    self.x_copy(block).start()

                @pl.when(place <= 2)
                def _():
                    self.z_copy(d, 0, block).start()
            else:

                @pl.when(place >= k)
                def _():
                    self.z_copy(d, k - 1, block).wait_recv()
                    if k < 3:

                        @pl.when(place <= 2)
                        def _():
                            self.z_copy(d, k, block).start()

                    self.x_copy(block).start()

    def arrive(self):
        for block in range(4):
            view = self.slot((1 - self.dp) * 4 + block)
            remote(view, view, self.x_send.at[block], self.x_recv.at[block], {"dp": 1 - self.dp}).wait_recv()

    def sent(self):
        for block in range(4):
            self.x_copy(block).wait_send()
        for d in range(2):
            place, _ = self.lane(d)
            for k in range(3):

                @pl.when((place >= k) & (place <= 2))
                def _():
                    self.z_copy(d, k, self.row - k if d == 0 else self.row + k).wait_send()


class Spread:
    def __init__(self, source, target, trade_send, trade_recv, send, recv):
        self.source, self.target = source, target
        self.trade_send, self.trade_recv, self.send, self.recv = trade_send, trade_recv, send, recv
        self.core, self.far = peers()
        self.row = lax.axis_index("row")

    def trade_copy(self, place):
        return remote(
            self.source.at[place],
            self.target.at[self.row, 0],
            self.trade_send.at[place],
            self.trade_recv.at[self.row],
            {"row": place},
        )

    def trade(self):
        for place in row_peers():
            self.trade_copy(place).start()

    def traded(self):
        for place in row_peers():
            self.trade_copy(place).wait_send()

    def hop(self, step, r):
        source, target, device = ((0, 1, self.core), (0, 2, self.far), (2, 3, self.core))[step]
        return remote(
            self.target.at[r, source], self.target.at[r, target], self.send.at[step, r], self.recv.at[step, r], device
        )

    def arrive(self, r):
        remote(
            self.source.at[r], self.target.at[r, 0], self.trade_send.at[r], self.trade_recv.at[r], {"row": r}
        ).wait_recv()

    def first(self, r):
        self.hop(1, r).start()
        self.hop(0, r).start()

    def relay(self, r):
        self.hop(1, r).wait()
        self.hop(2, r).start()

    def done(self, r):
        self.hop(0, r).wait()
        self.hop(2, r).wait()


class Reduce:
    def __init__(self, grads, sums, moving, x_send, x_recv, z_send, z_recv):
        self.grads, self.sums, self.moving = grads, sums, moving
        self.x_send, self.x_recv, self.z_send, self.z_recv = x_send, x_recv, z_send, z_recv
        self.row, self.dp = lax.axis_index("row"), lax.axis_index("dp")

    def x_copy(self):
        half = self.grads.at[pl.ds((1 - self.dp) * 4, 4)]
        return remote(half, self.sums, self.x_send, self.x_recv, {"dp": 1 - self.dp})

    def start(self):
        self.x_copy().start()

    def add(self):
        self.x_copy().wait()
        for b in range(4):
            self.sums[b] = (self.sums[b].astype(F32) + self.grads[self.dp * 4 + b].astype(F32)).astype(LOW)

    def lane(self, d):
        if d == 0:
            return self.row, {"row": jnp.minimum(self.row + 1, 3)}
        return 3 - self.row, {"row": jnp.maximum(self.row - 1, 0)}

    def z_copy(self, d, k, source):
        return remote(source, self.moving.at[d, k], self.z_send.at[d, k], self.z_recv.at[d, k], self.lane(d)[1])

    def pump(self, k):
        for d in range(2):
            place, _ = self.lane(d)

            @pl.when(place == 0)
            def _():
                self.z_copy(d, k, self.sums.at[3 - k if d == 0 else k]).start()

            if k >= 1:

                @pl.when((place >= 1) & (place <= k))
                def _():
                    block = 3 - k + place if d == 0 else k - place
                    self.z_copy(d, k - 1, self.sums.at[0]).wait_recv()
                    self.moving[d, k - 1] = (
                        self.moving[d, k - 1].astype(F32) + self.sums[block].astype(F32)
                    ).astype(LOW)
                    self.z_copy(d, k, self.moving.at[d, k - 1]).start()

    def finish(self, out):
        out[...] = self.sums[self.row].astype(F32)
        for d in range(2):
            place, _ = self.lane(d)

            @pl.when(place >= 1)
            def _():
                self.z_copy(d, 2, self.sums.at[0]).wait_recv()
                out[...] += self.moving[d, 2].astype(F32)

            for k in range(3):

                @pl.when(place <= k)
                def _():
                    self.z_copy(d, k, self.sums.at[0]).wait_send()


def positions_row(shape, place):
    own = shape // 4
    lane = lax.broadcasted_iota(jnp.int32, (1, own), 1)
    places = (place, place + 1 - 2 * (place % 2), (place + 2) % 4, 3 - place)
    return jnp.concatenate([lane + other * own for other in places], axis=1)


def positions_column(shape, place):
    own = shape // 4
    line = lax.broadcasted_iota(jnp.int32, (own, 1), 0)
    places = (place, place + 1 - 2 * (place % 2), (place + 2) % 4, 3 - place)
    return jnp.concatenate([line + other * own for other in places], axis=0)


def feed_kernel(
    lengths_ref,
    tokens_ref,
    cot_ref,
    wq_ref,
    wk_ref,
    wv_ref,
    wo_shard,
    wu_shard,
    wd_shard,
    vec_ref,
    bias_up_ref,
    bias_q_ref,
    bias_v_ref,
    q_ref,
    k_ref,
    v_ref,
    tok_ref,
    proj_out,
    att_ref,
    lse_ref,
    middle,
    far_out_q,
    gatt_ref,
    gout_ref,
    x_down,
    sums_ref,
    sum_up_ref,
    normed_out,
    gmid_ref,
    gup_ref,
    wo_ref,
    wu_all,
    wd_ref,
    g_all,
    kept,
    kept_q,
    core_out,
    core_in,
    core_in_q,
    far_out,
    far_in,
    second,
    act,
    gpre,
    branch,
    key_bias,
    causal,
    gdown,
    stage_sems,
    send_sems,
    recv_sems,
    trade_send,
    trade_recv,
    row_send,
    row_recv,
    grad_send,
    grad_recv,
    g_send,
    g_recv,
    za_send,
    za_recv,
    xa_send,
    xa_recv,
    zo_send,
    zo_recv,
    xo_send,
    xo_recv,
    zu_send,
    zu_recv,
    xu_send,
    xu_recv,
    zd_send,
    zd_recv,
    xd_send,
    xd_recv,
    rx_send,
    rx_recv,
    out_sems,
    load_sems,
):
    chunks, blocks, own, width = second.shape
    rows = blocks * own
    hidden = wu_all.shape[2]
    core, far = peers()
    row = lax.axis_index("row")
    mine = lax.axis_index("dp") * 4 + row
    wu_ref = wu_all.reshape(width, hidden)

    def wd_slot(block):
        return wd_ref.at[:, pl.ds(pl.multiple_of(block * own, own), own)]

    down = Gather(wd_slot, zd_send, zd_recv, xd_send, xd_recv)
    near, halfway, distant = row_peers()
    head_width = wq_ref.shape[1]
    rows_all = branch
    normed = gpre.reshape(chunks * rows, width)

    def wo_slot(block):
        return wo_ref.at[:, pl.ds(pl.multiple_of(block * own, own), own)]

    up = Gather(lambda block: wu_all.at[block], zu_send, zu_recv, xu_send, xu_recv)
    output = Gather(wo_slot, zo_send, zo_recv, xo_send, xo_recv)
    spread = Spread(tokens_ref, rows_all, trade_send, trade_recv, row_send, row_recv)
    cots = Spread(cot_ref, g_all, grad_send, grad_recv, g_send, g_recv)
    projs = [
        Gather(
            lambda block, n=n: proj_out.at[block, :, n * head_width : (n + 1) * head_width],
            za_send.at[n],
            za_recv.at[n],
            xa_send.at[n],
            xa_recv.at[n],
        )
        for n in range(3)
    ]
    loads = [
        pltpu.make_async_copy(source, target, load_sems.at[n])
        for n, (source, target) in enumerate(
            (
                (wq_ref, projs[0].slot(mine)),
                (wk_ref, projs[1].slot(mine)),
                (wv_ref, projs[2].slot(mine)),
                (tokens_ref.at[row], rows_all.at[row, 0]),
                (cot_ref.at[row], g_all.at[row, 0]),
                (wo_shard, wo_slot(mine)),
                (wu_shard, wu_all.at[mine]),
                (wd_shard, wd_slot(mine)),
            )
        )
    ]
    for load in loads:
        load.start()
    reduces = [
        Reduce(gdown.at[h], x_down.at[h], None, rx_send.at[h], rx_recv.at[h], None, None)
        for h in range(2)
    ]
    place = lax.axis_index("col")
    length = lengths_ref[0, row]
    key_row, query_column = positions_row(rows, place), positions_column(rows, place)
    causal[...] = jnp.where(key_row <= query_column, 0.0, MASKED).astype(LOW)
    for r in range(chunks):
        key_bias[:, r * rows : (r + 1) * rows] = jnp.where(key_row + r * rows < length, 0.0, MASKED)

    def core_copy(step, r, source, target):
        return remote(source.at[r], target.at[r], send_sems.at[step, r], recv_sems.at[step, r], core)

    def far_copy(step, r, source, target):
        return remote(source.at[r], target.at[r], send_sems.at[step, r], recv_sems.at[step, r], far)

    def spread_core(step, r, rows_ref):
        return remote(rows_ref.at[r, 0], rows_ref.at[r, 1], send_sems.at[step, r], recv_sems.at[step, r], core)

    def spread_far(step, r, rows_ref):
        return remote(rows_ref.at[r, 0], rows_ref.at[r, 2], send_sems.at[step, r], recv_sems.at[step, r], far)

    def spread_relay(step, r, rows_ref):
        return remote(rows_ref.at[r, 2], rows_ref.at[r, 3], send_sems.at[step, r], recv_sems.at[step, r], core)

    def split(r, total, kept_ref, out_ref):
        kept_ref[r, 0] = total[:own].astype(kept_ref.dtype)
        out_ref[r, 0] = total[own : 2 * own].astype(LOW)
        kept_ref[r, 1] = total[2 * own : 3 * own].astype(kept_ref.dtype)
        out_ref[r, 1] = total[3 * own :].astype(LOW)

    def fold(r, kept_ref, in_ref, out_ref):
        out_ref[r] = (kept_ref[r, 1].astype(F32) + in_ref[r, 1].astype(F32)).astype(LOW)
        kept_ref[r, 0] = (kept_ref[r, 0].astype(F32) + in_ref[r, 0].astype(F32)).astype(kept_ref.dtype)

    def each(body):
        lax.fori_loop(0, chunks, lambda r, carry: (body(r), carry)[1], 0)

    def out_projection(r):
        split(r, contract(att_ref[r * rows : (r + 1) * rows], wo_ref[...], 1, 0), kept, core_out)
        core_copy(0, r, core_out, core_in).start()

    def out_fold(r):
        core_copy(0, r, core_out, core_in).wait()
        fold(r, kept, core_in, far_out)
        far_copy(1, r, far_out, far_in).start()

    block = 256
    lane = lax.broadcasted_iota(jnp.int32, (block, 128), 1)

    def attention(r):
        long = (r + 1) * rows

        def part(step, carry):
            here = pl.ds(pl.multiple_of(r * rows + (step % 2) * block, block), block)
            pair = pl.ds(pl.multiple_of((step // 2) * 128, 128), 128)
            inside = pl.ds(pl.multiple_of((step % 2) * block, block), block)
            queries = q_ref[here, pair]
            parts = []
            for head in range(2):
                masked = jnp.where((lane // HD) == head, queries, 0) * jnp.asarray(HD**-0.5, LOW)
                scores = contract(masked, k_ref[:long, pair], 1, 1) + key_bias[:, :long]
                last = scores[:, long - rows :] + causal[inside].astype(F32)
                scores = last if r == 0 else jnp.concatenate([scores[:, : long - rows], last], axis=1)
                highest = jnp.max(scores, axis=1, keepdims=True)
                weights = jnp.exp(scores - highest)
                total = jnp.sum(weights, axis=1, keepdims=True)
                parts.append(contract(weights.astype(LOW), v_ref[:long, pair], 1, 0) / total)
                flat = jnp.broadcast_to(highest + jnp.log(total), (block, 128))
                lse_ref[step // 2, r, head : head + 1, inside] = flat.T[:1]
            att_ref[here, pair] = jnp.where(lane < HD, parts[0], parts[1]).astype(LOW)
            return carry

        lax.fori_loop(0, 4, part, 0)

    def norm(r):
        far_copy(1, r, far_out, far_in).wait()
        values = tok_ref[r].astype(F32) + (kept[r, 0] + far_in[r].astype(F32) + vec_ref[0:1])
        middle[r] = values
        second[r, 0] = (norm_parts(values)[0] * vec_ref[1:2] + vec_ref[2:3]).astype(LOW)
        spread_core(2, r, second).start()
        spread_far(3, r, second).start()

    def norm(r):
        far_copy(1, r, far_out, far_in).wait()
        values = tok_ref[r].astype(F32) + (kept[r, 0] + far_in[r].astype(F32) + vec_ref[0:1])
        middle[r] = values
        second[r, 0] = (norm_parts(values)[0] * vec_ref[1:2] + vec_ref[2:3]).astype(LOW)
        spread_core(2, r, second).start()
        spread_far(3, r, second).start()

    def pump(step):
        for proj in projs:
            proj.pump(step)

    def give_cot(r):
        line = lax.broadcasted_iota(jnp.int32, (own, width), 0) + (r * rows + place * own)
        g_all[r, 0] = jnp.where(line < length, g_all[r, 0], jnp.zeros((), LOW))
        cots.first(r)

    def norm_rows(r):
        spread.done(r)
        here = pl.ds(pl.multiple_of(r * rows, rows), rows)
        values = rows_all[r].reshape(rows, width).astype(F32)
        low = (norm_parts(values)[0] * vec_ref[4:5] + vec_ref[5:6]).astype(LOW)
        gpre[r] = low.reshape(blocks, own, width)
        pltpu.make_async_copy(normed.at[here], normed_out.at[here], out_sems.at[r]).start()
        tok_ref[r] = rows_all[r, 0]

    def project(r):
        here = pl.ds(pl.multiple_of(r * rows, rows), rows)
        total = contract(normed[here], proj_out.reshape(8 * own, 3 * head_width)[...], 1, 0)
        q_ref[here] = (total[:, :head_width] + bias_q_ref[...]).astype(LOW)
        k_ref[here] = total[:, head_width : 2 * head_width].astype(LOW)
        v_ref[here] = (total[:, 2 * head_width :] + bias_v_ref[...]).astype(LOW)

    greet_all(core, far)
    for load in loads[:3]:
        load.wait()
    pump(0)
    spread.trade()
    loads[3].wait()
    spread.first(row)
    loads[4].wait()
    give_cot(row)
    for load in loads[5:]:
        load.wait()
    spread.arrive(near)
    spread.first(near)
    pump(1)
    spread.relay(row)
    cots.relay(row)
    norm_rows(row)
    spread.arrive(halfway)
    spread.first(halfway)
    spread.relay(near)
    spread.arrive(distant)
    spread.first(distant)
    output.pump(0)
    cots.trade()
    norm_rows(near)
    pump(2)
    spread.relay(halfway)
    norm_rows(halfway)
    spread.relay(distant)
    pump(3)
    output.pump(1)
    norm_rows(distant)
    for proj in projs:
        proj.arrive()
    each(project)
    up.pump(0)
    down.pump(0)
    output.pump(2)
    attention(0)
    output.pump(3)
    cots.arrive(near)
    give_cot(near)
    attention(1)
    output.arrive()
    out_projection(0)
    out_projection(1)
    out_fold(0)
    cots.relay(near)
    attention(2)
    out_projection(2)
    out_fold(1)
    norm(0)
    up.pump(1)
    down.pump(1)
    cots.arrive(halfway)
    give_cot(halfway)
    attention(3)
    out_projection(3)
    out_fold(2)
    norm(1)
    out_fold(3)
    cots.arrive(distant)
    give_cot(distant)
    up.pump(2)
    norm(2)
    cots.relay(halfway)
    down.pump(2)
    up.pump(3)
    down.pump(3)
    cots.relay(distant)
    for r in range(chunks):
        here = slice(r * rows, (r + 1) * rows)
        pltpu.make_async_copy(normed.at[here], normed_out.at[here], out_sems.at[r]).wait()
    up.arrive()
    down.arrive()

    sum_up_ref[...] = jnp.zeros_like(sum_up_ref)

    def relay_start(r):
        spread_far(3, r, second).wait()
        spread_relay(4, r, second).start()

    def feed(r):
        spread_core(2, r, second).wait()
        spread_relay(4, r, second).wait()
        cots.done(r)
        pre = contract(second[r].reshape(rows, width), wu_ref[...], 1, 0) + bias_up_ref[...]
        activated, slope = gelu_parts(pre)
        act[r] = activated.astype(LOW).reshape(blocks, own, hidden)
        grads = contract(g_all[r].reshape(rows, width), wd_ref[...], 1, 1) * slope
        grads_low = grads.astype(LOW)
        gpre[r] = grads_low.reshape(blocks, own, hidden)
        sum_up_ref[...] += jnp.sum(grads_low.astype(F32), axis=0, keepdims=True)
        split(r, contract(grads_low, wu_ref[...], 1, 1), kept, core_out)
        core_copy(5, r, core_out, core_in).start()
        total = contract(act[r].reshape(rows, hidden), wd_ref[...], 1, 0)
        core_copy(5, r, core_out, core_in).wait()
        fold(r, kept, core_in, far_out)
        far_copy(6, r, far_out, far_in).start()
        kept_q[r] = total[:own].astype(LOW)
        core_out[r, 0] = total[own : 2 * own].astype(LOW)
        far_out_q[r] = total[2 * own : 3 * own].astype(LOW)
        core_out[r, 1] = total[3 * own :].astype(LOW)
        core_copy(7, r, core_out, core_in_q).start()

    wide = 256
    flat_second = second.reshape(chunks * rows, width)
    flat_act = act.reshape(chunks * rows, hidden)
    flat_gpre = gpre.reshape(chunks * rows, hidden)
    flat_g = g_all.reshape(chunks * rows, width)
    flat_branch = branch.reshape(chunks * rows, width)

    def some(first, last, body):
        lax.fori_loop(first, last, lambda t, carry: (body(t), carry)[1], 0)

    def down_grad(t):
        part = pl.ds(pl.multiple_of(t * wide, wide), wide)
        here = pl.ds(pl.multiple_of((t % 2) * wide, wide), wide)
        total = contract(flat_act[:, part], flat_g[...], 0, 0).astype(LOW)
        for b in range(8):
            gdown[t // 2, b, here] = total[:, b * own : (b + 1) * own]

    sums_ref[...] = jnp.zeros_like(sums_ref)

    def norm_grad(r):
        far_copy(6, r, far_out, far_in).wait()
        grads = kept[r, 0] + far_in[r].astype(F32)
        unit, scale = norm_parts(middle[r])
        own_grads = g_all[r, 0].astype(F32)
        total = own_grads + norm_back(grads, vec_ref[1:2], unit, scale)
        low = total.astype(LOW)
        branch[r, 0] = low
        spread_core(9, r, branch).start()
        spread_far(10, r, branch).start()
        sums_ref[0:1] += jnp.sum(low.astype(F32), axis=0, keepdims=True)
        sums_ref[1:2] += jnp.sum(grads * unit, axis=0, keepdims=True)
        sums_ref[2:3] += jnp.sum(grads, axis=0, keepdims=True)
        sums_ref[3:4] += jnp.sum(own_grads, axis=0, keepdims=True)

    relay_start(0)
    feed(0)
    norm(3)
    relay_start(1)

    def step(r):
        feed(r)
        norm_grad(r - 1)

        @pl.when(r < chunks - 1)
        def _():
            relay_start(r + 1)

    some(1, chunks, step)
    some(0, 2, down_grad)
    reduces[0].start()
    some(2, 4, down_grad)
    reduces[1].start()
    norm_grad(chunks - 1)
    given = pltpu.make_async_copy(branch.at[:, 0], gmid_ref, stage_sems.at[0])
    given.start()

    def result_fold(r):
        core_copy(7, r, core_out, core_in_q).wait()
        far_out_q[r] = (far_out_q[r].astype(F32) + core_in_q[r, 1].astype(F32)).astype(LOW)
        own_part = kept_q[r].astype(F32) + core_in_q[r, 0].astype(F32)
        middle[r] = middle[r] + (own_part + vec_ref[3:4])

    each(result_fold)

    def late(r):
        spread_far(10, r, branch).wait()
        spread_relay(11, r, branch).start()
        part = pl.ds(pl.multiple_of(r * wide, wide), wide)
        total = contract(flat_second[:, part], flat_gpre[...], 0, 0).astype(LOW)
        for b in range(2):
            core_out[0, b] = total[b * own : (b + 1) * own]
        copy = pltpu.make_async_copy(core_out.at[0], gup_ref.at[pl.ds(2 * r, 2)], stage_sems.at[1])
        copy.start()
        spread_core(9, r, branch).wait()
        spread_relay(11, r, branch).wait()
        rows_here = pl.ds(pl.multiple_of(r * rows, rows), rows)
        gatt_ref[rows_here] = contract(branch[r].reshape(rows, width), wo_ref[...], 1, 1).astype(LOW)
        copy.wait()

    some(0, 4, late)
    total_out = contract(att_ref[...], flat_branch[...], 0, 0).astype(LOW)
    for b in range(8):
        gout_ref[b] = total_out[:, b * own : (b + 1) * own]
    for h in range(2):
        reduces[h].add()
    given.wait()
    spread.traded()
    cots.traded()
    for gather in projs + [output, up, down]:
        gather.sent()


def feed_block(
    lengths, tokens, cotangent, w_query, w_key, w_value, w_output, w_up, w_down, vectors, bias_up, bias_query, bias_value
):
    chunks, own, width = tokens.shape
    rows = chunks * 4 * own
    head_width = w_query.shape[1]
    hidden = w_up.shape[1]
    half = (chunks, 2, own, width)
    one = (chunks, own, width)
    all_rows = (chunks, 4, own, width)
    vmem = pl.BlockSpec(memory_space=pltpu.VMEM)
    hbm = pl.BlockSpec(memory_space=pl.ANY)
    dma = pltpu.SemaphoreType.DMA
    gather_sems = [dma((2, 3)), dma((2, 3)), dma((4,)), dma((4,))]
    spread_sems = [dma((4,)), dma((4,)), dma((3, 4)), dma((3, 4))]
    return pl.pallas_call(
        feed_kernel,
        in_specs=[pl.BlockSpec(memory_space=pltpu.SMEM)] + [hbm] * 8 + [vmem] * 4,
        out_specs=[vmem] * 14 + [hbm] * 3,
        out_shape=[
            jax.ShapeDtypeStruct((rows, head_width), LOW),
            jax.ShapeDtypeStruct((rows, head_width), LOW),
            jax.ShapeDtypeStruct((rows, head_width), LOW),
            jax.ShapeDtypeStruct(one, LOW),
            jax.ShapeDtypeStruct((8, own, 3 * head_width), LOW),
            jax.ShapeDtypeStruct((rows, head_width), LOW),
            jax.ShapeDtypeStruct((head_width // 128, chunks, 2, rows // chunks), F32),
            jax.ShapeDtypeStruct(one, F32),
            jax.ShapeDtypeStruct(one, LOW),
            jax.ShapeDtypeStruct((rows, head_width), LOW),
            jax.ShapeDtypeStruct((8, head_width, width // 8), LOW),
            jax.ShapeDtypeStruct((2, 4, hidden // 2, width // 8), LOW),
            jax.ShapeDtypeStruct((8, width), F32),
            jax.ShapeDtypeStruct((1, hidden), F32),
            jax.ShapeDtypeStruct((rows, width), LOW),
            jax.ShapeDtypeStruct(one, LOW),
            jax.ShapeDtypeStruct((8, width // 8, hidden), LOW),
        ],
        scratch_shapes=[
            pltpu.VMEM((head_width, width), LOW),
            pltpu.VMEM((8, own, hidden), LOW),
            pltpu.VMEM((hidden, width), LOW),
            pltpu.VMEM(all_rows, LOW),
            pltpu.VMEM(half, F32),
            pltpu.VMEM(one, LOW),
            pltpu.VMEM(half, LOW),
            pltpu.VMEM(half, LOW),
            pltpu.VMEM(half, LOW),
            pltpu.VMEM(one, LOW),
            pltpu.VMEM(one, LOW),
            pltpu.VMEM(all_rows, LOW),
            pltpu.VMEM((chunks, 4, own, hidden), LOW),
            pltpu.VMEM((chunks, 4, own, hidden), LOW),
            pltpu.VMEM(all_rows, LOW),
            pltpu.VMEM((1, rows), F32),
            pltpu.VMEM((rows // chunks, rows // chunks), LOW),
            pltpu.VMEM((2, 8, hidden // 2, width // 8), LOW),
            dma((2,)),
            dma((12, chunks)),
            dma((12, chunks)),
        ]
        + spread_sems
        + spread_sems
        + [dma((3, 2, 3)), dma((3, 2, 3)), dma((3, 4)), dma((3, 4))]
        + gather_sems
        + gather_sems
        + gather_sems
        + [dma((2,)), dma((2,)), dma((4,)), dma((8,))],
        compiler_params=pltpu.CompilerParams(
            collective_id=1, has_side_effects=True, vmem_limit_bytes=62 * 1024 * 1024
        ),
        cost_estimate=pl.CostEstimate(flops=100_000_000_000, bytes_accessed=30_000_000, transcendentals=0),
        name="feed_block",
    )(lengths, tokens, cotangent, w_query, w_key, w_value, w_output, w_up, w_down, vectors, bias_up, bias_query, bias_value)


def back_kernel(
    q_ref,
    k_ref,
    v_ref,
    do_ref,
    o_ref,
    lse_ref,
    lengths_ref,
    w_ref,
    tok_ref,
    gmid_ref,
    base_ref,
    far_q_ref,
    sum_down_ref,
    gup_ref,
    gout_ref,
    gain_ref,
    sums_ref,
    sum_up_ref,
    normed_ref,
    res_out,
    gtok_out,
    down_out,
    up_out,
    out_out,
    query_out,
    key_out,
    value_out,
    shared_out,
    by_col_out,
    dk_sum,
    dv_sum,
    dproj,
    gproj,
    kept,
    core_out,
    core_in,
    far_out,
    far_in,
    gtok,
    norm_tile,
    key_bias,
    causal,
    far_q_in,
    result,
    x_up,
    x_out,
    x_proj,
    z_down,
    z_up,
    z_out,
    z_proj,
    proj_sum,
    vec,
    vec_in,
    q_send,
    q_recv,
    res_send,
    res_recv,
    tok_send,
    tok_recv,
    fold_send,
    fold_recv,
    x_send,
    x_recv,
    z_send,
    z_recv,
    d_send,
    d_recv,
    vec_send,
    vec_recv,
    tile_sem,
):
    chunks, own, width = tok_ref.shape
    rows = 4 * own
    head_width = q_ref.shape[1]
    core, far = peers()
    row = lax.axis_index("row")
    dp = lax.axis_index("dp")
    cross = {"dp": 1 - dp}
    other = lambda r: {"row": r}
    quarters = own // 2

    def reduce_of(n, grads, sums, moving):
        return Reduce(grads, sums, moving, x_send.at[n], x_recv.at[n], z_send.at[n], z_recv.at[n])

    ups = [
        reduce_of(h, gup_ref.at[:, h * quarters : (h + 1) * quarters], x_up.at[h], z_up.at[h]) for h in range(2)
    ]
    outs = reduce_of(2, gout_ref, x_out, z_out)
    projs = [
        reduce_of(3 + p, gproj.at[p], x_proj.at[p], z_proj.at[p]) for p in range(2)
    ]
    downs = [
        Reduce(None, sum_down_ref.at[h], z_down.at[h], None, None, d_send.at[h], d_recv.at[h]) for h in range(2)
    ]
    place = lax.axis_index("col")
    length = lengths_ref[0, row]
    query_row, key_column = positions_row(rows, place), positions_column(rows, place)
    causal[...] = jnp.where(key_column <= query_row, 0.0, MASKED)
    for r in range(chunks):
        key_bias[r * rows : (r + 1) * rows] = jnp.where(key_column + r * rows < length, 0.0, MASKED)

    barrier = pltpu.get_barrier_semaphore()
    for device in (core, far, cross, other((row + 1) % 4), other((row + 2) % 4), other((row + 3) % 4)):
        pl.semaphore_signal(barrier, inc=1, device_id=device, device_id_type=pl.DeviceIdType.MESH)
    pl.semaphore_wait(barrier, 6)

    def trade(r, source, target, send, recv):
        return remote(source.at[r], target.at[row], send.at[r], recv.at[row], other(r))

    def trade_start(r, source, target, send, recv):
        @pl.when(row != r)
        def _():
            trade(r, source, target, send, recv).start()

        @pl.when(row == r)
        def _():
            target[r] = source[r]

    def trade_wait(source, target, send, recv):
        for r in range(4):

            @pl.when(row != r)
            def _():
                trade(r, source, target, send, recv).wait_send()
                remote(source.at[r], target.at[r], send.at[r], recv.at[r], other(r)).wait_recv()

    def far_q_copy(r):
        return remote(far_q_ref.at[r], far_q_in.at[r], q_send.at[r], q_recv.at[r], far)

    ups[0].start()
    ups[1].start()
    outs.start()
    for r in range(4):
        far_q_copy(r).start()

    def give_result(r):
        far_q_copy(r).wait()
        result[r] = (base_ref[r] + far_q_in[r].astype(F32)).astype(LOW)
        trade_start(r, result, res_out, res_send, res_recv)

    block = 256
    lane = lax.broadcasted_iota(jnp.int32, (block, 128), 1)

    def attention(r, p):
        wide = (r + 1) * rows
        pair = slice(p * 128, (p + 1) * 128)

        def part(step, carry):
            here = pl.ds(pl.multiple_of(r * rows + step * block, block), block)
            inside = pl.ds(pl.multiple_of(step * block, block), block)
            queries = q_ref[here, pair]
            grads = do_ref[here, pair]
            inner = (grads.astype(F32) * o_ref[here, pair].astype(F32)).T
            parts = []
            for head in range(2):
                mine = (lane // HD) == head
                masked = jnp.where(mine, queries, 0) * jnp.asarray(HD**-0.5, LOW)
                masked_grads = jnp.where(mine, grads, 0)
                inner_row = jnp.sum(inner[head * HD : (head + 1) * HD], axis=0, keepdims=True)
                scores = contract(k_ref[:wide, pair], masked, 1, 1) + key_bias[:wide]
                last = scores[wide - rows :] + causal[:, inside]
                scores = last if r == 0 else jnp.concatenate([scores[: wide - rows], last], axis=0)
                weights = jnp.exp(scores - lse_ref[p, r, head : head + 1, inside])
                grad_weights = contract(v_ref[:wide, pair], masked_grads, 1, 1)
                grad_scores = (weights * (grad_weights - inner_row)).astype(LOW)
                dv_sum[:wide, pair] += contract(weights.astype(LOW), masked_grads, 1, 0)
                dk_sum[:wide, pair] += contract(grad_scores, masked, 1, 0)
                parts.append(contract(grad_scores, k_ref[:wide, pair], 0, 0))
            dproj[p, here, :128] = (jnp.where(lane < HD, parts[0], parts[1]) * HD**-0.5).astype(LOW)
            return carry

        lax.fori_loop(0, 2, part, 0)
        end = slice(wide - rows, wide)
        dproj[p, end, 128:256] = dk_sum[end, pair].astype(LOW)
        dproj[p, end, 256:] = dv_sum[end, pair].astype(LOW)

    def core_copy(r):
        return remote(core_out.at[r], core_in.at[r], fold_send.at[0, r], fold_recv.at[0, r], core)

    def far_copy(r):
        return remote(far_out.at[r], far_in.at[r], fold_send.at[1, r], fold_recv.at[1, r], far)

    def project(r):
        here = slice(r * rows, (r + 1) * rows)
        grads = jnp.concatenate(
            [dproj[p, here, n * 128 : (n + 1) * 128] for n in range(3) for p in range(2)], axis=1
        )
        total = contract(grads, w_ref[...], 1, 1)
        kept[r, 0] = total[:own]
        core_out[r, 0] = total[own : 2 * own].astype(LOW)
        kept[r, 1] = total[2 * own : 3 * own]
        core_out[r, 1] = total[3 * own :].astype(LOW)
        core_copy(r).start()

    def fold(r):
        core_copy(r).wait()
        far_out[r] = (kept[r, 1] + core_in[r, 1].astype(F32)).astype(LOW)
        kept[r, 0] = kept[r, 0] + core_in[r, 0].astype(F32)
        far_copy(r).start()

    vec[...] = jnp.zeros_like(vec)

    def norm_grad(r):
        far_copy(r).wait()
        grads = kept[r, 0] + far_in[r].astype(F32)
        unit, scale = norm_parts(tok_ref[r].astype(F32))
        gtok[r] = (gmid_ref[r].astype(F32) + norm_back(grads, gain_ref[...], unit, scale)).astype(LOW)
        trade_start(r, gtok, gtok_out, tok_send, tok_recv)
        vec[0:1] += jnp.sum(grads * unit, axis=0, keepdims=True)
        vec[1:2] += jnp.sum(grads, axis=0, keepdims=True)

    def tile_copy(t):
        tile = (2 * (1 - dp) + t) % 4
        part = pl.ds(pl.multiple_of(tile * 256, 256), 256)
        return pltpu.make_async_copy(normed_ref.at[:, part], norm_tile.at[t % 2], tile_sem.at[t % 2])

    dk_sum[...] = jnp.zeros_like(dk_sum)
    dv_sum[...] = jnp.zeros_like(dv_sum)
    tile_copy(0).start()
    tile_copy(1).start()
    def projection_grad(p):
        for t in range(width // 256):
            tile_copy(t).wait()
            tile = (2 * (1 - dp) + t) % 4
            total = contract(norm_tile[t % 2], dproj[p], 0, 0).astype(LOW)
            gproj[p, 2 * tile] = total[:own]
            gproj[p, 2 * tile + 1] = total[own:]
            if t + 2 < width // 256:
                tile_copy(t + 2).start()
            elif p == 0:
                tile_copy(t - 2).start()
            if t == 1:
                projs[p].start()

    def pump(parts, step):
        for part in parts:
            part.pump(step)

    pump(downs, 0)
    attention(3, 0)
    pump(downs, 1)
    attention(2, 0)
    give_result(0)
    give_result(1)
    ups[0].add()
    ups[0].pump(0)
    attention(1, 0)
    pump(downs, 2)
    attention(0, 0)
    give_result(2)
    give_result(3)
    ups[1].add()
    ups[1].pump(0)
    projection_grad(0)
    outs.add()
    outs.pump(0)
    attention(3, 1)
    project(3)
    fold(3)
    pump(ups + [outs], 1)
    attention(2, 1)
    project(2)
    projs[0].add()
    projs[0].pump(0)
    fold(2)
    norm_grad(3)
    attention(1, 1)
    project(1)
    fold(1)
    norm_grad(2)
    pump(ups + [outs], 2)
    attention(0, 1)
    project(0)
    fold(0)
    norm_grad(1)
    projection_grad(1)
    projs[0].pump(1)
    norm_grad(0)

    vec[2:6] = sums_ref[0:4]
    vec[8:9] = sum_up_ref[...]
    for p in range(2):
        part = slice(p * 128, (p + 1) * 128)
        vec[9:10, part] = jnp.sum(dproj[p, :, :128].astype(F32), axis=0, keepdims=True)
        vec[9:10, head_width + p * 128 : head_width + (p + 1) * 128] = jnp.sum(
            dproj[p, :, 256:].astype(F32), axis=0, keepdims=True
        )
    steps = (other(row + 1 - 2 * (row % 2)), other((row + 2) % 4), core, far, cross)

    def sum_copy(step):
        size = 8 if step in (2, 3) else 16
        return size, remote(
            vec.at[:size], vec_in.at[step, :size], vec_send.at[step], vec_recv.at[step], steps[step]
        )

    def sum_start(step):
        sum_copy(step)[1].start()

    def sum_finish(step):
        size, copy = sum_copy(step)
        copy.wait()
        vec[:size] = vec[:size] + vec_in[step, :size]

    sum_start(0)
    projs[0].pump(2)
    projs[1].add()
    projs[1].pump(0)
    sum_finish(0)
    sum_start(1)
    wide = down_out.shape[0] // 2
    for h in range(2):
        downs[h].finish(down_out.at[h * wide : (h + 1) * wide])
        ups[h].finish(up_out.at[h * quarters : (h + 1) * quarters])
    sum_finish(1)
    sum_start(2)
    projs[1].pump(1)
    sum_finish(2)
    sum_start(3)
    outs.finish(out_out)
    sum_finish(3)
    sum_start(4)
    projs[1].pump(2)
    for p in range(2):
        projs[p].finish(proj_sum.at[p])
        part = slice(p * 128, (p + 1) * 128)
        query_out[:, part] = proj_sum[p, :, :128]
        key_out[:, part] = proj_sum[p, :, 128:256]
        value_out[:, part] = proj_sum[p, :, 256:]
    sum_finish(4)
    shared_out[...] = vec[:8]
    by_col_out[...] = vec[8:]
    trade_wait(result, res_out, res_send, res_recv)
    trade_wait(gtok, gtok_out, tok_send, tok_recv)


def back_block(
    queries, keys, values, grads, attended, lse, lengths, w_proj, tokens, gmid, base, far_q, sum_down, gup, gout, gain, sums, sum_up, normed
):
    chunks, own, width = tokens.shape
    rows, head_width = queries.shape
    half = (chunks, 2, own, width)
    one = (chunks, own, width)
    hidden = gup.shape[2]
    quarters = own // 2
    out_block = (gout.shape[1], gout.shape[2])
    down_rows = sum_down.shape[2]
    outputs = ((2 * down_rows, own), (own, hidden), out_block, (own, head_width), (own, head_width), (own, head_width))
    vmem = pl.BlockSpec(memory_space=pltpu.VMEM)
    hbm = pl.BlockSpec(memory_space=pl.ANY)
    dma = pltpu.SemaphoreType.DMA
    return pl.pallas_call(
        back_kernel,
        in_specs=[vmem] * 6 + [pl.BlockSpec(memory_space=pltpu.SMEM)] + [vmem] * 11 + [hbm],
        out_specs=[vmem] * 10,
        out_shape=[jax.ShapeDtypeStruct(one, LOW), jax.ShapeDtypeStruct(one, LOW)]
        + [jax.ShapeDtypeStruct(shape, F32) for shape in outputs]
        + [jax.ShapeDtypeStruct((8, width), F32)] * 2,
        scratch_shapes=[
            pltpu.VMEM((rows, head_width), F32),
            pltpu.VMEM((rows, head_width), F32),
            pltpu.VMEM((2, rows, 384), LOW),
            pltpu.VMEM((2, 8, own, 384), LOW),
            pltpu.VMEM(half, F32),
            pltpu.VMEM(half, LOW),
            pltpu.VMEM(half, LOW),
            pltpu.VMEM(one, LOW),
            pltpu.VMEM(one, LOW),
            pltpu.VMEM(one, LOW),
            pltpu.VMEM((2, rows, 256), LOW),
        ]
        + [
            pltpu.VMEM((rows, 1), F32),
            pltpu.VMEM((rows // chunks, rows // chunks), F32),
            pltpu.VMEM(one, LOW),
            pltpu.VMEM(one, LOW),
            pltpu.VMEM((2, 4, quarters, hidden), LOW),
            pltpu.VMEM((4,) + out_block, LOW),
            pltpu.VMEM((2, 4, own, 384), LOW),
            pltpu.VMEM((2, 2, 3, down_rows, own), LOW),
            pltpu.VMEM((2, 2, 3, quarters, hidden), LOW),
            pltpu.VMEM((2, 3) + out_block, LOW),
            pltpu.VMEM((2, 2, 3, own, 384), LOW),
            pltpu.VMEM((2, own, 384), F32),
            pltpu.VMEM((16, width), F32),
            pltpu.VMEM((5, 16, width), F32),
            dma((4,)),
            dma((4,)),
            dma((4,)),
            dma((4,)),
            dma((4,)),
            dma((4,)),
            dma((2, 4)),
            dma((2, 4)),
            dma((5,)),
            dma((5,)),
            dma((5, 2, 3)),
            dma((5, 2, 3)),
            dma((2, 2, 3)),
            dma((2, 2, 3)),
            dma((5,)),
            dma((5,)),
            dma((2,)),
        ],
        compiler_params=pltpu.CompilerParams(
            collective_id=2, has_side_effects=True, vmem_limit_bytes=61 * 1024 * 1024
        ),
        cost_estimate=pl.CostEstimate(flops=100_000_000_000, bytes_accessed=30_000_000, transcendentals=0),
        name="back_block",
    )(
        queries, keys, values, grads, attended, lse, lengths, w_proj, tokens, gmid, base, far_q, sum_down, gup, gout, gain, sums, sum_up, normed
    )


def local_sequence(
    tokens,
    lengths,
    first_gain,
    first_shift,
    w_query,
    w_key,
    w_value,
    bias_query,
    bias_value,
    w_output,
    bias_output,
    second_gain,
    second_shift,
    w_up,
    bias_up,
    w_down,
    bias_down,
    cotangent,
):
    micro_count, own_rows, width = tokens.shape
    head_width = w_query.shape[1]
    vectors = jnp.stack(
        [bias_output, second_gain, second_shift, bias_down, first_gain, first_shift, bias_down, bias_down]
    )
    (
        queries,
        keys,
        values,
        inputs_low,
        w_projection,
        attended,
        lse,
        base,
        far_part,
        grad_attended,
        grad_output,
        sum_down,
        sums,
        sum_up,
        normed_all,
        grad_middle,
        grad_up,
    ) = feed_block(
        lengths,
        tokens,
        cotangent,
        w_query,
        w_key,
        w_value,
        w_output,
        w_up,
        w_down,
        vectors,
        bias_up.reshape(1, -1),
        bias_query.reshape(1, -1),
        bias_value.reshape(1, -1),
    )
    result, grad_tokens, grad_down, grad_up, grad_output, grad_query, grad_key, grad_value, shared, by_col = back_block(
        queries,
        keys,
        values,
        grad_attended,
        attended,
        lse,
        lengths,
        w_projection.reshape(width, 3 * head_width),
        inputs_low,
        grad_middle,
        base,
        far_part,
        sum_down,
        grad_up,
        grad_output,
        first_gain.reshape(1, width),
        sums,
        sum_up,
        normed_all,
    )
    return (
        result,
        grad_tokens,
        shared[0],
        shared[1],
        grad_query,
        grad_key,
        grad_value,
        by_col[1, :head_width],
        by_col[1, head_width : 2 * head_width],
        grad_output,
        shared[2],
        shared[3],
        shared[4],
        grad_up,
        by_col[0],
        grad_down,
        shared[5],
    )


def solution(mesh):
    return jax.shard_map(
        local_sequence if fits(mesh) else local_general,
        mesh=mesh,
        in_specs=(
            P(None, ("dp", "row", "col"), None),
            P("dp", None),
            P(),
            P(),
            P(("dp", "row"), "col"),
            P(("dp", "row"), "col"),
            P(("dp", "row"), "col"),
            P("col"),
            P("col"),
            P("col", ("dp", "row")),
            P(),
            P(),
            P(),
            P(("dp", "row"), "col"),
            P("col"),
            P("col", ("dp", "row")),
            P(),
            P(None, ("dp", "row", "col"), None),
        ),
        out_specs=(
            P(None, ("dp", "row", "col"), None),
            P(None, ("dp", "row", "col"), None),
            P(),
            P(),
            P(("dp", "row"), "col"),
            P(("dp", "row"), "col"),
            P(("dp", "row"), "col"),
            P("col"),
            P("col"),
            P("col", ("dp", "row")),
            P(),
            P(),
            P(),
            P(("dp", "row"), "col"),
            P("col"),
            P("col", ("dp", "row")),
            P(),
        ),
        check_vma=False,
    )
```
